32 devices in a mesh: expert: 4 (over z), context: 2 (over y), dp: 4 (over x, core).
Axes of the slice: x: 2, y: 2, z: 4, core: 2. Of those that a mesh axis runs over, the one named last changes fastest.
Arguments:
- hidden_in: bfloat16 [2, 16, 2048, 768], P(None, ('expert', 'dp'), 'context'), may hold values from -6 to 6
- segments: int32 [2, 16, 2048], P(None, ('expert', 'dp')), may hold values from 0 to 4, as said below
- routes: int32 [2, 16, 2048, 2], P(None, ('expert', 'dp'), 'context'), may hold values from 0 to 11, all different within a row; in each aligned block of 1024 rows (0 to 1023, 1024 to 2047, ..., all dimensions but the last counted through in order) at most 256 rows name the same one
- prev_logits: float32 [2, 16, 2048, 12], P(None, ('expert', 'dp'), 'context'), may hold values from -4 to 4
- out_grad: bfloat16 [2, 16, 2048, 768], P(None, ('expert', 'dp'), 'context'), may hold values from -6 to 6
- norm_attn: bfloat16 [2, 768], P(None, ('context', 'dp')), may hold values from 0.5 to 1.5
- w_query: bfloat16 [2, 768, 768], P(None, ('context', 'dp')), may hold values from -0.3125 to 0.3125
- w_key: bfloat16 [2, 768, 768], P(None, ('context', 'dp')), may hold values from -0.3125 to 0.3125
- w_value: bfloat16 [2, 768, 768], P(None, ('context', 'dp')), may hold values from -0.21875 to 0.21875
- w_out: bfloat16 [2, 768, 768], P(None, ('context', 'dp')), may hold values from -1.75 to 1.75
- norm_moe: bfloat16 [2, 768], P(None, ('context', 'dp')), may hold values from 0.5 to 1.5
- w_router: bfloat16 [2, 768, 12], P(None, ('context', 'dp')), may hold values from -0.109375 to 0.109375
- w_res: bfloat16 [2, 12, 12], replicated, may hold values from -1.75 to 1.75
- w_const: bfloat16 [2, 2, 768, 2], P(None, None, ('context', 'dp')), may hold values from -0.21875 to 0.21875
- const_vec: bfloat16 [2, 2, 768], P(None, None, ('context', 'dp')), may hold values from -5 to 5
- w_gate: bfloat16 [2, 8, 768, 2048], P(None, 'expert', ('context', 'dp')), may hold values from -0.21875 to 0.21875
- w_up: bfloat16 [2, 8, 768, 2048], P(None, 'expert', ('context', 'dp')), may hold values from -0.21875 to 0.21875
- w_down: bfloat16 [2, 8, 2048, 768], P(None, 'expert', ('context', 'dp')), may hold values from -0.125 to 0.125
Outputs:
- hidden_out: bfloat16 [2, 16, 2048, 768], P(None, ('expert', 'dp'), 'context')
- hidden_grad: bfloat16 [2, 16, 2048, 768], P(None, ('expert', 'dp'), 'context')
- norm_attn_grad: float32 [2, 768], P(None, ('context', 'dp'))
- query_grad: float32 [2, 768, 768], P(None, ('context', 'dp'))
- key_grad: float32 [2, 768, 768], P(None, ('context', 'dp'))
- value_grad: float32 [2, 768, 768], P(None, ('context', 'dp'))
- proj_out_grad: float32 [2, 768, 768], P(None, ('context', 'dp'))
- norm_moe_grad: float32 [2, 768], P(None, ('context', 'dp'))
- router_grad: float32 [2, 768, 12], P(None, ('context', 'dp'))
- gate_res_grad: float32 [2, 12, 12], replicated
- const_grad: float32 [2, 2, 768, 2], P(None, None, ('context', 'dp'))
- vector_grad: float32 [2, 2, 768], P(None, None, ('context', 'dp'))
- gate_grad: float32 [2, 8, 768, 2048], P(None, 'expert', ('context', 'dp'))
- up_grad: float32 [2, 8, 768, 2048], P(None, 'expert', ('context', 'dp'))
- down_grad: float32 [2, 8, 2048, 768], P(None, 'expert', ('context', 'dp'))
The draws below stay inside these ranges and needn't reach their ends.
Inputs may be any that keep to these rules, and one draw needn't show every extreme that they name: `routes`: each token names 2 different experts; numbers below 8 are feed-forward experts, 8 the zero expert, 9 the copy expert, the rest constant experts; within each aligned block of 1024 positions of a sequence no number is named more than 256 times, a bound that some block reaches. `segments`: document numbers never fall along a sequence.
All inputs are finite; a program needn't handle non-finite values.
Results may differ from the reference program's by a relative error of at most 0.028.
Values may be sent and summed in bfloat16 or wider, within the bound.
No kernel may reach another device: no remote copies, remote signals or barrier semaphores. Data moves between devices by JAX's collectives and lax.ppermute only.
A program may use at most 1.125 GiB of HBM per device.

```python
import math
import jax
import jax.numpy as jnp
import numpy as np
from jax import lax

D = 768
HEADS = 12
HEAD_DIM = 64
FF = 2048
EXPERTS = 8
TOP = 2
CONST = 2
WINDOW = 1024
LAYERS = 2
MB = 2
SEQLEN = 2048
ROUTED = 12
SEQS = 16
STRETCH = 1024
CAP = 256
N_CONTEXT = 2


def draw_segments(key, part):
    key = jax.random.fold_in(key, 11)
    keys = jax.random.split(key, 4)
    limit_start = STRETCH // 2 + 1
    first_doc = jax.random.randint(keys[0], (MB, SEQS, 1), 2, limit_start)
    tail_len = jax.random.randint(keys[1], (MB, SEQS, 1), 2, limit_start)
    first_cut = jax.random.randint(keys[2], (MB, SEQS, 1), 1, first_doc)
    finish = SEQLEN - tail_len
    last_cut = finish + jax.random.randint(keys[3], (MB, SEQS, 1), 1, tail_len)
    positions = jnp.arange(SEQLEN, dtype=jnp.int32)[None, None, :]
    numbers = (positions >= first_cut).astype(jnp.int32) + (positions >= first_doc).astype(jnp.int32)
    numbers = numbers + (positions >= finish).astype(jnp.int32) + (positions >= last_cut).astype(jnp.int32)
    return numbers.astype(jnp.int32)


def block_scale(rng, shape, cuts, smallest, largest):
    def one(dim, blocks):
        draws = jax.random.uniform(jax.random.fold_in(jax.random.fold_in(rng, 6), dim), (blocks,), jnp.float32, smallest / len(cuts), largest / len(cuts))
        return jnp.repeat(jnp.exp(draws), shape[dim] // blocks).reshape((-1,) + (1,) * (len(shape) - dim - 1))

    loudness = one(*cuts[0])
    for cut in cuts[1:]:
        loudness = loudness * one(*cut)
    return loudness


def deal_out(own_key, own, number, rows, amount, top, bound, slope):
    order = jax.random.permutation(own_key, amount)
    crowded, common = portions_of(amount, rows * top, bound, slope, True), portions_of(amount, rows * top, bound, slope, False)
    places = jnp.arange(amount)

    def named(lengths, offset_by):
        used = int((lengths > 0).sum())
        fixed = max(1, used // 4)
        shifted = fixed + (places - fixed + offset_by * (used - fixed)) % max(1, amount - fixed)
        return jnp.zeros((amount,), jnp.int32).at[order[jnp.where(places < fixed, places, shifted)]].set(jnp.asarray(lengths, jnp.int32))

    lengths = jnp.where(number % 4 == 0, named(crowded, number // 4), named(common, number - number // 4 - 1))
    mixed = jax.random.permutation(jax.random.fold_in(own, 3), amount)
    donor, taker = mixed[0:amount // 2 * 2:2], mixed[1:amount // 2 * 2:2]
    room = jnp.minimum(lengths[donor] - 1, bound - lengths[taker]) // 2
    room = jnp.where((donor == order[0]) | (taker == order[0]) | (lengths[taker] == 0), 0, jnp.maximum(room, 0))
    shifted = jax.random.randint(jax.random.fold_in(own, 4), (amount // 2,), 0, 1 << 20) % (room + 1)
    lengths = lengths.at[donor].add(-shifted).at[taker].add(shifted)
    members = jnp.searchsorted(jnp.cumsum(lengths), jnp.arange(rows * top), side="right").astype(jnp.int32)
    table = members.reshape(top, rows).T
    table = table[jax.random.permutation(jax.random.fold_in(own, 1), rows)]
    offset_by = jax.random.randint(jax.random.fold_in(own, 2), (rows, 1), 0, top)
    return jnp.take_along_axis(table, (jnp.arange(top)[None, :] + offset_by) % top, axis=1)


def portions_of(amount, total, limit, slope, full):
    portions = [(1 << 20) // math.isqrt(grade ** slope) + 1 for grade in range(1, amount + 1)]
    largest = limit if full else min(limit, max(-(-total // amount), total * portions[0] // sum(portions)))
    least = 1 if total - largest >= amount - 1 else 0
    holding, rest = [largest] + [least] * (amount - 1), total - largest - least * (amount - 1)
    while rest > 0:
        movable = [i for i in range(1, amount) if holding[i] < largest] or [i for i in range(1, amount) if holding[i] < limit]
        mass, left = sum([portions[i] for i in movable]), rest
        for i in movable:
            more = min(limit - holding[i], max(1, left * portions[i] // mass), rest)
            holding[i] = holding[i] + more
            rest = rest - more
    return np.array(holding)


def noise(stream_key, extent, deviation, most, cuts=(), held_as=jnp.bfloat16):
    array = jax.random.normal(stream_key, extent, jnp.float32) * deviation
    if len(cuts) > 0:
        array = block_scale(stream_key, extent, cuts, -0.22, 0.18) * array
    return jnp.clip(array, min=-most, max=most).astype(held_as)


def setup_inputs(seed: int = 0) -> dict:
    key_of = jax.random.split(jax.random.key(seed), 19)
    hidden_in = noise(key_of[0], (MB, SEQS, SEQLEN, D), 1.0, 6.0, ((1, 16), (2, 2)))
    segments = draw_segments(jax.random.fold_in(key_of[18], 71), 0)
    routes_keys = jax.random.split(jax.random.fold_in(key_of[2], 1), MB * SEQS * SEQLEN // STRETCH)
    routes_turns = jax.random.permutation(jax.random.fold_in(key_of[2], 3), MB * SEQS * SEQLEN // STRETCH)
    routes = jax.vmap(lambda own, number: deal_out(jax.random.fold_in(key_of[2], 2), own, number, STRETCH, ROUTED, TOP, STRETCH // 4, 1))(routes_keys, routes_turns).reshape((MB, SEQS, SEQLEN, TOP))
    prev_logits = noise(key_of[3], (MB, SEQS, SEQLEN, ROUTED), 0.5, 4.0, ((1, 16), (2, 2)), jnp.float32)
    out_grad = noise(key_of[4], (MB, SEQS, SEQLEN, D), 1.0, 6.0, ((1, 16), (2, 2)))
    norm_attn = jnp.clip(1.0 + 0.1 * jax.random.normal(key_of[5], (LAYERS, D), jnp.float32), 0.5, 1.5).astype(jnp.bfloat16)
    w_query = noise(key_of[6], (LAYERS, D, D), (D // 2) ** -0.5, 0.3125, ((1, 8),))
    w_key = noise(key_of[7], (LAYERS, D, D), (D // 2) ** -0.5, 0.3125, ((1, 8),))
    w_value = noise(key_of[8], (LAYERS, D, D), D ** -0.5, 0.21875, ((1, 8),))
    w_out = noise(key_of[9], (LAYERS, D, D), (max(D // 64, 1)) ** -0.5, 1.75, ((1, 8),))
    norm_moe = jnp.clip(1.0 + 0.1 * jax.random.normal(key_of[10], (LAYERS, D), jnp.float32), 0.5, 1.5).astype(jnp.bfloat16)
    w_router = noise(key_of[11], (LAYERS, D, ROUTED), (4 * D) ** -0.5, 0.109375, ((1, 8),))
    w_res = noise(key_of[12], (LAYERS, ROUTED, ROUTED), ROUTED ** -0.5, 1.75)
    w_const = noise(key_of[13], (LAYERS, CONST, D, 2), D ** -0.5, 0.21875, ((2, 8),))
    const_vec = noise(key_of[14], (LAYERS, CONST, D), 1.0, 5.0, ((2, 8),))
    w_gate = noise(key_of[15], (LAYERS, EXPERTS, D, FF), D ** -0.5, 0.21875, ((1, 4), (2, 8)))
    w_up = noise(key_of[16], (LAYERS, EXPERTS, D, FF), D ** -0.5, 0.21875, ((1, 4), (2, 8)))
    w_down = noise(key_of[17], (LAYERS, EXPERTS, FF, D), FF ** -0.5, 0.125, ((1, 4), (2, 8)))
    return {"hidden_in": hidden_in, "segments": segments, "routes": routes, "prev_logits": prev_logits, "out_grad": out_grad, "norm_attn": norm_attn, "w_query": w_query, "w_key": w_key, "w_value": w_value, "w_out": w_out, "norm_moe": norm_moe, "w_router": w_router, "w_res": w_res, "w_const": w_const, "const_vec": const_vec, "w_gate": w_gate, "w_up": w_up, "w_down": w_down}


@jax.custom_vjp
def low(v):
    return lax.optimization_barrier(v.astype(jnp.bfloat16)).astype(jnp.float32)

@jax.custom_vjp
def low_back(v):
    return v

def low_keep(v):
    return (low(v), None)

def low_pass(kept, grad):
    return (grad,)

def back_keep(v):
    return (v, None)

def back_low(kept, grad):
    return (low(grad),)
low.defvjp(low_keep, low_pass)
low_back.defvjp(back_keep, back_low)
norm_eps = 1e-05
masked = -1000000000.0
highest = lax.Precision.HIGHEST

def rms_norm(rows_in, gain_vec):
    return rows_in * lax.rsqrt(lax.optimization_barrier(jnp.mean(rows_in * rows_in, axis=-1, keepdims=True)) + norm_eps) * gain_vec

def mixture(normed, normed_low, earlier, router_w, residual_w, const_w, const_v, expert_rows, chosen_onehot):
    logits = jnp.dot(normed_low, router_w, precision=highest) + jnp.dot(earlier, residual_w, precision=highest)
    chosen = lax.optimization_barrier(jnp.sum(chosen_onehot * logits[:, None, :], axis=-1))
    gate_vals = jax.nn.softmax(chosen, axis=-1)
    mix_weights = jax.nn.softmax(jnp.einsum('td,jdk->tjk', normed_low, const_w, precision=highest), axis=-1)
    constant = mix_weights[:, :, 0:1] * normed[:, None, :] + mix_weights[:, :, 1:2] * const_v[None, :, :]
    copied = chosen_onehot[:, :, EXPERTS + 1:EXPERTS + 2] * normed[:, None, :]
    outputs = expert_rows + copied + jnp.einsum('tkj,tjd->tkd', chosen_onehot[:, :, EXPERTS + 2:], constant, precision=highest)
    return (lax.optimization_barrier(jnp.sum(gate_vals[:, :, None] * outputs, axis=1)), logits)

def attend(query_h, key_h, value_h, seg_ids):
    length = query_h.shape[0]
    block_len = min(512, length)
    scale_factor = HEAD_DIM ** (-0.5)
    key_pad = jnp.concatenate([jnp.zeros((WINDOW, HEADS, HEAD_DIM), jnp.float32), key_h], axis=0)
    value_pad = jnp.concatenate([jnp.zeros((WINDOW, HEADS, HEAD_DIM), jnp.float32), value_h], axis=0)
    seg_pad = jnp.concatenate([jnp.full((WINDOW,), -1, jnp.int32), seg_ids.astype(jnp.int32)])

    def one_block(block_index):
        first = (block_index * block_len).astype(jnp.int32)
        query_blk = lax.dynamic_slice_in_dim(query_h, first, block_len, 0)
        key_blk = lax.dynamic_slice_in_dim(key_pad, first, block_len + WINDOW, 0)
        value_blk = lax.dynamic_slice_in_dim(value_pad, first, block_len + WINDOW, 0)
        seg_query = lax.dynamic_slice_in_dim(seg_ids.astype(jnp.int32), first, block_len, 0)
        seg_key = lax.dynamic_slice_in_dim(seg_pad, first, block_len + WINDOW, 0)
        query_place = first + jnp.arange(block_len, dtype=jnp.int32)
        key_place = first - WINDOW + jnp.arange(block_len + WINDOW, dtype=jnp.int32)
        allowed = (key_place[None, :] >= 0) & (key_place[None, :] <= query_place[:, None])
        allowed = allowed & (query_place[:, None] - key_place[None, :] < WINDOW) & (seg_query[:, None] == seg_key[None, :])
        scores = low_back(jnp.einsum('qhd,khd->hqk', query_blk, key_blk, precision=highest) * scale_factor)
        scores = jnp.where(allowed[None], scores, masked)
        row_max = lax.optimization_barrier(jnp.max(scores, axis=-1, keepdims=True))
        exponent = jnp.exp(scores - row_max)
        prob_low = low(exponent / lax.optimization_barrier(jnp.sum(exponent, axis=-1, keepdims=True)))
        return jnp.einsum('hqk,khd->qhd', prob_low, value_blk, precision=highest)
    blocks = lax.map(jax.checkpoint(one_block), jnp.arange(length // block_len, dtype=jnp.int32))
    return blocks.reshape(length, HEADS * HEAD_DIM)

def experts_apply(normed_low, route_ids, gate_w, up_w, down_w):
    length = normed_low.shape[0]
    buffer_len = N_CONTEXT * CAP
    flat = route_ids.reshape(-1).astype(jnp.int32)
    onehot = (flat[:, None] == jnp.arange(ROUTED, dtype=jnp.int32)[None, :]).astype(jnp.int32)
    before = (jnp.cumsum(onehot, axis=0).astype(jnp.int32) - onehot) * onehot
    slot_rank = lax.optimization_barrier(jnp.sum(before, axis=1)).astype(jnp.int32)
    target = jnp.where(flat < EXPERTS, flat * buffer_len + slot_rank, EXPERTS * buffer_len).astype(jnp.int32)
    token_ids = (jnp.arange(TOP * length, dtype=jnp.int32) // TOP).astype(jnp.int32)
    source = jnp.full((EXPERTS * buffer_len + 1,), length, jnp.int32).at[target].set(token_ids)
    padded_rows = jnp.concatenate([normed_low, jnp.zeros((1, D), jnp.float32)], axis=0)
    inputs = low_back(padded_rows[source[:EXPERTS * buffer_len]].reshape(EXPERTS, buffer_len, D))
    gate_pre = low_back(jnp.einsum('erd,edf->erf', inputs, gate_w, precision=highest))
    up_pre = low_back(jnp.einsum('erd,edf->erf', inputs, up_w, precision=highest))
    activated = low(jax.nn.silu(gate_pre) * up_pre)
    produced = low(low_back(jnp.einsum('erf,efd->erd', activated, down_w, precision=highest)))
    out_table = jnp.concatenate([produced.reshape(EXPERTS * buffer_len, D), jnp.zeros((1, D), jnp.float32)], axis=0)
    return out_table[target].reshape(length, TOP, D)

def layer_apply(hidden, earlier, seg_ids, route_ids, layer_w):
    attn_gain, query_w, key_w, value_w, out_w, moe_gain, router_w, residual_w, const_w, const_v, gate_w, up_w, down_w = layer_w
    length = hidden.shape[0]
    normed_attn = low(rms_norm(hidden, attn_gain))
    query_f = low(low_back(jnp.dot(normed_attn, query_w, precision=highest)))
    key_f = low(low_back(jnp.dot(normed_attn, key_w, precision=highest)))
    value_f = low(low_back(jnp.dot(normed_attn, value_w, precision=highest)))
    shape_heads = (length, HEADS, HEAD_DIM)
    attended = low(low_back(attend(query_f.reshape(shape_heads), key_f.reshape(shape_heads), value_f.reshape(shape_heads), seg_ids)))
    mid_rows = hidden + jnp.dot(attended, out_w, precision=highest)
    normed = rms_norm(mid_rows, moe_gain)
    normed_low = low(normed)
    expert_rows = experts_apply(normed_low, route_ids, gate_w, up_w, down_w)
    chosen_onehot = (route_ids[:, :, None] == jnp.arange(ROUTED, dtype=jnp.int32)[None, None, :]).astype(jnp.float32)
    mixed_out, logits = mixture(normed, normed_low, earlier, router_w, residual_w, const_w, const_v, expert_rows, chosen_onehot)
    return (mid_rows + mixed_out, logits)

def stack_forward(hidden, earlier, seg_ids, route_ids, params):
    for current_layer_index in range(LAYERS):
        layer_w = tuple((tensor[current_layer_index] for tensor in params))
        hidden, earlier = layer_apply(hidden, earlier, seg_ids, route_ids, layer_w)
    return hidden

def reference(hidden_in, segments, routes, prev_logits, out_grad, norm_attn, w_query, w_key, w_value, w_out, norm_moe, w_router, w_res, w_const, const_vec, w_gate, w_up, w_down):
    params = tuple((tensor.astype(jnp.float32) for tensor in (norm_attn, w_query, w_key, w_value, w_out, norm_moe, w_router, w_res, w_const, const_vec, w_gate, w_up, w_down)))
    count = MB * SEQS
    inputs = (hidden_in.astype(jnp.float32).reshape(count, SEQLEN, D), prev_logits.astype(jnp.float32).reshape(count, SEQLEN, ROUTED), segments.reshape(count, SEQLEN), routes.reshape(count, SEQLEN, TOP), out_grad.astype(jnp.float32).reshape(count, SEQLEN, D))

    def one_sequence(grand_totals, item):
        hidden, earlier, seg_ids, route_ids, cotangent = item

        def forward(hid, par):
            return stack_forward(hid, earlier, seg_ids, route_ids, par)
        result, pull = jax.vjp(forward, hidden, params)
        d_hidden, d_params = pull(cotangent)
        grand_totals = tuple((running_total + summand_term for running_total, summand_term in zip(grand_totals, d_params)))
        return (grand_totals, (result.astype(jnp.bfloat16), d_hidden.astype(jnp.bfloat16)))
    start_totals = tuple((jnp.zeros_like(tensor) for tensor in params))
    grand_totals, (results, grads_in) = lax.scan(one_sequence, start_totals, inputs)
    return (results.reshape(MB, SEQS, SEQLEN, D), grads_in.reshape(MB, SEQS, SEQLEN, D), grand_totals[0], grand_totals[1], grand_totals[2], grand_totals[3], grand_totals[4], grand_totals[5], grand_totals[6], grand_totals[7], grand_totals[8], grand_totals[9], grand_totals[10], grand_totals[11], grand_totals[12])
```

```python
import functools

import jax
import jax.numpy as jnp
from jax import lax
from jax.experimental import pallas as pl
from jax.experimental.pallas import tpu as pltpu
from jax.sharding import PartitionSpec as P

HEADS = 12
HEAD_DIM = 64
EXPERTS = 8
TOP = 2
WINDOW = 1024
ROUTED = 12
LANES = 128
MIB = 1 << 20

norm_eps = 1e-05
masked = -1000000000.0
highest = lax.Precision.HIGHEST
f32 = jnp.float32
bf16 = jnp.bfloat16
SHARDED = ("context", "dp")


ANY_SPEC = pl.BlockSpec(memory_space=pl.ANY)


def dot_on(left_op, right_op, left_dim, right_dim):
    return lax.dot_general(
        left_op,
        right_op,
        (((left_dim,), (right_dim,)), ((), ())),
        preferred_element_type=f32,
    )


def rows_of(values, picks):
    count = 8 if len(picks) <= 8 else 16
    row = lax.broadcasted_iota(jnp.int32, (count, LANES), 0)
    lane = lax.broadcasted_iota(jnp.int32, (count, LANES), 1)
    pick = jnp.zeros((count, LANES), f32)
    for index, source in enumerate(picks):
        pick = jnp.where((row == index) & (lane == source), 1.0, pick)
    return lax.dot_general(
        pick, values, (((1,), (1,)), ((), ())), precision=highest, preferred_element_type=f32
    )


def join_spans(buffer_ref, earlier_ref, own_ref):
    buffer_ref[:WINDOW, :] = earlier_ref[...]
    buffer_ref[WINDOW:, :] = own_ref[...]


def attention_forward_kernel(
    rows, keys, blocks, q_ref, ko_ref, vo_ref, kp_ref, vp_ref, sq_ref, sk_ref, *rest
):
    out_ref, lse_rows_ref, lse_ref, bias_ref, k_ref, v_ref = rest[-6:]
    pair = pl.program_id(0)

    @pl.when(pair == 0)
    def _():
        lse_ref[...] = jnp.zeros_like(lse_ref)
        rel = lax.broadcasted_iota(jnp.int32, (rows, keys), 1) - lax.broadcasted_iota(
            jnp.int32, (rows, keys), 0
        )
        inside = (rel > 0) & (rel <= WINDOW)
        for block in range(blocks):
            first = block * rows
            same = sq_ref[first : first + rows, :] == sk_ref[:, first : first + keys]
            bias_ref[block] = jnp.where(inside & same, 0.0, masked)

    join_spans(k_ref, kp_ref, ko_ref)
    join_spans(v_ref, vp_ref, vo_ref)
    lane = lax.broadcasted_iota(jnp.int32, (rows, LANES), 1)
    low = lane < HEAD_DIM
    for block in range(blocks):
        own = slice(block * rows, (block + 1) * rows)
        span = slice(block * rows, block * rows + keys)
        query = q_ref[own, :] * (HEAD_DIM ** -0.5)
        key = k_ref[span, :]
        value = v_ref[span, :]
        heads_out = []
        for half in range(2):
            mine = low if half == 0 else ~low
            scores = (
                dot_on(jnp.where(mine, query, jnp.zeros_like(query)), key, 1, 1) + bias_ref[block]
            )
            row_max = jnp.max(scores, axis=1, keepdims=True)
            exponent = jnp.exp(scores - row_max)
            row_sum = jnp.sum(exponent, axis=1, keepdims=True)
            heads_out.append(dot_on(exponent.astype(bf16), value, 1, 0) * (1.0 / row_sum))
            lse_ref[own, :] = jnp.where(
                lane == 2 * pair + half, row_max + jnp.log(row_sum), lse_ref[own, :]
            )
        out_ref[own, :] = jnp.where(low, heads_out[0], heads_out[1]).astype(bf16)

    @pl.when(pair == pl.num_programs(0) - 1)
    def _():
        lse_rows_ref[...] = rows_of(lse_ref[...], range(HEADS))


def attention_forward(qkv, kv_earlier, seg_query, seg_key, after):
    length = qkv.shape[0]
    width = qkv.shape[1] // 3
    pairs = width // LANES
    rows = min(256, length)
    keys = rows + WINDOW
    blocks = length // rows
    span = WINDOW + length

    def column(count, offset):
        return pl.BlockSpec((count, LANES), lambda p: (0, offset + p))

    return pl.pallas_call(
        functools.partial(attention_forward_kernel, rows, keys, blocks),
        grid=(pairs,),
        in_specs=[
            column(length, 0),
            column(length, pairs),
            column(length, 2 * pairs),
            column(WINDOW, 0),
            column(WINDOW, pairs),
            pl.BlockSpec((length, 1), lambda p: (0, 0)),
            pl.BlockSpec((1, span), lambda p: (0, 0)),
        ]
        + [ANY_SPEC] * len(after),
        out_specs=[column(length, 0), pl.BlockSpec((16, length), lambda p: (0, 0))],
        out_shape=[
            jax.ShapeDtypeStruct((length, width), bf16),
            jax.ShapeDtypeStruct((16, length), f32),
        ],
        scratch_shapes=[
            pltpu.VMEM((length, LANES), f32),
            pltpu.VMEM((blocks, rows, keys), f32),
            pltpu.VMEM((span, LANES), bf16),
            pltpu.VMEM((span, LANES), bf16),
        ],
        compiler_params=pltpu.CompilerParams(vmem_limit_bytes=40 * MIB),
        cost_estimate=pl.CostEstimate(
            flops=4 * length * keys * width * 4, bytes_accessed=12 * length * width,
            transcendentals=length * keys * HEADS,
        ),
        name="attention_forward",
    )(qkv, qkv, qkv, kv_earlier, kv_earlier, seg_query, seg_key, *after)


def attention_backward_kernel(
    rows, keys, blocks, q_ref, ko_ref, vo_ref, kp_ref, vp_ref, do_ref, out_ref, lse_ref,
    sq_ref, sk_ref, *rest
):
    dq_ref, dk_ref, dv_ref, bias_ref, k_ref, v_ref, dk_sum, dv_sum = rest[-8:]
    pair = pl.program_id(0)

    @pl.when(pair == 0)
    def _():
        rel = lax.broadcasted_iota(jnp.int32, (keys, rows), 0) - lax.broadcasted_iota(
            jnp.int32, (keys, rows), 1
        )
        inside = (rel > 0) & (rel <= WINDOW)
        for block in range(blocks):
            first = block * rows
            same = sk_ref[first : first + keys, :] == sq_ref[:, first : first + rows]
            bias_ref[block] = jnp.where(inside & same, 0.0, masked)

    join_spans(k_ref, kp_ref, ko_ref)
    join_spans(v_ref, vp_ref, vo_ref)
    dk_sum[...] = jnp.zeros_like(dk_sum)
    dv_sum[...] = jnp.zeros_like(dv_sum)
    low = lax.broadcasted_iota(jnp.int32, (rows, LANES), 1) < HEAD_DIM
    ones = jnp.ones((8, LANES), bf16)
    for block in range(blocks):
        own = slice(block * rows, (block + 1) * rows)
        span = slice(block * rows, block * rows + keys)
        query = q_ref[own, :] * (HEAD_DIM ** -0.5)
        grad = do_ref[own, :]
        key = k_ref[span, :]
        value = v_ref[span, :]
        product = grad.astype(f32) * out_ref[own, :].astype(f32)
        heads_dq = []
        for half in range(2):
            mine = low if half == 0 else ~low
            query_h = jnp.where(mine, query, jnp.zeros_like(query))
            grad_h = jnp.where(mine, grad, jnp.zeros_like(grad))
            product_h = jnp.where(mine, product, 0.0)
            coarse = product_h.astype(bf16)
            fine = (product_h - coarse.astype(f32)).astype(bf16)
            delta = (dot_on(ones, coarse, 1, 1) + dot_on(ones, fine, 1, 1))[0:1, :]
            scores = dot_on(key, query_h, 1, 1) + bias_ref[block]
            probs = jnp.exp(scores - lse_ref[pl.ds(2 * pair + half, 1), own])
            d_probs = dot_on(value, grad_h, 1, 1)
            d_scores = (probs * (d_probs - delta)).astype(bf16)
            dv_sum[span, :] += dot_on(probs.astype(bf16), grad_h, 1, 0)
            dk_sum[span, :] += dot_on(d_scores, query_h, 1, 0)
            heads_dq.append(dot_on(d_scores, key, 0, 0))
        dq_ref[own, :] = (
            jnp.where(low, heads_dq[0], heads_dq[1]) * (HEAD_DIM ** -0.5)
        ).astype(bf16)
    dk_ref[...] = dk_sum[...].astype(bf16)
    dv_ref[...] = dv_sum[...].astype(bf16)


def attention_backward(qkv, kv_earlier, grad_att, attended, lse, seg_query, seg_key, after):
    length = qkv.shape[0]
    width = qkv.shape[1] // 3
    pairs = width // LANES
    rows = min(256, length)
    keys = rows + WINDOW
    blocks = length // rows
    span = WINDOW + length

    def column(count, offset):
        return pl.BlockSpec((count, LANES), lambda p: (0, offset + p))

    return pl.pallas_call(
        functools.partial(attention_backward_kernel, rows, keys, blocks),
        grid=(pairs,),
        in_specs=[
            column(length, 0),
            column(length, pairs),
            column(length, 2 * pairs),
            column(WINDOW, 0),
            column(WINDOW, pairs),
            column(length, 0),
            column(length, 0),
            pl.BlockSpec((16, length), lambda p: (0, 0)),
            pl.BlockSpec((1, length), lambda p: (0, 0)),
            pl.BlockSpec((span, 1), lambda p: (0, 0)),
        ]
        + [ANY_SPEC] * len(after),
        out_specs=[column(length, 0), column(span, 0), column(span, 0)],
        out_shape=[
            jax.ShapeDtypeStruct((length, width), bf16),
            jax.ShapeDtypeStruct((span, width), bf16),
            jax.ShapeDtypeStruct((span, width), bf16),
        ],
        scratch_shapes=[
            pltpu.VMEM((blocks, keys, rows), f32),
            pltpu.VMEM((span, LANES), bf16),
            pltpu.VMEM((span, LANES), bf16),
            pltpu.VMEM((span, LANES), f32),
            pltpu.VMEM((span, LANES), f32),
        ],
        compiler_params=pltpu.CompilerParams(vmem_limit_bytes=48 * MIB),
        cost_estimate=pl.CostEstimate(
            flops=10 * length * keys * width * 4, bytes_accessed=24 * length * width,
            transcendentals=length * keys * HEADS,
        ),
        name="attention_backward",
    )(
        qkv, qkv, qkv, kv_earlier, kv_earlier, grad_att, attended, lse, seg_query, seg_key, *after
    )


def sigmoid(values):
    return 1.0 / (1.0 + jnp.exp(-values))


def experts_forward_kernel(
    chunks, x_ref, gate_w_ref, up_w_ref, down_w_ref, *rest
):
    out_ref, gate_ref, up_ref, total_ref = rest[-4:]
    chunk = pl.program_id(1)
    rows_in = x_ref[0]
    gate_pre = dot_on(rows_in, gate_w_ref[0], 1, 0)
    up_pre = dot_on(rows_in, up_w_ref[0], 1, 0)
    activated = (gate_pre * sigmoid(gate_pre) * up_pre).astype(bf16)
    gate_ref[0] = gate_pre.astype(bf16)
    up_ref[0] = up_pre.astype(bf16)
    part = dot_on(activated, down_w_ref[0], 1, 0)

    @pl.when(chunk == 0)
    def _():
        total_ref[...] = part

    @pl.when(chunk > 0)
    def _():
        total_ref[...] += part

    @pl.when(chunk == chunks - 1)
    def _():
        out_ref[0] = total_ref[...].astype(bf16)


def experts_forward(rows_in, gate_up_w, down_w, after):
    count, rows, _ = rows_in.shape
    width, hidden = gate_up_w.shape[1:]
    chunk = hidden
    chunks = hidden // chunk
    return pl.pallas_call(
        functools.partial(experts_forward_kernel, chunks),
        grid=(count, chunks),
        in_specs=[
            pl.BlockSpec((1, rows, width), lambda j, f: (j, 0, 0)),
            pl.BlockSpec((1, width, chunk), lambda j, f: (j, 0, f)),
            pl.BlockSpec((1, width, chunk), lambda j, f: (count + j, 0, f)),
            pl.BlockSpec((1, chunk, width), lambda j, f: (j, f, 0)),
        ]
        + [ANY_SPEC] * len(after),
        out_specs=[
            pl.BlockSpec((1, rows, width), lambda j, f: (j, 0, 0)),
            pl.BlockSpec((1, rows, chunk), lambda j, f: (j, 0, f)),
            pl.BlockSpec((1, rows, chunk), lambda j, f: (j, 0, f)),
        ],
        out_shape=[
            jax.ShapeDtypeStruct((count, rows, width), bf16),
            jax.ShapeDtypeStruct((count, rows, hidden), bf16),
            jax.ShapeDtypeStruct((count, rows, hidden), bf16),
        ],
        scratch_shapes=[pltpu.VMEM((rows, width), f32)],
        compiler_params=pltpu.CompilerParams(vmem_limit_bytes=48 * MIB),
        cost_estimate=pl.CostEstimate(
            flops=6 * count * rows * width * hidden,
            bytes_accessed=6 * count * width * hidden + 4 * count * rows * (width + hidden),
            transcendentals=count * rows * hidden,
        ),
        name="experts_forward",
    )(rows_in, gate_up_w, gate_up_w, down_w, *after)


def experts_backward_kernel(chunks, has_gate, has_sums, *refs):
    x_ref, dy_ref, gate_ref, up_ref, gate_w_ref, up_w_ref, down_w_ref = refs[:7]
    given = refs[7:]
    dx_ref, gate_up_grad_ref, down_grad_ref, total_ref, scaled_ref = refs[-5:]
    chunk = pl.program_id(1)
    rows_in = x_ref[0]
    if has_gate:
        share_ref, given = given[0], given[1:]

        @pl.when(chunk == 0)
        def _():
            share = share_ref[0].astype(f32)
            share = share[:, 0:1] + share[:, 1:2]
            scaled_ref[...] = (dy_ref[0].astype(f32) * share).astype(bf16)

        d_out = scaled_ref[...]
    else:
        d_out = dy_ref[0]
    gate_pre = gate_ref[0].astype(f32)
    up_pre = up_ref[0].astype(f32)
    share = sigmoid(gate_pre)
    swish = gate_pre * share
    activated = (swish * up_pre).astype(bf16)
    d_act = dot_on(d_out, down_w_ref[0], 1, 1)
    d_gate = (d_act * up_pre * (share * (1.0 + gate_pre * (1.0 - share)))).astype(bf16)
    d_up = (d_act * swish).astype(bf16)
    part = dot_on(d_gate, gate_w_ref[0], 1, 1) + dot_on(d_up, up_w_ref[0], 1, 1)
    gate_grad = dot_on(rows_in, d_gate, 0, 0)
    up_grad = dot_on(rows_in, d_up, 0, 0)
    down_grad = dot_on(activated, d_out, 0, 0)
    if has_sums:
        gate_up_sum_ref, down_sum_ref = given[:2]
        gate_grad += gate_up_sum_ref[0, 0].astype(f32)
        up_grad += gate_up_sum_ref[1, 0].astype(f32)
        down_grad += down_sum_ref[0].astype(f32)
    gate_up_grad_ref[0, 0] = gate_grad.astype(bf16)
    gate_up_grad_ref[1, 0] = up_grad.astype(bf16)
    down_grad_ref[0] = down_grad.astype(bf16)

    @pl.when(chunk == 0)
    def _():
        total_ref[...] = part

    @pl.when(chunk > 0)
    def _():
        total_ref[...] += part

    @pl.when(chunk == chunks - 1)
    def _():
        dx_ref[0] = total_ref[...].astype(bf16)


def experts_backward(rows_in, d_out, gate_pre, up_pre, gate_up_w, down_w, has_gate, sums, after):
    count, rows, _ = rows_in.shape
    width, hidden = gate_up_w.shape[1:]
    chunk = min(512, hidden)
    chunks = hidden // chunk
    row_spec = pl.BlockSpec((1, rows, width), lambda j, f: (j, 0, 0))
    hidden_spec = pl.BlockSpec((1, rows, chunk), lambda j, f: (j, 0, f))
    wide_spec = pl.BlockSpec((1, width, chunk), lambda j, f: (j, 0, f))
    up_spec = pl.BlockSpec((1, width, chunk), lambda j, f: (count + j, 0, f))
    tall_spec = pl.BlockSpec((1, chunk, width), lambda j, f: (j, f, 0))
    both_spec = pl.BlockSpec((2, 1, width, chunk), lambda j, f: (0, j, 0, f))
    operands = [rows_in, d_out, gate_pre, up_pre, gate_up_w, gate_up_w, down_w]
    specs = [row_spec, row_spec, hidden_spec, hidden_spec, wide_spec, up_spec, tall_spec]
    if has_gate:
        operands.append(rows_in)
        specs.append(pl.BlockSpec((1, rows, LANES), lambda j, f: (j, 0, width // LANES)))
    if sums is not None:
        operands.extend(sums)
        specs.extend([both_spec, tall_spec])
    return pl.pallas_call(
        functools.partial(experts_backward_kernel, chunks, has_gate, sums is not None),
        grid=(count, chunks),
        in_specs=specs + [ANY_SPEC] * len(after),
        out_specs=[row_spec, both_spec, tall_spec],
        out_shape=[
            jax.ShapeDtypeStruct((count, rows, width), bf16),
            jax.ShapeDtypeStruct((2, count, width, hidden), bf16),
            jax.ShapeDtypeStruct((count, hidden, width), bf16),
        ],
        scratch_shapes=[pltpu.VMEM((rows, width), f32), pltpu.VMEM((rows, width), bf16)],
        compiler_params=pltpu.CompilerParams(vmem_limit_bytes=56 * MIB),
        cost_estimate=pl.CostEstimate(
            flops=12 * count * rows * width * hidden,
            bytes_accessed=12 * count * width * hidden + 4 * count * rows * (width + hidden),
            transcendentals=count * rows * hidden,
        ),
        name="experts_backward",
    )(*operands, *after)


def passed_along(block, axis, distance):
    devices = range(lax.axis_size(axis))
    route = [(i - distance, i) for i in devices if i - distance in devices]
    return lax.ppermute(block, axis, route)


def earlier_rows(block, hop_count):
    pieces = [passed_along(block, "context", hop) for hop in range(hop_count, 0, -1)]
    missing = WINDOW - hop_count * block.shape[-2]
    if missing > 0:
        shape = block.shape[:-2] + (missing, block.shape[-1])
        pieces = [jnp.zeros(shape, block.dtype)] + pieces
    rows = pieces[0] if len(pieces) == 1 else jnp.concatenate(pieces, axis=-2)
    return rows[..., rows.shape[-2] - WINDOW :, :]


def returned_rows(block, length, hop_count):
    total = None
    for hop in range(1, hop_count + 1):
        first = WINDOW - hop * length
        part = block[max(first, 0) : first + length]
        if first < 0:
            part = jnp.concatenate([jnp.zeros((-first, block.shape[1]), block.dtype), part])
        part = passed_along(part, "context", -hop).astype(f32)
        total = part if total is None else total + part
    return total


def exchange(rows, groups, capacity):
    return lax.all_to_all(
        rows.reshape((EXPERTS // groups, groups, capacity) + rows.shape[1:]),
        "expert",
        split_axis=1,
        concat_axis=1,
        tiled=True,
    )


GATE, OF_NORMED, NORMED_SHARE, VECTOR_SHARE, MIX, SCALE, CHOSEN = 0, 2, 4, 5, 7, 9, 10
VECTOR_ROW, ATTN_GAIN_ROW, MOE_GAIN_ROW = 0, 2, 3


def inverse_rms(rows):
    return lax.rsqrt(jnp.mean(rows * rows, axis=-1, keepdims=True) + norm_eps)


def lane_iota(rows):
    return lax.broadcasted_iota(jnp.int32, (rows, LANES), 1)


def placed_on_lanes(rows, values):
    lane = lane_iota(rows)
    total = jnp.zeros((rows, LANES), f32)
    for index, value in values.items():
        total = jnp.where(lane == index, value, total)
    return total


def routing_kernel(groups, capacity, routes_ref, columns_ref, rows_ref):
    length = routes_ref.shape[1]
    lane = lane_iota(length)
    per_dev = EXPERTS // groups
    base = jnp.full((length, LANES), -1.0, f32)
    for e in range(EXPERTS):
        base = jnp.where(lane == e, float(e % per_dev * groups * capacity + e // per_dev * capacity), base)
    onehots = [(lane == routes_ref[0, :, k : k + 1]).astype(f32) for k in range(TOP)]
    counts = (onehots[0] + onehots[1]).astype(bf16)
    earlier = lax.broadcasted_iota(jnp.int32, (length, length), 0) > lax.broadcasted_iota(
        jnp.int32, (length, length), 1
    )
    rank = dot_on(jnp.where(earlier, 1.0, 0.0).astype(bf16), counts, 1, 0)
    place = base + jnp.where(lane < EXPERTS, rank, 0.0)
    slots = placed_on_lanes(
        length,
        {k: jnp.sum(onehots[k] * place, axis=1, keepdims=True) for k in range(TOP)},
    )
    columns_ref[0] = slots.astype(jnp.int32)
    rows_ref[0] = jnp.round(rows_of(slots, range(TOP))).astype(jnp.int32)


def routing_slots(routes, groups, capacity):
    count, length, _ = routes.shape
    return pl.pallas_call(
        functools.partial(routing_kernel, groups, capacity),
        grid=(count,),
        in_specs=[pl.BlockSpec((1, length, TOP), lambda m: (m, 0, 0))],
        out_specs=[
            pl.BlockSpec((1, length, LANES), lambda m: (m, 0, 0)),
            pl.BlockSpec((1, 8, length), lambda m: (m, 0, 0)),
        ],
        out_shape=[
            jax.ShapeDtypeStruct((count, length, LANES), jnp.int32),
            jax.ShapeDtypeStruct((count, 8, length), jnp.int32),
        ],
        compiler_params=pltpu.CompilerParams(vmem_limit_bytes=32 * MIB),
        cost_estimate=pl.CostEstimate(
            flops=2 * count * length * length * LANES, bytes_accessed=count * length * 1024,
            transcendentals=0,
        ),
        name="routing",
    )(routes)


def dispatch_kernel(mode, rows_ref, slots_ref, gates_ref, *rest):
    out_ref = rest[-1]
    count, length = out_ref.shape[0], rows_ref.shape[0]
    width = rows_ref.shape[1]
    slot = pl.program_id(0) * count + lax.broadcasted_iota(jnp.int32, (count, length), 0)
    hits = [slot == slots_ref[k : k + 1, :] for k in range(TOP)]
    table = jnp.where(hits[0] | hits[1], 1.0, 0.0).astype(bf16)
    found = dot_on(table, rows_ref[...].astype(bf16), 1, 0)
    if mode == "plain":
        out_ref[...] = found.astype(bf16)
        return
    gate = jnp.sum(
        jnp.where(hits[0], gates_ref[0:1, :], 0.0) + jnp.where(hits[1], gates_ref[1:2, :], 0.0),
        axis=1,
        keepdims=True,
    )
    if mode == "scaled":
        out_ref[...] = (found * gate).astype(bf16)
        return
    out_ref[:, :width] = found.astype(bf16)
    coarse = gate.astype(bf16).astype(f32)
    out_ref[:, width:] = placed_on_lanes(count, {0: coarse, 1: gate - coarse}).astype(bf16)


def dispatch(rows, slot_rows, gate_rows, mode, slots, after=()):
    length, width = rows.shape
    count = min(256, slots)
    out_width = width + LANES if mode == "with gate" else width
    return pl.pallas_call(
        functools.partial(dispatch_kernel, mode),
        grid=(slots // count,),
        in_specs=[
            pl.BlockSpec((length, width), lambda s: (0, 0)),
            pl.BlockSpec((8, length), lambda s: (0, 0)),
            pl.BlockSpec((8, length), lambda s: (0, 0)),
        ]
        + [ANY_SPEC] * len(after),
        out_specs=pl.BlockSpec((count, out_width), lambda s: (s, 0)),
        out_shape=jax.ShapeDtypeStruct((slots, out_width), bf16),
        compiler_params=pltpu.CompilerParams(vmem_limit_bytes=24 * MIB),
        cost_estimate=pl.CostEstimate(
            flops=2 * slots * length * out_width,
            bytes_accessed=2 * (slots + length) * width, transcendentals=0,
        ),
        name="dispatch",
    )(rows, slot_rows, gate_rows, *after)


def attention_output_kernel(
    hidden_ref, attended_ref, out_w_ref, small_w_ref, vectors_ref, prior_ref, residual_ref,
    routes_ref, mid_ref, low_ref, logits_ref, scalars_ref, gates_ref,
):
    rows = hidden_ref.shape[0]
    mid = hidden_ref[...] + dot_on(attended_ref[...], out_w_ref[...], 1, 0)
    mid_ref[...] = mid
    scale = inverse_rms(mid)
    low = (mid * scale * vectors_ref[MOE_GAIN_ROW : MOE_GAIN_ROW + 1, :]).astype(bf16)
    low_ref[...] = low
    logits = dot_on(low, small_w_ref[...], 1, 0) + jnp.dot(
        prior_ref[...], residual_ref[...], precision=highest
    )
    logits_ref[...] = logits
    lane = lane_iota(rows)
    onehots = [lane == routes_ref[:, k : k + 1] for k in range(TOP)]

    def lane_sum(values):
        return jnp.sum(values, axis=1, keepdims=True)

    difference = lane_sum(jnp.where(onehots[0], logits, jnp.where(onehots[1], -logits, 0.0)))
    gates = (sigmoid(difference), sigmoid(-difference))
    chosen = [
        [jnp.where(routes_ref[:, k : k + 1] == EXPERTS + 2 + j, 1.0, 0.0) for j in range(2)]
        for k in range(TOP)
    ]
    alphas = []
    for j in range(2):
        at = ROUTED + 2 * j
        gap = lane_sum(jnp.where(lane == at, logits, jnp.where(lane == at + 1, -logits, 0.0)))
        alphas.append((sigmoid(gap), sigmoid(-gap)))
    of_normed = [
        jnp.where(routes_ref[:, k : k + 1] == EXPERTS + 1, 1.0, 0.0)
        + chosen[k][0] * alphas[0][0]
        + chosen[k][1] * alphas[1][0]
        for k in range(TOP)
    ]
    vector_gate = [gates[0] * chosen[0][j] + gates[1] * chosen[1][j] for j in range(2)]
    values = {
        GATE: gates[0], GATE + 1: gates[1],
        OF_NORMED: of_normed[0], OF_NORMED + 1: of_normed[1],
        NORMED_SHARE: gates[0] * of_normed[0] + gates[1] * of_normed[1],
        SCALE: scale,
    }
    for j in range(2):
        values[VECTOR_SHARE + j] = vector_gate[j] * alphas[j][1]
        values[MIX + j] = vector_gate[j] * alphas[j][0] * alphas[j][1]
        for k in range(TOP):
            values[CHOSEN + 2 * k + j] = chosen[k][j] * alphas[j][1]
    scalars = placed_on_lanes(rows, values)
    scalars_ref[...] = scalars
    gates_ref[...] = rows_of(scalars, (GATE, GATE + 1))


def attention_output(hidden, attended, weights, prior, routes):
    length, width = hidden.shape
    rows = min(256, length)
    wide = pl.BlockSpec((rows, width), lambda t: (t, 0))
    lanes = pl.BlockSpec((rows, LANES), lambda t: (t, 0))
    return pl.pallas_call(
        attention_output_kernel,
        grid=(length // rows,),
        in_specs=[
            wide,
            wide,
            pl.BlockSpec((width, width), lambda t: (0, 3)),
            pl.BlockSpec((width, LANES), lambda t: (0, 4 * width // LANES)),
            pl.BlockSpec((8, width), lambda t: (0, 0)),
            lanes,
            pl.BlockSpec((LANES, LANES), lambda t: (0, 0)),
            pl.BlockSpec((rows, TOP), lambda t: (t, 0)),
        ],
        out_specs=[wide, wide, lanes, lanes, pl.BlockSpec((8, rows), lambda t: (0, t))],
        out_shape=[
            jax.ShapeDtypeStruct((length, width), f32),
            jax.ShapeDtypeStruct((length, width), bf16),
            jax.ShapeDtypeStruct((length, LANES), f32),
            jax.ShapeDtypeStruct((length, LANES), f32),
            jax.ShapeDtypeStruct((8, length), f32),
        ],
        compiler_params=pltpu.CompilerParams(vmem_limit_bytes=24 * MIB),
        cost_estimate=pl.CostEstimate(
            flops=2 * length * width * (width + LANES), bytes_accessed=14 * length * width,
            transcendentals=length,
        ),
        name="attention_output",
    )(
        hidden, attended, weights["dense"], weights["dense"], weights["vectors"], prior,
        weights["residual"], routes,
    )


def selection(columns, slots, which):
    slot = lax.broadcasted_iota(jnp.int32, (columns.shape[0], slots), 1)
    hit = slot == columns[:, which[0] : which[0] + 1]
    for k in which[1:]:
        hit = hit | (slot == columns[:, k : k + 1])
    return jnp.where(hit, 1.0, 0.0).astype(bf16)


def combine_kernel(
    last, back_ref, columns_ref, mid_ref, scalars_ref, vectors_ref, next_ref, *out_refs
):
    columns, scalars = columns_ref[...], scalars_ref[...]
    slots = back_ref.shape[0]
    mid = mid_ref[...]
    normed = mid * scalars[:, SCALE : SCALE + 1] * vectors_ref[MOE_GAIN_ROW : MOE_GAIN_ROW + 1, :]
    total = mid + scalars[:, NORMED_SHARE : NORMED_SHARE + 1] * normed
    for j in range(2):
        row = vectors_ref[VECTOR_ROW + j : VECTOR_ROW + j + 1, :]
        total += scalars[:, VECTOR_SHARE + j : VECTOR_SHARE + j + 1] * row
    for k in range(TOP):
        branch = dot_on(selection(columns, slots, (k,)), back_ref[...], 1, 0)
        out_refs[k][...] = branch.astype(bf16)
        total += scalars[:, GATE + k : GATE + k + 1] * branch
    if last:
        out_refs[TOP][...] = total.astype(bf16)
    else:
        out_refs[TOP][...] = total
        out_refs[TOP + 1][...] = (
            total * inverse_rms(total) * next_ref[ATTN_GAIN_ROW : ATTN_GAIN_ROW + 1, :]
        ).astype(bf16)


def combine(back, columns, mid, scalars, vectors, next_vectors):
    last = next_vectors is None
    length, width = mid.shape
    slots = back.shape[0]
    rows = min(256, length)
    wide = pl.BlockSpec((rows, width), lambda t: (t, 0))
    lanes = pl.BlockSpec((rows, LANES), lambda t: (t, 0))
    vector_spec = pl.BlockSpec((8, width), lambda t: (0, 0))
    low = jax.ShapeDtypeStruct((length, width), bf16)
    return pl.pallas_call(
        functools.partial(combine_kernel, last),
        grid=(length // rows,),
        in_specs=[
            pl.BlockSpec((slots, width), lambda t: (0, 0)), lanes, wide, lanes, vector_spec,
            vector_spec,
        ],
        out_specs=[wide] * (TOP + 1 if last else TOP + 2),
        out_shape=[low, low, low]
        if last
        else [low, low, jax.ShapeDtypeStruct((length, width), f32), low],
        compiler_params=pltpu.CompilerParams(vmem_limit_bytes=24 * MIB),
        cost_estimate=pl.CostEstimate(
            flops=4 * slots * length * width, bytes_accessed=(2 * slots + 14 * length) * width,
            transcendentals=0,
        ),
        name="combine",
    )(back, columns, mid, scalars, vectors, vectors if last else next_vectors)


def token_backward_kernel(
    has_prior, back_ref, columns_ref, grad_ref, mid_ref, scalars_ref, branch0_ref, branch1_ref,
    low_ref, prior_ref, attended_ref, routes_ref, out_w_ref, small_w_ref, vectors_ref,
    residual_ref, *rest
):
    d_mid_ref, d_att_ref, d_prior_ref, g_out_ref, g_small_ref, g_residual_ref, g_gain_ref = (
        rest[-7:]
    )
    step = pl.program_id(0)
    rows = mid_ref.shape[0]
    columns, scalars = columns_ref[...], scalars_ref[...]
    grad = grad_ref[...].astype(f32)
    mid = mid_ref[...]
    gain = vectors_ref[MOE_GAIN_ROW : MOE_GAIN_ROW + 1, :]
    scale = scalars[:, SCALE : SCALE + 1]
    unit = mid * scale
    lane = lane_iota(rows)

    def scalar(index):
        return scalars[:, index : index + 1]

    def row_sum(values):
        return jnp.sum(values, axis=1, keepdims=True)

    along = row_sum(grad * (unit * gain))
    along_vector = [
        row_sum(grad * vectors_ref[VECTOR_ROW + j : VECTOR_ROW + j + 1, :]) for j in range(2)
    ]
    d_gate = []
    for k, branch_ref in enumerate((branch0_ref, branch1_ref)):
        value = row_sum(grad * branch_ref[...].astype(f32)) + scalar(OF_NORMED + k) * along
        for j in range(2):
            value += scalar(CHOSEN + 2 * k + j) * along_vector[j]
        d_gate.append(value)
    d_choice = scalar(GATE) * scalar(GATE + 1) * (d_gate[0] - d_gate[1])
    d_small = jnp.where(
        lane == routes_ref[:, 0:1], d_choice, jnp.where(lane == routes_ref[:, 1:2], -d_choice, 0.0)
    )
    if has_prior:
        d_small += jnp.where(lane < ROUTED, rest[0][...], 0.0)
    d_logits = d_small
    for j in range(2):
        value = scalar(MIX + j) * (along - along_vector[j])
        at = ROUTED + 2 * j
        d_small = jnp.where(lane == at, value, jnp.where(lane == at + 1, -value, d_small))
    d_small_low = d_small.astype(bf16)
    d_prior_ref[...] = lax.dot_general(
        d_logits, residual_ref[...], (((1,), (1,)), ((), ())), precision=highest
    )
    vector_shares = placed_on_lanes(
        rows, {ROUTED + 4 + j: scalar(VECTOR_SHARE + j) for j in range(2)}
    ).astype(bf16)
    g_small = dot_on(low_ref[...], d_small_low, 0, 0) + dot_on(
        grad.astype(bf16), vector_shares, 0, 0
    )
    g_residual = lax.dot_general(
        prior_ref[...], d_logits, (((0,), (0,)), ((), ())), precision=highest
    )
    d_normed = (
        dot_on(selection(columns, back_ref.shape[0], (0, 1)), back_ref[...], 1, 0)
        + scalar(NORMED_SHARE) * grad
        + dot_on(d_small_low, small_w_ref[...], 1, 1)
    )
    g_gain = jnp.sum(d_normed * unit, axis=0, keepdims=True)
    d_unit = d_normed * gain
    d_mid = grad + (d_unit - unit * jnp.mean(d_unit * unit, axis=-1, keepdims=True)) * scale
    d_mid_ref[...] = d_mid
    d_mid_low = d_mid.astype(bf16)
    d_att_ref[...] = dot_on(d_mid_low, out_w_ref[...], 1, 1).astype(bf16)
    g_out = dot_on(attended_ref[...], d_mid_low, 0, 0)

    @pl.when(step == 0)
    def _():
        g_out_ref[...] = g_out
        g_small_ref[...] = g_small
        g_residual_ref[...] = g_residual
        g_gain_ref[...] = jnp.broadcast_to(g_gain, g_gain_ref.shape)

    @pl.when(step > 0)
    def _():
        g_out_ref[...] += g_out
        g_small_ref[...] += g_small
        g_residual_ref[...] += g_residual
        g_gain_ref[...] += jnp.broadcast_to(g_gain, g_gain_ref.shape)


def token_backward(back, kept, grad, weights, columns, routes, d_prior, after):
    length, width = grad.shape
    slots = back.shape[0]
    rows = min(256, length)
    wide = pl.BlockSpec((rows, width), lambda t: (t, 0))
    lanes = pl.BlockSpec((rows, LANES), lambda t: (t, 0))

    def fixed(*shape, at=0):
        return pl.BlockSpec(shape, lambda t: (0, at))

    operands = [
        back, columns, grad, kept["mid"], kept["scalars"], kept["branch"][0], kept["branch"][1],
        kept["low"], kept["prior"], kept["attended"], routes, weights["dense"], weights["dense"],
        weights["vectors"], weights["residual"],
    ]
    specs = [
        fixed(slots, width), lanes, wide, wide, lanes, wide, wide, wide, lanes, wide,
        pl.BlockSpec((rows, TOP), lambda t: (t, 0)), fixed(width, width, at=3),
        fixed(width, LANES, at=4 * width // LANES), fixed(8, width), fixed(LANES, LANES),
    ]
    if d_prior is not None:
        operands.append(d_prior)
        specs.append(lanes)
    return pl.pallas_call(
        functools.partial(token_backward_kernel, d_prior is not None),
        grid=(length // rows,),
        in_specs=specs + [ANY_SPEC] * len(after),
        out_specs=[
            wide, wide, lanes, fixed(width, width), fixed(width, LANES), fixed(LANES, LANES),
            fixed(8, width),
        ],
        out_shape=[
            jax.ShapeDtypeStruct((length, width), f32),
            jax.ShapeDtypeStruct((length, width), bf16),
            jax.ShapeDtypeStruct((length, LANES), f32),
            jax.ShapeDtypeStruct((width, width), f32),
            jax.ShapeDtypeStruct((width, LANES), f32),
            jax.ShapeDtypeStruct((LANES, LANES), f32),
            jax.ShapeDtypeStruct((8, width), f32),
        ],
        compiler_params=pltpu.CompilerParams(vmem_limit_bytes=48 * MIB),
        cost_estimate=pl.CostEstimate(
            flops=2 * length * width * (slots + 2 * width),
            bytes_accessed=(2 * slots + 24 * length) * width, transcendentals=0,
        ),
        name="token_backward",
    )(*operands, *after)


def fetch_layer(layer, local):
    width = local["w_query"].shape[2]
    shard = local["w_query"].shape[1]
    const_w = jnp.transpose(local["w_const"][layer], (1, 0, 2)).reshape(shard, 4)
    small = jnp.concatenate(
        [
            local["w_router"][layer], const_w, local["const_vec"][layer].T,
            local["norm_attn"][layer][:, None], local["norm_moe"][layer][:, None],
            jnp.zeros((shard, LANES - ROUTED - 8), bf16),
        ],
        axis=1,
    )
    packed = jnp.concatenate(
        [local["w_query"][layer], local["w_key"][layer], local["w_value"][layer],
         local["w_out"][layer], small],
        axis=1,
    )
    dense = lax.all_gather(packed, SHARDED, axis=0, tiled=True)
    gate_up = jnp.concatenate([local["w_gate"][layer], local["w_up"][layer]], axis=0)
    gate_up = lax.all_gather(gate_up, SHARDED, axis=1, tiled=True)
    down = lax.all_gather(local["w_down"][layer], SHARDED, axis=1, tiled=True)
    at = 4 * width + ROUTED + 4
    vectors = dense[:, at : at + 8].T.astype(f32)
    residual = local["w_res"][layer].astype(f32)
    blank = LANES - ROUTED
    return dict(
        dense=dense, vectors=vectors, gate_up=gate_up, down=down,
        residual=jnp.pad(residual, ((0, blank), (0, blank))),
    )


def per_device(
    hidden_in, segments, routes, prev_logits, out_grad, norm_attn, w_query, w_key, w_value,
    w_out, norm_moe, w_router, w_res, w_const, const_vec, w_gate, w_up, w_down,
):
    local = dict(
        norm_attn=norm_attn, w_query=w_query, w_key=w_key, w_value=w_value, w_out=w_out,
        norm_moe=norm_moe, w_router=w_router, w_res=w_res, w_const=w_const,
        const_vec=const_vec, w_gate=w_gate, w_up=w_up, w_down=w_down,
    )
    micro_count, _, length, width = hidden_in.shape
    micros = range(micro_count)
    layers = norm_attn.shape[0]
    groups = lax.axis_size("expert")
    hop_count = min((WINDOW + length - 2) // length, lax.axis_size("context") - 1)
    capacity = length // 4
    slots = EXPERTS * capacity
    block_start = lax.axis_index("context") * length
    hidden_earlier = earlier_rows(hidden_in[:, 0], hop_count)
    fetched = [fetch_layer(layer, local) for layer in range(layers)]
    routes = routes[:, 0]
    columns, slot_rows = routing_slots(routes, groups, capacity)
    blank_gates = jnp.zeros((8, length), f32)

    def to_experts(rows):
        return exchange(rows, groups, capacity).reshape(
            EXPERTS // groups, groups * capacity, rows.shape[1]
        )

    def to_tokens(rows):
        return exchange(rows.reshape(-1, width), groups, capacity).reshape(-1, width)

    def normed(hidden, gain):
        return (hidden * inverse_rms(hidden) * gain).astype(bf16)

    segs, early, state = [], [], []
    for micro in micros:
        whole = segments[micro, 0]
        padded = jnp.concatenate([jnp.full((WINDOW,), -1, jnp.int32), whole])
        query = lax.dynamic_slice_in_dim(whole, block_start, length, 0)
        key = lax.dynamic_slice_in_dim(padded, block_start, WINDOW + length, 0)
        segs.append((query, key))
        sent = dispatch(out_grad[micro, 0], slot_rows[micro], blank_gates, "plain", slots)
        early.append(to_experts(sent))
        hidden = hidden_in[micro, 0].astype(f32)
        gain = fetched[0]["vectors"][ATTN_GAIN_ROW : ATTN_GAIN_ROW + 1]
        prior = jnp.pad(prev_logits[micro, 0], ((0, 0), (0, LANES - ROUTED)))
        state.append(
            (
                hidden, normed(hidden, gain),
                normed(hidden_earlier[micro].astype(f32), gain), prior,
            )
        )

    saved = [[None] * layers for _ in micros]

    def attention_part(layer, micro, after):
        weights = fetched[layer]
        hidden, attn_in, attn_earlier, prior = state[micro]
        qkv = dot_on(attn_in, weights["dense"][:, : 3 * width], 1, 0).astype(bf16)
        kv_earlier = dot_on(attn_earlier, weights["dense"][:, width : 3 * width], 1, 0).astype(bf16)
        query, key = segs[micro]
        attended, lse = attention_forward(qkv, kv_earlier, query[:, None], key[None, :], after)
        mid, low, logits, scalars, gate_rows = attention_output(
            hidden, attended, weights, prior, routes[micro]
        )
        mode = "with gate" if layer == layers - 1 else "plain"
        sent = dispatch(low, slot_rows[micro], gate_rows, mode, slots)
        saved[micro][layer] = dict(
            hidden=hidden, attn_in=attn_in, attn_earlier=attn_earlier, prior=prior, qkv=qkv,
            kv_earlier=kv_earlier, attended=attended, lse=lse, mid=mid, low=low,
            scalars=scalars, gate_rows=gate_rows, logits=logits, arrived=to_experts(sent),
        )
        return sent

    def experts_part(layer, micro, after):
        kept = saved[micro][layer]
        produced, kept["gate_pre"], kept["up_pre"] = experts_forward(
            kept["arrived"], fetched[layer]["gate_up"], fetched[layer]["down"], after
        )
        kept["returned"] = to_tokens(produced)
        return produced

    def combine_part(layer, micro):
        kept = saved[micro][layer]
        last = layer == layers - 1
        outs = combine(
            kept["returned"], columns[micro], kept["mid"], kept["scalars"],
            fetched[layer]["vectors"], None if last else fetched[layer + 1]["vectors"],
        )
        kept["branch"] = outs[:TOP]
        if last:
            return outs[TOP]
        state[micro] = (
            outs[TOP], outs[TOP + 1], earlier_rows(outs[TOP + 1], hop_count), kept["logits"],
        )
        return None

    expert_sums = [None] * layers

    def experts_back_part(layer, micro, d_rows, after):
        kept = saved[micro][layer]
        dx, *expert_sums_new = experts_backward(
            kept["arrived"], d_rows, kept["gate_pre"], kept["up_pre"],
            fetched[layer]["gate_up"], fetched[layer]["down"], layer == layers - 1,
            expert_sums[layer], after,
        )
        expert_sums[layer] = tuple(expert_sums_new)
        kept["back"] = to_tokens(dx)
        return dx

    dense_parts = [[None] * micro_count for _ in range(layers)]
    residual_parts = [[None] * micro_count for _ in range(layers)]

    def attention_back_part(layer, micro, grad, d_prior, after):
        kept, weights = saved[micro][layer], fetched[layer]
        d_mid, d_att, d_prior, g_out, g_small, g_residual, g_moe_gain = token_backward(
            kept["back"], kept, grad, weights, columns[micro], routes[micro], d_prior, after
        )
        query, key = segs[micro]
        dq, dk, dv = attention_backward(
            kept["qkv"], kept["kv_earlier"], d_att, kept["attended"], kept["lse"],
            query[None, :], key[:, None], (),
        )
        dense = weights["dense"]
        query_w, key_w, value_w = (dense[:, i * width : (i + 1) * width] for i in range(3))
        d_earlier = (
            dot_on(dk[:WINDOW], key_w, 1, 1) + dot_on(dv[:WINDOW], value_w, 1, 1)
        ).astype(bf16)
        later = returned_rows(d_earlier, length, hop_count) if hop_count > 0 else 0.0
        d_attn = (
            dot_on(dq, query_w, 1, 1)
            + dot_on(dk[WINDOW:], key_w, 1, 1)
            + dot_on(dv[WINDOW:], value_w, 1, 1)
        )
        grads = [
            dot_on(kept["attn_in"], dq, 0, 0),
            dot_on(kept["attn_in"], dk[WINDOW:], 0, 0)
            + dot_on(kept["attn_earlier"], dk[:WINDOW], 0, 0),
            dot_on(kept["attn_in"], dv[WINDOW:], 0, 0)
            + dot_on(kept["attn_earlier"], dv[:WINDOW], 0, 0),
            g_out,
            g_small,
        ]
        residual_parts[layer][micro] = g_residual
        return d_mid, d_prior, d_attn, later, grads, g_moe_gain[0], dq

    def finish_back_part(layer, micro, parts):
        d_mid, d_prior, d_attn, later, grads, g_moe_gain, _ = parts
        hidden = saved[micro][layer]["hidden"]
        gain = fetched[layer]["vectors"][ATTN_GAIN_ROW : ATTN_GAIN_ROW + 1]
        d_attn = d_attn + later
        scale = inverse_rms(hidden)
        unit = hidden * scale
        g_attn_gain = jnp.sum(d_attn * unit, axis=0)
        d_unit = d_attn * gain
        d_hidden = d_mid + (
            d_unit - unit * jnp.mean(d_unit * unit, axis=-1, keepdims=True)
        ) * scale
        lane = jnp.arange(LANES)[None, :]
        grads[4] = (
            grads[4]
            + jnp.where(lane == ROUTED + 6, g_attn_gain[:, None], 0.0)
            + jnp.where(lane == ROUTED + 7, g_moe_gain[:, None], 0.0)
        )
        dense_parts[layer][micro] = grads
        return d_hidden, d_prior

    expert_shares, dense_shares = [None] * layers, [None] * layers

    def reduce_experts(layer):
        gate_up, down = expert_sums[layer]
        gate_up = gate_up.reshape((-1,) + gate_up.shape[2:])
        expert_shares[layer] = (
            lax.psum_scatter(gate_up, SHARDED, scatter_dimension=1, tiled=True),
            lax.psum_scatter(down, SHARDED, scatter_dimension=1, tiled=True),
        )
        return expert_shares[layer]

    def reduce_dense(layer):
        sums = [sum(parts[1:], parts[0]).astype(bf16) for parts in zip(*dense_parts[layer])]
        packed = jnp.concatenate(sums, axis=1)
        share = lax.psum_scatter(packed, SHARDED, scatter_dimension=0, tiled=True)
        dense_shares[layer] = lax.psum(share, "expert")
        return (dense_shares[layer],)

    last = layers - 1
    before = ()
    for layer in range(layers):
        for micro in micros:
            if layer > 0:
                combine_part(layer - 1, micro)
        for micro in micros:
            before = (attention_part(layer, micro, before),)
        for micro in micros:
            before = (experts_part(layer, micro, before),)
            if layer == last:
                before = (experts_back_part(layer, micro, early[micro], before),)
    hidden_out = [combine_part(last, micro) for micro in micros]
    expert_ready = reduce_experts(last)

    grads = [(out_grad[micro, 0], None) for micro in micros]
    waits = ()
    for layer in range(last, -1, -1):
        parts = []
        for micro in micros:
            parts.append(attention_back_part(layer, micro, *grads[micro], before + waits))
            before = (parts[-1][-1],)
        grads = [finish_back_part(layer, micro, parts[micro]) for micro in micros]
        if layer > 0:
            dense_ready = reduce_dense(layer)
            sent = [
                dispatch(
                    grads[micro][0], slot_rows[micro], saved[micro][layer - 1]["gate_rows"],
                    "scaled", slots, before,
                )
                for micro in micros
            ]
            before = (sent[-1],)
            d_rows = [to_experts(rows) for rows in sent]
            for micro in micros:
                before = (experts_back_part(layer - 1, micro, d_rows[micro], before),)
            waits = tuple(expert_ready)
            expert_ready = reduce_experts(layer - 1)
    reduce_dense(0)
    residual_total = lax.psum(
        jnp.stack([sum(parts[1:], parts[0]) for parts in residual_parts])[:, :ROUTED, :ROUTED],
        ("expert", "context", "dp"),
    )
    hidden_out = jnp.stack(hidden_out)[:, None]
    hidden_grad = jnp.stack([grad[0].astype(bf16) for grad in grads])[:, None]

    dense = jnp.stack(dense_shares).astype(f32)
    small = dense[:, :, 4 * width :]
    shard = small.shape[1]
    experts_total = [jnp.stack(parts).astype(f32) for parts in zip(*expert_shares)]
    per_dev = EXPERTS // groups
    return (
        hidden_out,
        hidden_grad,
        small[:, :, ROUTED + 6],
        dense[:, :, :width],
        dense[:, :, width : 2 * width],
        dense[:, :, 2 * width : 3 * width],
        dense[:, :, 3 * width : 4 * width],
        small[:, :, ROUTED + 7],
        small[:, :, :ROUTED],
        residual_total,
        jnp.transpose(
            small[:, :, ROUTED : ROUTED + 4].reshape(layers, shard, 2, 2), (0, 2, 1, 3)
        ),
        jnp.transpose(small[:, :, ROUTED + 4 : ROUTED + 6], (0, 2, 1)),
        experts_total[0][:, :per_dev],
        experts_total[0][:, per_dev:],
        experts_total[1],
    )


def solution(mesh):
    tokens = P(None, ("expert", "dp"), "context", None)
    rows = P(None, SHARDED, None)
    vector = P(None, SHARDED)
    experts = P(None, "expert", SHARDED, None)
    const = P(None, None, SHARDED, None)
    const_vector = P(None, None, SHARDED)
    return jax.shard_map(
        per_device,
        mesh=mesh,
        in_specs=(
            tokens, P(None, ("expert", "dp"), None), tokens, tokens, tokens, vector, rows, rows,
            rows, rows, vector, rows, P(), const, const_vector, experts, experts, experts,
        ),
        out_specs=(
            tokens, tokens, vector, rows, rows, rows, rows, vector, rows, P(), const,
            const_vector, experts, experts, experts,
        ),
        check_vma=False,
    )
```

```python
import functools

import jax
import jax.numpy as jnp
from jax import lax
from jax.experimental import pallas as pl
from jax.experimental.pallas import tpu as pltpu
from jax.sharding import PartitionSpec as P

HEADS = 12
HEAD_DIM = 64
EXPERTS = 8
TOP = 2
WINDOW = 1024
ROUTED = 12
LANES = 128
MIB = 1 << 20

norm_eps = 1e-05
masked = -1000000000.0
highest = lax.Precision.HIGHEST
f32 = jnp.float32
bf16 = jnp.bfloat16
SHARDED = ("context", "dp")


COST_SHARE = 0.8


def cost(microseconds):
    return pl.CostEstimate(
        flops=int(microseconds * COST_SHARE * 1.15e9), bytes_accessed=1, transcendentals=0
    )


ANY_SPEC = pl.BlockSpec(memory_space=pl.ANY)


def dot_on(left_op, right_op, left_dim, right_dim):
    return lax.dot_general(
        left_op,
        right_op,
        (((left_dim,), (right_dim,)), ((), ())),
        preferred_element_type=f32,
    )


def held(arrays, after):
    count = len(arrays)
    if not after:
        return list(arrays)
    return list(
        pl.pallas_call(
            lambda *refs: None,
            in_specs=[ANY_SPEC] * (count + len(after)),
            out_specs=[ANY_SPEC] * count,
            out_shape=[jax.ShapeDtypeStruct(array.shape, array.dtype) for array in arrays],
            input_output_aliases={index: index for index in range(count)},
            name="held",
        )(*arrays, *after)
    )


def rows_of(values, picks):
    count = 8 if len(picks) <= 8 else 16
    row = lax.broadcasted_iota(jnp.int32, (count, LANES), 0)
    lane = lax.broadcasted_iota(jnp.int32, (count, LANES), 1)
    pick = jnp.zeros((count, LANES), f32)
    for index, source in enumerate(picks):
        pick = jnp.where((row == index) & (lane == source), 1.0, pick)
    return lax.dot_general(
        pick, values, (((1,), (1,)), ((), ())), precision=highest, preferred_element_type=f32
    )


def join_spans(buffer_ref, earlier_ref, own_ref):
    buffer_ref[:WINDOW, :] = earlier_ref[...]
    buffer_ref[WINDOW:, :] = own_ref[...]


def attention_forward_kernel(
    rows, keys, blocks, q_ref, ko_ref, vo_ref, kp_ref, vp_ref, sq_ref, sk_ref, *rest
):
    out_ref, lse_rows_ref, lse_ref, bias_ref, k_ref, v_ref = rest[-6:]
    pair = pl.program_id(0)

    @pl.when(pair == 0)
    def _():
        lse_ref[...] = jnp.zeros_like(lse_ref)
        rel = lax.broadcasted_iota(jnp.int32, (rows, keys), 1) - lax.broadcasted_iota(
            jnp.int32, (rows, keys), 0
        )
        inside = (rel > 0) & (rel <= WINDOW)
        for block in range(blocks):
            first = block * rows
            same = sq_ref[first : first + rows, :] == sk_ref[:, first : first + keys]
            bias_ref[block] = jnp.where(inside & same, 0.0, masked)

    join_spans(k_ref, kp_ref, ko_ref)
    join_spans(v_ref, vp_ref, vo_ref)
    lane = lax.broadcasted_iota(jnp.int32, (rows, LANES), 1)
    low = lane < HEAD_DIM
    for block in range(blocks):
        own = slice(block * rows, (block + 1) * rows)
        span = slice(block * rows, block * rows + keys)
        query = q_ref[own, :] * (HEAD_DIM ** -0.5)
        key = k_ref[span, :]
        value = v_ref[span, :]
        heads_out = []
        for half in range(2):
            mine = low if half == 0 else ~low
            scores = (
                dot_on(jnp.where(mine, query, jnp.zeros_like(query)), key, 1, 1) + bias_ref[block]
            )
            row_max = jnp.max(scores, axis=1, keepdims=True)
            exponent = jnp.exp(scores - row_max)
            row_sum = jnp.sum(exponent, axis=1, keepdims=True)
            heads_out.append(dot_on(exponent.astype(bf16), value, 1, 0) * (1.0 / row_sum))
            lse_ref[own, :] = jnp.where(
                lane == 2 * pair + half, row_max + jnp.log(row_sum), lse_ref[own, :]
            )
        out_ref[own, :] = jnp.where(low, heads_out[0], heads_out[1]).astype(bf16)

    @pl.when(pair == pl.num_programs(0) - 1)
    def _():
        lse_rows_ref[...] = rows_of(lse_ref[...], range(HEADS))


def attention_forward(qkv, kv_earlier, seg_query, seg_key, after):
    length = qkv.shape[0]
    width = qkv.shape[1] // 3
    pairs = width // LANES
    rows = min(256, length)
    keys = rows + WINDOW
    blocks = length // rows
    span = WINDOW + length

    def column(count, offset):
        return pl.BlockSpec((count, LANES), lambda p: (0, offset + p))

    return pl.pallas_call(
        functools.partial(attention_forward_kernel, rows, keys, blocks),
        grid=(pairs,),
        in_specs=[
            column(length, 0),
            column(length, pairs),
            column(length, 2 * pairs),
            column(WINDOW, 0),
            column(WINDOW, pairs),
            pl.BlockSpec((length, 1), lambda p: (0, 0)),
            pl.BlockSpec((1, span), lambda p: (0, 0)),
        ]
        + [ANY_SPEC] * len(after),
        out_specs=[column(length, 0), pl.BlockSpec((16, length), lambda p: (0, 0))],
        out_shape=[
            jax.ShapeDtypeStruct((length, width), bf16),
            jax.ShapeDtypeStruct((16, length), f32),
        ],
        scratch_shapes=[
            pltpu.VMEM((length, LANES), f32),
            pltpu.VMEM((blocks, rows, keys), f32),
            pltpu.VMEM((span, LANES), bf16),
            pltpu.VMEM((span, LANES), bf16),
        ],
        compiler_params=pltpu.CompilerParams(vmem_limit_bytes=40 * MIB),
        cost_estimate=cost(32),
        name="attention_forward",
    )(qkv, qkv, qkv, kv_earlier, kv_earlier, seg_query, seg_key, *after)


def attention_backward_kernel(
    rows, keys, blocks, q_ref, ko_ref, vo_ref, kp_ref, vp_ref, do_ref, out_ref, lse_ref,
    sq_ref, sk_ref, *rest
):
    dq_ref, dk_ref, dv_ref, bias_ref, k_ref, v_ref, dk_sum, dv_sum = rest[-8:]
    pair = pl.program_id(0)

    @pl.when(pair == 0)
    def _():
        rel = lax.broadcasted_iota(jnp.int32, (keys, rows), 0) - lax.broadcasted_iota(
            jnp.int32, (keys, rows), 1
        )
        inside = (rel > 0) & (rel <= WINDOW)
        for block in range(blocks):
            first = block * rows
            same = sk_ref[first : first + keys, :] == sq_ref[:, first : first + rows]
            bias_ref[block] = jnp.where(inside & same, 0.0, masked)

    join_spans(k_ref, kp_ref, ko_ref)
    join_spans(v_ref, vp_ref, vo_ref)
    dk_sum[...] = jnp.zeros_like(dk_sum)
    dv_sum[...] = jnp.zeros_like(dv_sum)
    low = lax.broadcasted_iota(jnp.int32, (rows, LANES), 1) < HEAD_DIM
    ones = jnp.ones((8, LANES), bf16)
    for block in range(blocks):
        own = slice(block * rows, (block + 1) * rows)
        span = slice(block * rows, block * rows + keys)
        query = q_ref[own, :] * (HEAD_DIM ** -0.5)
        grad = do_ref[own, :]
        key = k_ref[span, :]
        value = v_ref[span, :]
        product = grad.astype(f32) * out_ref[own, :].astype(f32)
        heads_dq = []
        for half in range(2):
            mine = low if half == 0 else ~low
            query_h = jnp.where(mine, query, jnp.zeros_like(query))
            grad_h = jnp.where(mine, grad, jnp.zeros_like(grad))
            product_h = jnp.where(mine, product, 0.0)
            coarse = product_h.astype(bf16)
            fine = (product_h - coarse.astype(f32)).astype(bf16)
            delta = (dot_on(ones, coarse, 1, 1) + dot_on(ones, fine, 1, 1))[0:1, :]
            scores = dot_on(key, query_h, 1, 1) + bias_ref[block]
            probs = jnp.exp(scores - lse_ref[pl.ds(2 * pair + half, 1), own])
            d_probs = dot_on(value, grad_h, 1, 1)
            d_scores = (probs * (d_probs - delta)).astype(bf16)
            dv_sum[span, :] += dot_on(probs.astype(bf16), grad_h, 1, 0)
            dk_sum[span, :] += dot_on(d_scores, query_h, 1, 0)
            heads_dq.append(dot_on(d_scores, key, 0, 0))
        dq_ref[own, :] = (
            jnp.where(low, heads_dq[0], heads_dq[1]) * (HEAD_DIM ** -0.5)
        ).astype(bf16)
    dk_ref[...] = dk_sum[...].astype(bf16)
    dv_ref[...] = dv_sum[...].astype(bf16)


def attention_backward(qkv, kv_earlier, grad_att, attended, lse, seg_query, seg_key, after):
    length = qkv.shape[0]
    width = qkv.shape[1] // 3
    pairs = width // LANES
    rows = min(256, length)
    keys = rows + WINDOW
    blocks = length // rows
    span = WINDOW + length

    def column(count, offset):
        return pl.BlockSpec((count, LANES), lambda p: (0, offset + p))

    return pl.pallas_call(
        functools.partial(attention_backward_kernel, rows, keys, blocks),
        grid=(pairs,),
        in_specs=[
            column(length, 0),
            column(length, pairs),
            column(length, 2 * pairs),
            column(WINDOW, 0),
            column(WINDOW, pairs),
            column(length, 0),
            column(length, 0),
            pl.BlockSpec((16, length), lambda p: (0, 0)),
            pl.BlockSpec((1, length), lambda p: (0, 0)),
            pl.BlockSpec((span, 1), lambda p: (0, 0)),
        ]
        + [ANY_SPEC] * len(after),
        out_specs=[column(length, 0), column(span, 0), column(span, 0)],
        out_shape=[
            jax.ShapeDtypeStruct((length, width), bf16),
            jax.ShapeDtypeStruct((span, width), bf16),
            jax.ShapeDtypeStruct((span, width), bf16),
        ],
        scratch_shapes=[
            pltpu.VMEM((blocks, keys, rows), f32),
            pltpu.VMEM((span, LANES), bf16),
            pltpu.VMEM((span, LANES), bf16),
            pltpu.VMEM((span, LANES), f32),
            pltpu.VMEM((span, LANES), f32),
        ],
        compiler_params=pltpu.CompilerParams(vmem_limit_bytes=48 * MIB),
        cost_estimate=cost(48),
        name="attention_backward",
    )(
        qkv, qkv, qkv, kv_earlier, kv_earlier, grad_att, attended, lse, seg_query, seg_key, *after
    )


def sigmoid(values):
    return 1.0 / (1.0 + jnp.exp(-values))


def gathered(rows_ref, block_refs):
    count = block_refs[0].shape[0]
    width = rows_ref.shape[1]
    for index, block_ref in enumerate(block_refs):
        rows_ref[index * count : (index + 1) * count, :] = block_ref[:, :width]


def scattered(block_refs, rows, which=0):
    count = block_refs[0].shape[1]
    for index, block_ref in enumerate(block_refs):
        block_ref[which] = rows[index * count : (index + 1) * count, :].astype(bf16)


def experts_forward_kernel(groups, *refs):
    block_refs, (gate_w_ref, up_w_ref, down_w_ref) = refs[:groups], refs[groups : groups + 3]
    out_refs, (gate_ref, up_ref, rows_ref) = refs[-groups - 3 : -3], refs[-3:]
    gathered(rows_ref, block_refs)
    rows_in = rows_ref[...]
    gate_pre = dot_on(rows_in, gate_w_ref[0], 1, 0)
    up_pre = dot_on(rows_in, up_w_ref[0], 1, 0)
    activated = (gate_pre * sigmoid(gate_pre) * up_pre).astype(bf16)
    gate_ref[0] = gate_pre.astype(bf16)
    up_ref[0] = up_pre.astype(bf16)
    scattered(out_refs, dot_on(activated, down_w_ref[0], 1, 0))


def experts_forward(blocks, gate_up_w, down_w, after):
    groups = len(blocks)
    count = down_w.shape[0]
    width, hidden = gate_up_w.shape[1:]
    part = blocks[0].shape[0] // count
    rows = groups * part
    block_spec = pl.BlockSpec((part, width), lambda j: (j, 0))
    hidden_spec = pl.BlockSpec((1, rows, hidden), lambda j: (j, 0, 0))
    hidden_shape = jax.ShapeDtypeStruct((count, rows, hidden), bf16)
    *produced, gate_pre, up_pre = pl.pallas_call(
        functools.partial(experts_forward_kernel, groups),
        grid=(count,),
        in_specs=[block_spec] * groups
        + [
            pl.BlockSpec((1, width, hidden), lambda j: (j, 0, 0)),
            pl.BlockSpec((1, width, hidden), lambda j: (count + j, 0, 0)),
            pl.BlockSpec((1, hidden, width), lambda j: (j, 0, 0)),
        ]
        + [ANY_SPEC] * len(after),
        out_specs=[pl.BlockSpec((1, part, width), lambda j: (0, j, 0))] * groups
        + [hidden_spec, hidden_spec],
        out_shape=[jax.ShapeDtypeStruct((1, count * part, width), bf16)] * groups
        + [hidden_shape, hidden_shape],
        scratch_shapes=[pltpu.VMEM((rows, width), bf16)],
        compiler_params=pltpu.CompilerParams(vmem_limit_bytes=48 * MIB),
        cost_estimate=cost(26),
        name="experts_forward",
    )(*blocks, gate_up_w, gate_up_w, down_w, *after)
    return produced, gate_pre, up_pre


def experts_backward_kernel(groups, chunks, whole, has_sums, *refs):
    block_refs, d_refs, given = refs[:groups], refs[groups : 2 * groups], refs[2 * groups :]
    gate_w_ref, up_w_ref, down_w_ref = given[:3]
    if whole:
        share_refs, given = given[3 : 3 + groups], given[3 + groups :]
        *refs, produced_ref = refs
    else:
        (gate_ref, up_ref), given = given[3:5], given[5:]
    out_refs = refs[-5 - groups : -5]
    gate_up_grad_ref, down_grad_ref, total_ref, rows_ref, d_ref = refs[-5:]
    chunk = pl.program_id(1)

    @pl.when(chunk == 0)
    def _():
        gathered(rows_ref, block_refs)
        if whole:
            count = d_refs[0].shape[0]
            for index in range(groups):
                share = share_refs[index][...].astype(f32)
                share = share[:, 0:1] + share[:, 1:2]
                d_ref[index * count : (index + 1) * count, :] = (
                    d_refs[index][...].astype(f32) * share
                ).astype(bf16)
        else:
            gathered(d_ref, d_refs)

    rows_in = rows_ref[...]
    d_out = d_ref[...]
    if whole:
        gate_pre = dot_on(rows_in, gate_w_ref[0], 1, 0)
        up_pre = dot_on(rows_in, up_w_ref[0], 1, 0)
    else:
        gate_pre = gate_ref[0].astype(f32)
        up_pre = up_ref[0].astype(f32)
    share = sigmoid(gate_pre)
    swish = gate_pre * share
    activated = (swish * up_pre).astype(bf16)
    d_act = dot_on(d_out, down_w_ref[0], 1, 1)
    d_gate = (d_act * up_pre * (share * (1.0 + gate_pre * (1.0 - share)))).astype(bf16)
    d_up = (d_act * swish).astype(bf16)
    part = dot_on(d_gate, gate_w_ref[0], 1, 1) + dot_on(d_up, up_w_ref[0], 1, 1)
    gate_grad = dot_on(rows_in, d_gate, 0, 0)
    up_grad = dot_on(rows_in, d_up, 0, 0)
    down_grad = dot_on(activated, d_out, 0, 0)
    if has_sums:
        gate_up_sum_ref, down_sum_ref = given[:2]
        gate_grad += gate_up_sum_ref[0, 0].astype(f32)
        up_grad += gate_up_sum_ref[1, 0].astype(f32)
        down_grad += down_sum_ref[0].astype(f32)
    gate_up_grad_ref[0, 0] = gate_grad.astype(bf16)
    gate_up_grad_ref[1, 0] = up_grad.astype(bf16)
    down_grad_ref[0] = down_grad.astype(bf16)
    sums = [(total_ref, part)]
    if whole:
        sums.append((produced_ref, dot_on(activated, down_w_ref[0], 1, 0)))

    @pl.when(chunk == 0)
    def _():
        for sum_ref, value in sums:
            sum_ref[...] = value

    @pl.when(chunk > 0)
    def _():
        for sum_ref, value in sums:
            sum_ref[...] += value

    @pl.when(chunk == chunks - 1)
    def _():
        scattered(out_refs, total_ref[...], len(sums) - 1)
        if whole:
            scattered(out_refs, produced_ref[...])


def experts_backward(blocks, d_blocks, pre, gate_up_w, down_w, sums, after):
    groups = len(blocks)
    count, hidden, width = down_w.shape
    part = blocks[0].shape[0] // count
    rows = groups * part
    whole = pre is None
    chunk = min(512, hidden)
    chunks = hidden // chunk
    block_spec = pl.BlockSpec((part, width), lambda j, f: (j, 0))
    hidden_spec = pl.BlockSpec((1, rows, chunk), lambda j, f: (j, 0, f))
    wide_spec = pl.BlockSpec((1, width, chunk), lambda j, f: (j, 0, f))
    up_spec = pl.BlockSpec((1, width, chunk), lambda j, f: (count + j, 0, f))
    tall_spec = pl.BlockSpec((1, chunk, width), lambda j, f: (j, f, 0))
    both_spec = pl.BlockSpec((2, 1, width, chunk), lambda j, f: (0, j, 0, f))
    operands = [*blocks, *d_blocks, gate_up_w, gate_up_w, down_w]
    specs = [block_spec] * (2 * groups) + [wide_spec, up_spec, tall_spec]
    if whole:
        operands.extend(blocks)
        specs += [pl.BlockSpec((part, LANES), lambda j, f: (j, width // LANES))] * groups
    else:
        operands.extend(pre)
        specs += [hidden_spec, hidden_spec]
    if sums is not None:
        operands.extend(sums)
        specs.extend([both_spec, tall_spec])
    outs = 2 if whole else 1
    *out, gate_up_grad, down_grad = pl.pallas_call(
        functools.partial(experts_backward_kernel, groups, chunks, whole, sums is not None),
        grid=(count, chunks),
        in_specs=specs + [ANY_SPEC] * len(after),
        out_specs=[pl.BlockSpec((outs, part, width), lambda j, f: (0, j, 0))] * groups
        + [both_spec, tall_spec],
        out_shape=[jax.ShapeDtypeStruct((outs, count * part, width), bf16)] * groups
        + [
            jax.ShapeDtypeStruct((2, count, width, hidden), bf16),
            jax.ShapeDtypeStruct((count, hidden, width), bf16),
        ],
        scratch_shapes=[
            pltpu.VMEM((rows, width), f32),
            pltpu.VMEM((rows, width), bf16),
            pltpu.VMEM((rows, width), bf16),
        ]
        + ([pltpu.VMEM((rows, width), f32)] if whole else []),
        compiler_params=pltpu.CompilerParams(vmem_limit_bytes=58 * MIB),
        cost_estimate=cost(75 if whole else 52),
        name="experts_whole" if whole else "experts_backward",
    )(*operands, *after)
    return out, (gate_up_grad, down_grad)


def passed_along(block, axis, distance):
    devices = range(lax.axis_size(axis))
    route = [(i - distance, i) for i in devices if i - distance in devices]
    return lax.ppermute(block, axis, route)


def earlier_rows(block, hop_count):
    pieces = [passed_along(block, "context", hop) for hop in range(hop_count, 0, -1)]
    missing = WINDOW - hop_count * block.shape[-2]
    if missing > 0:
        shape = block.shape[:-2] + (missing, block.shape[-1])
        pieces = [jnp.zeros(shape, block.dtype)] + pieces
    rows = pieces[0] if len(pieces) == 1 else jnp.concatenate(pieces, axis=-2)
    return rows[..., rows.shape[-2] - WINDOW :, :]


def returned_rows(block, length, hop_count):
    total = None
    for hop in range(1, hop_count + 1):
        first = WINDOW - hop * length
        part = block[max(first, 0) : first + length]
        if first < 0:
            part = jnp.concatenate([jnp.zeros((-first, block.shape[1]), block.dtype), part])
        part = passed_along(part, "context", -hop).astype(f32)
        total = part if total is None else total + part
    return total


def exchange(blocks, direction):
    groups = lax.axis_size("expert")
    out = []
    for d, block in enumerate(blocks):
        step = d * direction
        route = [(i, (i + step) % groups) for i in range(groups)]
        out.append(block if d == 0 else lax.ppermute(block, "expert", route))
    return out


GATE, OF_NORMED, NORMED_SHARE, VECTOR_SHARE, MIX, SCALE, CHOSEN = 0, 2, 4, 5, 7, 9, 10
GAINS_LANE = 2 * ROUTED + 8
VECTOR_ROW, ATTN_GAIN_ROW, MOE_GAIN_ROW = 0, 2, 3


def inverse_rms(rows):
    return lax.rsqrt(jnp.mean(rows * rows, axis=-1, keepdims=True) + norm_eps)


def lane_iota(rows):
    return lax.broadcasted_iota(jnp.int32, (rows, LANES), 1)


def placed_on_lanes(rows, values):
    lane = lane_iota(rows)
    total = jnp.zeros((rows, LANES), f32)
    for index, value in values.items():
        total = jnp.where(lane == index, value, total)
    return total


def routing_kernel(routes_ref, base_ref, columns_ref, rows_ref):
    length = routes_ref.shape[1]
    lane = lane_iota(length)
    onehots = [(lane == routes_ref[0, :, k : k + 1]).astype(f32) for k in range(TOP)]
    counts = (onehots[0] + onehots[1]).astype(bf16)
    earlier = lax.broadcasted_iota(jnp.int32, (length, length), 0) > lax.broadcasted_iota(
        jnp.int32, (length, length), 1
    )
    rank = dot_on(jnp.where(earlier, 1.0, 0.0).astype(bf16), counts, 1, 0)
    place = base_ref[...] + jnp.where(lane < EXPERTS, rank, 0.0)
    slots = placed_on_lanes(
        length,
        {k: jnp.sum(onehots[k] * place, axis=1, keepdims=True) for k in range(TOP)},
    )
    columns_ref[0] = slots.astype(jnp.int32)
    rows_ref[0] = jnp.round(rows_of(slots, range(TOP))).astype(jnp.int32)


def routing_slots(routes, groups, capacity):
    count, length, _ = routes.shape
    per_dev = EXPERTS // groups
    expert = jnp.arange(LANES)
    place = (expert // per_dev - lax.axis_index("expert")) % groups
    base = (place * per_dev + expert % per_dev) * capacity
    base = jnp.where(expert < EXPERTS, base, -1).astype(f32)[None, :]
    return pl.pallas_call(
        routing_kernel,
        grid=(count,),
        in_specs=[
            pl.BlockSpec((1, length, TOP), lambda m: (m, 0, 0)),
            pl.BlockSpec((1, LANES), lambda m: (0, 0)),
        ],
        out_specs=[
            pl.BlockSpec((1, length, LANES), lambda m: (m, 0, 0)),
            pl.BlockSpec((1, 8, length), lambda m: (m, 0, 0)),
        ],
        out_shape=[
            jax.ShapeDtypeStruct((count, length, LANES), jnp.int32),
            jax.ShapeDtypeStruct((count, 8, length), jnp.int32),
        ],
        compiler_params=pltpu.CompilerParams(vmem_limit_bytes=32 * MIB),
        cost_estimate=cost(4),
        name="routing",
    )(routes, base)


def dispatch_kernel(mode, per_group, groups, rows_ref, slots_ref, gates_ref, *rest):
    out_refs = rest[-groups:]
    count, length = out_refs[0].shape[0], rows_ref.shape[0]
    width = rows_ref.shape[1]
    rows = rows_ref[...].astype(bf16)
    for group, out_ref in enumerate(out_refs):
        first = group * per_group + pl.program_id(0) * count
        slot = first + lax.broadcasted_iota(jnp.int32, (count, length), 0)
        hits = [slot == slots_ref[k : k + 1, :] for k in range(TOP)]
        table = jnp.where(hits[0] | hits[1], 1.0, 0.0).astype(bf16)
        found = dot_on(table, rows, 1, 0)
        if mode == "plain":
            out_ref[...] = found.astype(bf16)
            continue
        gate = jnp.sum(
            jnp.where(hits[0], gates_ref[0:1, :], 0.0)
            + jnp.where(hits[1], gates_ref[1:2, :], 0.0),
            axis=1,
            keepdims=True,
        )
        if mode == "scaled":
            out_ref[...] = (found * gate).astype(bf16)
            continue
        out_ref[:, :width] = found.astype(bf16)
        coarse = gate.astype(bf16).astype(f32)
        out_ref[:, width:] = placed_on_lanes(count, {0: coarse, 1: gate - coarse}).astype(bf16)


def dispatch(rows, slot_rows, gate_rows, mode, slots, groups, after=()):
    length, width = rows.shape
    per_group = slots // groups
    count = min(256, per_group)
    out_width = width + LANES if mode == "with gate" else width
    return pl.pallas_call(
        functools.partial(dispatch_kernel, mode, per_group, groups),
        grid=(per_group // count,),
        in_specs=[
            pl.BlockSpec((length, width), lambda s: (0, 0)),
            pl.BlockSpec((8, length), lambda s: (0, 0)),
            pl.BlockSpec((8, length), lambda s: (0, 0)),
        ]
        + [ANY_SPEC] * len(after),
        out_specs=[pl.BlockSpec((count, out_width), lambda s: (s, 0))] * groups,
        out_shape=[jax.ShapeDtypeStruct((per_group, out_width), bf16)] * groups,
        compiler_params=pltpu.CompilerParams(vmem_limit_bytes=32 * MIB),
        cost_estimate=cost(6),
        name="dispatch",
    )(rows, slot_rows, gate_rows, *after)


def attention_output_kernel(
    hidden_ref, attended_ref, out_w_ref, small_w_ref, vectors_ref, prior_ref, residual_ref,
    routes_ref, mid_ref, low_ref, logits_ref, scalars_ref, gates_ref,
):
    rows = hidden_ref.shape[0]
    mid = hidden_ref[...] + dot_on(attended_ref[...], out_w_ref[...], 1, 0)
    mid_ref[...] = mid
    scale = inverse_rms(mid)
    low = (mid * scale * vectors_ref[MOE_GAIN_ROW : MOE_GAIN_ROW + 1, :]).astype(bf16)
    low_ref[...] = low
    logits = dot_on(low, small_w_ref[...], 1, 0) + jnp.dot(
        prior_ref[...], residual_ref[...], precision=highest
    )
    logits_ref[...] = logits
    lane = lane_iota(rows)
    onehots = [lane == routes_ref[:, k : k + 1] for k in range(TOP)]

    def lane_sum(values):
        return jnp.sum(values, axis=1, keepdims=True)

    difference = lane_sum(jnp.where(onehots[0], logits, jnp.where(onehots[1], -logits, 0.0)))
    gates = (sigmoid(difference), sigmoid(-difference))
    chosen = [
        [jnp.where(routes_ref[:, k : k + 1] == EXPERTS + 2 + j, 1.0, 0.0) for j in range(2)]
        for k in range(TOP)
    ]
    alphas = []
    for j in range(2):
        at = ROUTED + 2 * j
        gap = lane_sum(jnp.where(lane == at, logits, jnp.where(lane == at + 1, -logits, 0.0)))
        alphas.append((sigmoid(gap), sigmoid(-gap)))
    of_normed = [
        jnp.where(routes_ref[:, k : k + 1] == EXPERTS + 1, 1.0, 0.0)
        + chosen[k][0] * alphas[0][0]
        + chosen[k][1] * alphas[1][0]
        for k in range(TOP)
    ]
    vector_gate = [gates[0] * chosen[0][j] + gates[1] * chosen[1][j] for j in range(2)]
    values = {
        GATE: gates[0], GATE + 1: gates[1],
        OF_NORMED: of_normed[0], OF_NORMED + 1: of_normed[1],
        NORMED_SHARE: gates[0] * of_normed[0] + gates[1] * of_normed[1],
        SCALE: scale,
    }
    for j in range(2):
        values[VECTOR_SHARE + j] = vector_gate[j] * alphas[j][1]
        values[MIX + j] = vector_gate[j] * alphas[j][0] * alphas[j][1]
        for k in range(TOP):
            values[CHOSEN + 2 * k + j] = chosen[k][j] * alphas[j][1]
    scalars = placed_on_lanes(rows, values)
    scalars_ref[...] = scalars
    gates_ref[...] = rows_of(scalars, (GATE, GATE + 1))


def attention_output(hidden, attended, weights, prior, routes):
    length, width = hidden.shape
    rows = min(256, length)
    wide = pl.BlockSpec((rows, width), lambda t: (t, 0))
    lanes = pl.BlockSpec((rows, LANES), lambda t: (t, 0))
    return pl.pallas_call(
        attention_output_kernel,
        grid=(length // rows,),
        in_specs=[
            wide,
            wide,
            pl.BlockSpec((width, width), lambda t: (0, 3)),
            pl.BlockSpec((width, LANES), lambda t: (0, 4 * width // LANES)),
            pl.BlockSpec((8, width), lambda t: (0, 0)),
            lanes,
            pl.BlockSpec((LANES, LANES), lambda t: (0, 0)),
            pl.BlockSpec((rows, TOP), lambda t: (t, 0)),
        ],
        out_specs=[wide, wide, lanes, lanes, pl.BlockSpec((8, rows), lambda t: (0, t))],
        out_shape=[
            jax.ShapeDtypeStruct((length, width), f32),
            jax.ShapeDtypeStruct((length, width), bf16),
            jax.ShapeDtypeStruct((length, LANES), f32),
            jax.ShapeDtypeStruct((length, LANES), f32),
            jax.ShapeDtypeStruct((8, length), f32),
        ],
        compiler_params=pltpu.CompilerParams(vmem_limit_bytes=24 * MIB),
        cost_estimate=cost(8),
        name="attention_output",
    )(
        hidden, attended, weights["dense"], weights["dense"], weights["vectors"], prior,
        weights["residual"], routes,
    )


def selected(columns, block_refs, which):
    per_group = block_refs[0].shape[0]
    total = None
    for group, block_ref in enumerate(block_refs):
        slot = group * per_group + lax.broadcasted_iota(
            jnp.int32, (columns.shape[0], per_group), 1
        )
        hit = slot == columns[:, which[0] : which[0] + 1]
        for k in which[1:]:
            hit = hit | (slot == columns[:, k : k + 1])
        part = dot_on(jnp.where(hit, 1.0, 0.0).astype(bf16), block_ref[...], 1, 0)
        total = part if total is None else total + part
    return total


def combine_kernel(last, groups, waits, *refs):
    back_refs, (columns_ref, mid_ref, scalars_ref, vectors_ref, next_ref) = (
        refs[:groups], refs[groups : groups + 5],
    )
    out_refs = refs[groups + 5 + waits :]
    columns, scalars = columns_ref[...], scalars_ref[...]
    mid = mid_ref[...]
    normed = mid * scalars[:, SCALE : SCALE + 1] * vectors_ref[MOE_GAIN_ROW : MOE_GAIN_ROW + 1, :]
    total = mid + scalars[:, NORMED_SHARE : NORMED_SHARE + 1] * normed
    for j in range(2):
        row = vectors_ref[VECTOR_ROW + j : VECTOR_ROW + j + 1, :]
        total += scalars[:, VECTOR_SHARE + j : VECTOR_SHARE + j + 1] * row
    for k in range(TOP):
        branch = selected(columns, back_refs, (k,))
        out_refs[k][...] = branch.astype(bf16)
        total += scalars[:, GATE + k : GATE + k + 1] * branch
    if last:
        out_refs[TOP][...] = total.astype(bf16)
    else:
        out_refs[TOP][...] = total
        out_refs[TOP + 1][...] = (
            total * inverse_rms(total) * next_ref[ATTN_GAIN_ROW : ATTN_GAIN_ROW + 1, :]
        ).astype(bf16)


def combine(back, columns, mid, scalars, vectors, next_vectors, after):
    last = next_vectors is None
    length, width = mid.shape
    back, which = back
    groups, per_group = len(back), back[0].shape[1]
    rows = min(256, length)
    wide = pl.BlockSpec((rows, width), lambda t: (t, 0))
    lanes = pl.BlockSpec((rows, LANES), lambda t: (t, 0))
    vector_spec = pl.BlockSpec((8, width), lambda t: (0, 0))
    low = jax.ShapeDtypeStruct((length, width), bf16)
    return pl.pallas_call(
        functools.partial(combine_kernel, last, groups, len(after)),
        grid=(length // rows,),
        in_specs=[pl.BlockSpec((None, per_group, width), lambda t: (which, 0, 0))] * groups
        + [lanes, wide, lanes, vector_spec, vector_spec]
        + [ANY_SPEC] * len(after),
        out_specs=[wide] * (TOP + 1 if last else TOP + 2),
        out_shape=[low, low, low]
        if last
        else [low, low, jax.ShapeDtypeStruct((length, width), f32), low],
        compiler_params=pltpu.CompilerParams(vmem_limit_bytes=24 * MIB),
        cost_estimate=cost(8),
        name="combine",
    )(*back, columns, mid, scalars, vectors, vectors if last else next_vectors, *after)


def token_backward_kernel(
    has_prior, groups, *refs
):
    back_refs, rest = refs[:groups], refs[groups:]
    (
        columns_ref, grad_ref, mid_ref, scalars_ref, branch0_ref, branch1_ref, low_ref, prior_ref,
        attended_ref, routes_ref, out_w_ref, small_w_ref, vectors_ref, residual_ref,
    ) = rest[:14]
    rest = rest[14:]
    d_mid_ref, d_att_ref, d_prior_ref, g_out_ref, g_small_ref, g_residual_ref, g_gain_ref = (
        rest[-7:]
    )
    step = pl.program_id(0)
    rows = mid_ref.shape[0]
    columns, scalars = columns_ref[...], scalars_ref[...]
    grad = grad_ref[...].astype(f32)
    mid = mid_ref[...]
    gain = vectors_ref[MOE_GAIN_ROW : MOE_GAIN_ROW + 1, :]
    scale = scalars[:, SCALE : SCALE + 1]
    unit = mid * scale
    lane = lane_iota(rows)

    def scalar(index):
        return scalars[:, index : index + 1]

    def row_sum(values):
        return jnp.sum(values, axis=1, keepdims=True)

    along = row_sum(grad * (unit * gain))
    along_vector = [
        row_sum(grad * vectors_ref[VECTOR_ROW + j : VECTOR_ROW + j + 1, :]) for j in range(2)
    ]
    d_gate = []
    for k, branch_ref in enumerate((branch0_ref, branch1_ref)):
        value = row_sum(grad * branch_ref[...].astype(f32)) + scalar(OF_NORMED + k) * along
        for j in range(2):
            value += scalar(CHOSEN + 2 * k + j) * along_vector[j]
        d_gate.append(value)
    d_choice = scalar(GATE) * scalar(GATE + 1) * (d_gate[0] - d_gate[1])
    d_small = jnp.where(
        lane == routes_ref[:, 0:1], d_choice, jnp.where(lane == routes_ref[:, 1:2], -d_choice, 0.0)
    )
    if has_prior:
        d_small += jnp.where(lane < ROUTED, rest[0][...], 0.0)
    d_logits = d_small
    for j in range(2):
        value = scalar(MIX + j) * (along - along_vector[j])
        at = ROUTED + 2 * j
        d_small = jnp.where(lane == at, value, jnp.where(lane == at + 1, -value, d_small))
    d_small_low = d_small.astype(bf16)
    d_prior_ref[...] = lax.dot_general(
        d_logits, residual_ref[...], (((1,), (1,)), ((), ())), precision=highest
    )
    vector_shares = placed_on_lanes(
        rows, {ROUTED + 4 + j: scalar(VECTOR_SHARE + j) for j in range(2)}
    ).astype(bf16)
    g_small = dot_on(low_ref[...], d_small_low, 0, 0) + dot_on(
        grad.astype(bf16), vector_shares, 0, 0
    )
    g_residual = lax.dot_general(
        prior_ref[...], d_logits, (((0,), (0,)), ((), ())), precision=highest
    )
    d_normed = (
        selected(columns, back_refs, (0, 1))
        + scalar(NORMED_SHARE) * grad
        + dot_on(d_small_low, small_w_ref[...], 1, 1)
    )
    g_gain = jnp.sum(d_normed * unit, axis=0, keepdims=True)
    d_unit = d_normed * gain
    d_mid = grad + (d_unit - unit * jnp.mean(d_unit * unit, axis=-1, keepdims=True)) * scale
    d_mid_ref[...] = d_mid
    d_mid_low = d_mid.astype(bf16)
    d_att_ref[...] = dot_on(d_mid_low, out_w_ref[...], 1, 1).astype(bf16)
    g_out = dot_on(attended_ref[...], d_mid_low, 0, 0)

    @pl.when(step == 0)
    def _():
        g_out_ref[...] = g_out
        g_small_ref[...] = g_small
        g_residual_ref[...] = g_residual
        g_gain_ref[...] = jnp.broadcast_to(g_gain, g_gain_ref.shape)

    @pl.when(step > 0)
    def _():
        g_out_ref[...] += g_out
        g_small_ref[...] += g_small
        g_residual_ref[...] += g_residual
        g_gain_ref[...] += jnp.broadcast_to(g_gain, g_gain_ref.shape)


def token_backward(back, kept, grad, weights, columns, routes, d_prior, after):
    length, width = grad.shape
    back, which = back
    groups, per_group = len(back), back[0].shape[1]
    rows = min(256, length)
    wide = pl.BlockSpec((rows, width), lambda t: (t, 0))
    lanes = pl.BlockSpec((rows, LANES), lambda t: (t, 0))

    def fixed(*shape, at=0):
        return pl.BlockSpec(shape, lambda t: (0, at))

    operands = [
        *back, columns, grad, kept["mid"], kept["scalars"], kept["branch"][0], kept["branch"][1],
        kept["low"], kept["prior"], kept["attended"], routes, weights["dense"], weights["dense"],
        weights["vectors"], weights["residual"],
    ]
    specs = [
        *[pl.BlockSpec((None, per_group, width), lambda t: (which, 0, 0))] * groups,
        lanes, wide, wide, lanes, wide, wide, wide, lanes, wide,
        pl.BlockSpec((rows, TOP), lambda t: (t, 0)), fixed(width, width, at=3),
        fixed(width, LANES, at=4 * width // LANES), fixed(8, width), fixed(LANES, LANES),
    ]
    if d_prior is not None:
        operands.append(d_prior)
        specs.append(lanes)
    return pl.pallas_call(
        functools.partial(token_backward_kernel, d_prior is not None, groups),
        grid=(length // rows,),
        in_specs=specs + [ANY_SPEC] * len(after),
        out_specs=[
            wide, wide, lanes, fixed(width, width), fixed(width, LANES), fixed(LANES, LANES),
            fixed(8, width),
        ],
        out_shape=[
            jax.ShapeDtypeStruct((length, width), f32),
            jax.ShapeDtypeStruct((length, width), bf16),
            jax.ShapeDtypeStruct((length, LANES), f32),
            jax.ShapeDtypeStruct((width, width), f32),
            jax.ShapeDtypeStruct((width, LANES), f32),
            jax.ShapeDtypeStruct((LANES, LANES), f32),
            jax.ShapeDtypeStruct((8, width), f32),
        ],
        compiler_params=pltpu.CompilerParams(vmem_limit_bytes=48 * MIB),
        cost_estimate=cost(25),
        name="token_backward",
    )(*operands, *after)


def finish_backward_kernel(
    has_later, hidden_ref, d_mid_ref, d_attn_ref, vectors_ref, *rest
):
    out_ref, g_gain_ref = rest[-2:]
    hidden = hidden_ref[...]
    d_attn = d_attn_ref[...]
    if has_later:
        d_attn += rest[0][...].astype(f32)
    scale = inverse_rms(hidden)
    unit = hidden * scale
    g_gain = jnp.broadcast_to(jnp.sum(d_attn * unit, axis=0, keepdims=True), g_gain_ref.shape)
    d_unit = d_attn * vectors_ref[ATTN_GAIN_ROW : ATTN_GAIN_ROW + 1, :]
    out_ref[...] = (
        d_mid_ref[...] + (d_unit - unit * jnp.mean(d_unit * unit, axis=-1, keepdims=True)) * scale
    ).astype(out_ref.dtype)

    @pl.when(pl.program_id(0) == 0)
    def _():
        g_gain_ref[...] = g_gain

    @pl.when(pl.program_id(0) > 0)
    def _():
        g_gain_ref[...] += g_gain


def finish_backward(hidden, d_mid, d_attn, vectors, later, out_type, after):
    length, width = hidden.shape
    rows = min(256, length)
    wide = pl.BlockSpec((rows, width), lambda t: (t, 0))
    vector_spec = pl.BlockSpec((8, width), lambda t: (0, 0))
    extra = [] if later is None else [later]
    return pl.pallas_call(
        functools.partial(finish_backward_kernel, later is not None),
        grid=(length // rows,),
        in_specs=[wide, wide, wide, vector_spec] + [wide] * len(extra) + [ANY_SPEC] * len(after),
        out_specs=[wide, vector_spec],
        out_shape=[
            jax.ShapeDtypeStruct((length, width), out_type),
            jax.ShapeDtypeStruct((8, width), f32),
        ],
        compiler_params=pltpu.CompilerParams(vmem_limit_bytes=24 * MIB),
        cost_estimate=cost(6),
        name="finish_backward",
    )(hidden, d_mid, d_attn, vectors, *extra, *after)


def fetch_layer(layer, local):
    width = local["w_query"].shape[2]
    shard = local["w_query"].shape[1]
    const_w = jnp.transpose(local["w_const"][layer], (1, 0, 2)).reshape(shard, 4)
    small = jnp.concatenate(
        [
            local["w_router"][layer], const_w, local["const_vec"][layer].T,
            local["norm_attn"][layer][:, None], local["norm_moe"][layer][:, None],
            jnp.zeros((shard, LANES - ROUTED - 8), bf16),
        ],
        axis=1,
    )
    packed = jnp.concatenate(
        [local["w_query"][layer], local["w_key"][layer], local["w_value"][layer],
         local["w_out"][layer], small],
        axis=1,
    )
    dense = lax.all_gather(packed, SHARDED, axis=0, tiled=True)
    gate_up = jnp.concatenate([local["w_gate"][layer], local["w_up"][layer]], axis=0)
    gate_up = lax.all_gather(gate_up, SHARDED, axis=1, tiled=True)
    down = lax.all_gather(local["w_down"][layer], SHARDED, axis=1, tiled=True)
    at = 4 * width + ROUTED + 4
    vectors = dense[:, at : at + 8].T.astype(f32)
    residual = local["w_res"][layer].astype(f32)
    blank = LANES - ROUTED
    return dict(
        dense=dense, vectors=vectors, gate_up=gate_up, down=down,
        residual=jnp.pad(residual, ((0, blank), (0, blank))),
    )


def per_device(
    hidden_in, segments, routes, prev_logits, out_grad, norm_attn, w_query, w_key, w_value,
    w_out, norm_moe, w_router, w_res, w_const, const_vec, w_gate, w_up, w_down,
):
    local = dict(
        norm_attn=norm_attn, w_query=w_query, w_key=w_key, w_value=w_value, w_out=w_out,
        norm_moe=norm_moe, w_router=w_router, w_res=w_res, w_const=w_const,
        const_vec=const_vec, w_gate=w_gate, w_up=w_up, w_down=w_down,
    )
    micro_count, _, length, width = hidden_in.shape
    micros = range(micro_count)
    layers = norm_attn.shape[0]
    groups = lax.axis_size("expert")
    hop_count = min((WINDOW + length - 2) // length, lax.axis_size("context") - 1)
    capacity = length // 4
    slots = EXPERTS * capacity
    block_start = lax.axis_index("context") * length
    hidden_earlier = [earlier_rows(hidden_in[micro, 0], hop_count) for micro in micros]
    fetched = [fetch_layer(layer, local) for layer in range(layers)]
    routes = routes[:, 0]
    columns, slot_rows = routing_slots(routes, groups, capacity)
    blank_gates = jnp.zeros((8, length), f32)

    def normed(hidden, gain):
        return (hidden * inverse_rms(hidden) * gain).astype(bf16)

    segs, early, state = [], [], []
    for micro in micros:
        whole = segments[micro, 0]
        padded = jnp.concatenate([jnp.full((WINDOW,), -1, jnp.int32), whole])
        query = lax.dynamic_slice_in_dim(whole, block_start, length, 0)
        key = lax.dynamic_slice_in_dim(padded, block_start, WINDOW + length, 0)
        segs.append((query, key))
        sent = dispatch(out_grad[micro, 0], slot_rows[micro], blank_gates, "plain", slots, groups)
        early.append(exchange(sent, 1))
        hidden = hidden_in[micro, 0].astype(f32)
        gain = fetched[0]["vectors"][ATTN_GAIN_ROW : ATTN_GAIN_ROW + 1]
        prior = jnp.pad(prev_logits[micro, 0], ((0, 0), (0, LANES - ROUTED)))
        state.append(
            (
                hidden, normed(hidden, gain),
                normed(hidden_earlier[micro].astype(f32), gain), prior,
            )
        )

    saved = [[None] * layers for _ in micros]
    expert_sums = [None] * layers
    last_arrived = []

    def attention_part(layer, micro, after, after_output):
        weights = fetched[layer]
        hidden, attn_in, attn_earlier, prior = state[micro]
        qkv = dot_on(attn_in, weights["dense"][:, : 3 * width], 1, 0).astype(bf16)
        kv_earlier = dot_on(attn_earlier, weights["dense"][:, width : 3 * width], 1, 0).astype(bf16)
        query, key = segs[micro]
        attended, lse = attention_forward(qkv, kv_earlier, query[:, None], key[None, :], after)
        mid, low, logits, scalars, gate_rows = attention_output(
            hidden, attended, weights, prior, routes[micro]
        )
        mode = "with gate" if layer == layers - 1 else "plain"
        sent = dispatch(low, slot_rows[micro], gate_rows, mode, slots, groups, after_output)
        saved[micro][layer] = dict(
            hidden=hidden, attn_in=attn_in, attn_earlier=attn_earlier, prior=prior, qkv=qkv,
            kv_earlier=kv_earlier, attended=attended, lse=lse, mid=mid, low=low,
            scalars=scalars, gate_rows=gate_rows, logits=logits, arrived=exchange(sent, 1),
        )
        return sent[-1]

    def send_out(blocks, micro):
        own, others = blocks[:1], blocks[1:]
        others = held(others, last_arrived[1:] if micro > 0 else ())
        last_arrived[:] = exchange(list(own) + others, -1)
        return list(last_arrived)

    def experts_part(layer, micro, after):
        kept = saved[micro][layer]
        gate_up_w, down_w = fetched[layer]["gate_up"], fetched[layer]["down"]
        if layer == layers - 1:
            out, expert_sums[layer] = experts_backward(
                kept["arrived"], early[micro], None, gate_up_w, down_w, expert_sums[layer], after
            )
            arrived = send_out(out, micro)
            kept["returned"], kept["back"] = (arrived, 0), (arrived, 1)
        else:
            out, *kept["pre"] = experts_forward(kept["arrived"], gate_up_w, down_w, after)
            kept["returned"] = (send_out(out, micro), 0)
        return out[-1]

    def combine_part(layer, micro, after):
        kept = saved[micro][layer]
        last = layer == layers - 1
        outs = combine(
            kept["returned"], columns[micro], kept["mid"], kept["scalars"],
            fetched[layer]["vectors"], None if last else fetched[layer + 1]["vectors"], after,
        )
        kept["branch"] = outs[:TOP]
        if last:
            return outs[TOP]
        state[micro] = (
            outs[TOP], outs[TOP + 1], earlier_rows(outs[TOP + 1], hop_count), kept["logits"],
        )
        return outs[TOP]

    def experts_back_part(layer, micro, d_rows, after):
        kept = saved[micro][layer]
        dx, expert_sums[layer] = experts_backward(
            kept["arrived"], d_rows, kept["pre"], fetched[layer]["gate_up"],
            fetched[layer]["down"], expert_sums[layer], after,
        )
        kept["back"] = (send_out(dx, micro), 0)
        return dx[-1]

    def token_back_part(layer, micro, grad, d_prior, after):
        kept = saved[micro][layer]
        (
            kept["d_mid"], kept["d_att"], d_prior, kept["g_out"], kept["g_small"],
            kept["g_residual"], g_moe_gain,
        ) = token_backward(
            kept["back"], kept, grad, fetched[layer], columns[micro], routes[micro], d_prior, after
        )
        kept["g_moe_gain"] = g_moe_gain[0]
        return d_prior

    def attention_back_part(layer, micro, after):
        kept, dense = saved[micro][layer], fetched[layer]["dense"]
        query, key = segs[micro]
        dq, dk, dv = attention_backward(
            kept["qkv"], kept["kv_earlier"], kept["d_att"], kept["attended"], kept["lse"],
            query[None, :], key[:, None], after,
        )
        query_w, key_w, value_w = (dense[:, i * width : (i + 1) * width] for i in range(3))
        kept["later"] = None
        if hop_count > 0:
            d_earlier = (
                dot_on(dk[:WINDOW], key_w, 1, 1) + dot_on(dv[:WINDOW], value_w, 1, 1)
            ).astype(bf16)
            kept["later"] = returned_rows(d_earlier, length, hop_count)
        kept["d_attn"] = (
            dot_on(dq, query_w, 1, 1)
            + dot_on(dk[WINDOW:], key_w, 1, 1)
            + dot_on(dv[WINDOW:], value_w, 1, 1)
        )
        kept["grads"] = [
            dot_on(kept["attn_in"], dq, 0, 0),
            dot_on(kept["attn_in"], dk[WINDOW:], 0, 0)
            + dot_on(kept["attn_earlier"], dk[:WINDOW], 0, 0),
            dot_on(kept["attn_in"], dv[WINDOW:], 0, 0)
            + dot_on(kept["attn_earlier"], dv[:WINDOW], 0, 0),
            kept["g_out"],
            kept["g_small"],
        ]
        return dq

    def finish_back_part(layer, micro, after):
        kept = saved[micro][layer]
        d_hidden, g_attn_gain = finish_backward(
            kept["hidden"], kept["d_mid"], kept["d_attn"], fetched[layer]["vectors"],
            kept["later"], f32 if layer > 0 else bf16, after,
        )
        kept["g_attn_gain"] = g_attn_gain[0]
        return d_hidden

    expert_shares, dense_shares = [None] * layers, [None] * layers

    def reduce_experts(layer):
        gate_up, down = held(expert_sums[layer], saved[0][layer]["back"][0][1:])
        gate_up = gate_up.reshape((-1,) + gate_up.shape[2:])
        expert_shares[layer] = (
            lax.psum_scatter(gate_up, SHARDED, scatter_dimension=1, tiled=True),
            lax.psum_scatter(down, SHARDED, scatter_dimension=1, tiled=True),
        )
        return expert_shares[layer]

    def total_of(layer, name):
        parts = [saved[micro][layer][name] for micro in micros]
        return sum(parts[1:], parts[0])

    def packed_dense(layer):
        parts = [saved[micro][layer]["grads"] for micro in micros]
        sums = [sum(values[1:], values[0]) for values in zip(*parts)]
        shards = lax.axis_size("context") * lax.axis_size("dp")
        at = ROUTED + 8
        residual = jnp.pad(
            total_of(layer, "g_residual")[:ROUTED, :ROUTED],
            ((0, width // shards - ROUTED), (at, LANES - at - ROUTED)),
        )
        small = sums[-1] + jnp.tile(residual, (shards, 1))
        if layer == 0:
            gains = [total_of(l, "g_moe_gain") for l in range(layers)]
            gains += [total_of(l, "g_attn_gain") for l in range(layers)]
            blank = jnp.zeros((LANES - GAINS_LANE - len(gains), width), f32)
            above = jnp.zeros((GAINS_LANE, width), f32)
            small = small + jnp.concatenate([above, jnp.stack(gains), blank]).T
        return jnp.concatenate([total.astype(bf16) for total in sums[:-1] + [small]], axis=1)

    def reduce_dense(layer):
        packed = packed_dense(layer)
        shards = lax.axis_size("context") * lax.axis_size("dp")
        parts = packed.reshape(shards, width // shards, packed.shape[1])
        parts = lax.all_to_all(parts, SHARDED, split_axis=0, concat_axis=0, tiled=True)
        share = jnp.sum(parts.astype(f32), axis=0)
        span = 1
        while span < groups:
            sent = share.astype(bf16)
            route = [(i, i ^ span) for i in range(groups)]
            share = sent.astype(f32) + lax.ppermute(sent, "expert", route).astype(f32)
            span *= 2
        dense_shares[layer] = share
        return (share,)

    last = layers - 1
    d_rows = [None] * micro_count

    def send_back(layer, micro, after):
        grads[micro] = finish_back_part(layer, micro, after)
        sent = dispatch(
            grads[micro], slot_rows[micro], saved[micro][layer - 1]["gate_rows"], "scaled", slots,
            groups,
        )
        d_rows[micro] = exchange(sent, 1)
        return sent[-1]

    before = ()
    for layer in range(layers):
        for micro in micros:
            if layer > 0:
                before = (combine_part(layer - 1, micro, before),)
        for micro in micros:
            waits = tuple(early[micro][1:]) if layer == 0 else ()
            before = (attention_part(layer, micro, before, waits),)
        for micro in micros:
            before = (experts_part(layer, micro, before),)
    hidden_out = []

    grads = [out_grad[micro, 0] for micro in micros]
    d_priors = [None] * micro_count
    dense_wait = ()
    for layer in range(last, -1, -1):
        experts_ready = reduce_experts(layer)
        for micro in micros:
            if layer == last:
                hidden_out.append(combine_part(last, micro, before))
                before = (hidden_out[-1],)
            d_priors[micro] = token_back_part(layer, micro, grads[micro], d_priors[micro], before)
            before = (saved[micro][layer]["d_att"],)
            if micro > 0 and layer > 0:
                before = (send_back(layer, micro - 1, before),)
            if micro == micro_count - 1:
                before += dense_wait
            before = (attention_back_part(layer, micro, before),)
        if layer > 0:
            before = (send_back(layer, micro_count - 1, before),)
            dense_wait = reduce_dense(layer)
            for micro in micros:
                if micro < len(experts_ready):
                    before += (experts_ready[micro],)
                before = (experts_back_part(layer - 1, micro, d_rows[micro], before),)
        else:
            for micro in micros:
                grads[micro] = finish_back_part(layer, micro, tuple(experts_ready))
    reduce_dense(0)
    hidden_out = jnp.stack(hidden_out)[:, None]
    hidden_grad = jnp.stack(grads)[:, None]

    dense = jnp.stack(dense_shares)
    small = dense[:, :, 4 * width :]
    shard = small.shape[1]
    experts_total = [jnp.stack(parts).astype(f32) for parts in zip(*expert_shares)]
    per_dev = EXPERTS // groups
    return (
        hidden_out,
        hidden_grad,
        jnp.stack([small[0, :, GAINS_LANE + layers + l] for l in range(layers)]),
        dense[:, :, :width],
        dense[:, :, width : 2 * width],
        dense[:, :, 2 * width : 3 * width],
        dense[:, :, 3 * width : 4 * width],
        jnp.stack([small[0, :, GAINS_LANE + l] for l in range(layers)]),
        small[:, :, :ROUTED],
        small[:, :ROUTED, ROUTED + 8 : 2 * ROUTED + 8],
        jnp.transpose(
            small[:, :, ROUTED : ROUTED + 4].reshape(layers, shard, 2, 2), (0, 2, 1, 3)
        ),
        jnp.transpose(small[:, :, ROUTED + 4 : ROUTED + 6], (0, 2, 1)),
        experts_total[0][:, :per_dev],
        experts_total[0][:, per_dev:],
        experts_total[1],
    )

def solution(mesh):
    tokens = P(None, ("expert", "dp"), "context", None)
    rows = P(None, SHARDED, None)
    vector = P(None, SHARDED)
    experts = P(None, "expert", SHARDED, None)
    const = P(None, None, SHARDED, None)
    const_vector = P(None, None, SHARDED)
    return jax.shard_map(
        per_device,
        mesh=mesh,
        in_specs=(
            tokens, P(None, ("expert", "dp"), None), tokens, tokens, tokens, vector, rows, rows,
            rows, rows, vector, rows, P(), const, const_vector, experts, experts, experts,
        ),
        out_specs=(
            tokens, tokens, vector, rows, rows, rows, rows, vector, rows, P(), const,
            const_vector, experts, experts, experts,
        ),
        check_vma=False,
    )
```

```python
import functools

import jax
import jax.numpy as jnp
from jax import lax
from jax.experimental import pallas as pl
from jax.experimental.pallas import tpu as pltpu
from jax.sharding import PartitionSpec as P

HEADS = 12
HEAD_DIM = 64
EXPERTS = 8
TOP = 2
WINDOW = 1024
ROUTED = 12
LANES = 128
MIB = 1 << 20

norm_eps = 1e-05
masked = -1000000000.0
highest = lax.Precision.HIGHEST
f32 = jnp.float32
bf16 = jnp.bfloat16
SHARDED = ("context", "dp")


COST_SHARE = 0.8


def cost(microseconds):
    return pl.CostEstimate(
        flops=int(microseconds * COST_SHARE * 1.15e9), bytes_accessed=1, transcendentals=0
    )


ANY_SPEC = pl.BlockSpec(memory_space=pl.ANY)


def dot_on(left_op, right_op, left_dim, right_dim):
    return lax.dot_general(
        left_op,
        right_op,
        (((left_dim,), (right_dim,)), ((), ())),
        preferred_element_type=f32,
    )


def held(arrays, after):
    count = len(arrays)
    if not after:
        return list(arrays)
    return list(
        pl.pallas_call(
            lambda *refs: None,
            in_specs=[ANY_SPEC] * (count + len(after)),
            out_specs=[ANY_SPEC] * count,
            out_shape=[jax.ShapeDtypeStruct(array.shape, array.dtype) for array in arrays],
            input_output_aliases={index: index for index in range(count)},
            name="held",
        )(*arrays, *after)
    )


def rows_of(values, picks):
    count = 8 if len(picks) <= 8 else 16
    row = lax.broadcasted_iota(jnp.int32, (count, LANES), 0)
    lane = lax.broadcasted_iota(jnp.int32, (count, LANES), 1)
    pick = jnp.zeros((count, LANES), f32)
    for index, source in enumerate(picks):
        pick = jnp.where((row == index) & (lane == source), 1.0, pick)
    return lax.dot_general(
        pick, values, (((1,), (1,)), ((), ())), precision=highest, preferred_element_type=f32
    )


def join_spans(buffer_ref, earlier_ref, own_ref):
    buffer_ref[:WINDOW, :] = earlier_ref[...]
    buffer_ref[WINDOW:, :] = own_ref[...]


def attention_forward_kernel(
    rows, keys, blocks, q_ref, ko_ref, vo_ref, kp_ref, vp_ref, sq_ref, sk_ref, *rest
):
    out_ref, lse_rows_ref, lse_ref, bias_ref, k_ref, v_ref = rest[-6:]
    pair = pl.program_id(0)

    @pl.when(pair == 0)
    def _():
        lse_ref[...] = jnp.zeros_like(lse_ref)
        rel = lax.broadcasted_iota(jnp.int32, (rows, keys), 1) - lax.broadcasted_iota(
            jnp.int32, (rows, keys), 0
        )
        inside = (rel > 0) & (rel <= WINDOW)
        for block in range(blocks):
            first = block * rows
            same = sq_ref[first : first + rows, :] == sk_ref[:, first : first + keys]
            bias_ref[block] = jnp.where(inside & same, 0.0, masked)

    join_spans(k_ref, kp_ref, ko_ref)
    join_spans(v_ref, vp_ref, vo_ref)
    lane = lax.broadcasted_iota(jnp.int32, (rows, LANES), 1)
    low = lane < HEAD_DIM
    for block in range(blocks):
        own = slice(block * rows, (block + 1) * rows)
        span = slice(block * rows, block * rows + keys)
        query = q_ref[own, :] * (HEAD_DIM ** -0.5)
        key = k_ref[span, :]
        value = v_ref[span, :]
        heads_out = []
        for half in range(2):
            mine = low if half == 0 else ~low
            scores = (
                dot_on(jnp.where(mine, query, jnp.zeros_like(query)), key, 1, 1) + bias_ref[block]
            )
            row_max = jnp.max(scores, axis=1, keepdims=True)
            exponent = jnp.exp(scores - row_max)
            row_sum = jnp.sum(exponent, axis=1, keepdims=True)
            heads_out.append(dot_on(exponent.astype(bf16), value, 1, 0) * (1.0 / row_sum))
            lse_ref[own, :] = jnp.where(
                lane == 2 * pair + half, row_max + jnp.log(row_sum), lse_ref[own, :]
            )
        out_ref[own, :] = jnp.where(low, heads_out[0], heads_out[1]).astype(bf16)

    @pl.when(pair == pl.num_programs(0) - 1)
    def _():
        lse_rows_ref[...] = rows_of(lse_ref[...], range(HEADS))


def attention_forward(qkv, kv_earlier, seg_query, seg_key, after):
    length = qkv.shape[0]
    width = qkv.shape[1] // 3
    pairs = width // LANES
    rows = min(256, length)
    keys = rows + WINDOW
    blocks = length // rows
    span = WINDOW + length

    def column(count, offset):
        return pl.BlockSpec((count, LANES), lambda p: (0, offset + p))

    return pl.pallas_call(
        functools.partial(attention_forward_kernel, rows, keys, blocks),
        grid=(pairs,),
        in_specs=[
            column(length, 0),
            column(length, pairs),
            column(length, 2 * pairs),
            column(WINDOW, 0),
            column(WINDOW, pairs),
            pl.BlockSpec((length, 1), lambda p: (0, 0)),
            pl.BlockSpec((1, span), lambda p: (0, 0)),
        ]
        + [ANY_SPEC] * len(after),
        out_specs=[column(length, 0), pl.BlockSpec((16, length), lambda p: (0, 0))],
        out_shape=[
            jax.ShapeDtypeStruct((length, width), bf16),
            jax.ShapeDtypeStruct((16, length), f32),
        ],
        scratch_shapes=[
            pltpu.VMEM((length, LANES), f32),
            pltpu.VMEM((blocks, rows, keys), f32),
            pltpu.VMEM((span, LANES), bf16),
            pltpu.VMEM((span, LANES), bf16),
        ],
        compiler_params=pltpu.CompilerParams(vmem_limit_bytes=60 * MIB),
        cost_estimate=cost(32),
        name="attention_forward",
    )(qkv, qkv, qkv, kv_earlier, kv_earlier, seg_query, seg_key, *after)


def attention_backward_kernel(
    rows, keys, blocks, q_ref, ko_ref, vo_ref, kp_ref, vp_ref, do_ref, out_ref, lse_ref,
    sq_ref, sk_ref, *rest
):
    dq_ref, dk_ref, dv_ref, bias_ref, k_ref, v_ref, dk_sum, dv_sum = rest[-8:]
    pair = pl.program_id(0)

    @pl.when(pair == 0)
    def _():
        rel = lax.broadcasted_iota(jnp.int32, (keys, rows), 0) - lax.broadcasted_iota(
            jnp.int32, (keys, rows), 1
        )
        inside = (rel > 0) & (rel <= WINDOW)
        for block in range(blocks):
            first = block * rows
            same = sk_ref[first : first + keys, :] == sq_ref[:, first : first + rows]
            bias_ref[block] = jnp.where(inside & same, 0.0, masked)

    join_spans(k_ref, kp_ref, ko_ref)
    join_spans(v_ref, vp_ref, vo_ref)
    dk_sum[...] = jnp.zeros_like(dk_sum)
    dv_sum[...] = jnp.zeros_like(dv_sum)
    low = lax.broadcasted_iota(jnp.int32, (rows, LANES), 1) < HEAD_DIM
    ones = jnp.ones((8, LANES), bf16)
    for block in range(blocks):
        own = slice(block * rows, (block + 1) * rows)
        span = slice(block * rows, block * rows + keys)
        query = q_ref[own, :] * (HEAD_DIM ** -0.5)
        grad = do_ref[own, :]
        key = k_ref[span, :]
        value = v_ref[span, :]
        product = grad.astype(f32) * out_ref[own, :].astype(f32)
        heads_dq = []
        for half in range(2):
            mine = low if half == 0 else ~low
            query_h = jnp.where(mine, query, jnp.zeros_like(query))
            grad_h = jnp.where(mine, grad, jnp.zeros_like(grad))
            product_h = jnp.where(mine, product, 0.0)
            coarse = product_h.astype(bf16)
            fine = (product_h - coarse.astype(f32)).astype(bf16)
            delta = (dot_on(ones, coarse, 1, 1) + dot_on(ones, fine, 1, 1))[0:1, :]
            scores = dot_on(key, query_h, 1, 1) + bias_ref[block]
            probs = jnp.exp(scores - lse_ref[pl.ds(2 * pair + half, 1), own])
            d_probs = dot_on(value, grad_h, 1, 1)
            d_scores = (probs * (d_probs - delta)).astype(bf16)
            dv_sum[span, :] += dot_on(probs.astype(bf16), grad_h, 1, 0)
            dk_sum[span, :] += dot_on(d_scores, query_h, 1, 0)
            heads_dq.append(dot_on(d_scores, key, 0, 0))
        dq_ref[own, :] = (
            jnp.where(low, heads_dq[0], heads_dq[1]) * (HEAD_DIM ** -0.5)
        ).astype(bf16)
    dk_ref[...] = dk_sum[...].astype(bf16)
    dv_ref[...] = dv_sum[...].astype(bf16)


def attention_backward(qkv, kv_earlier, grad_att, attended, lse, seg_query, seg_key, after):
    length = qkv.shape[0]
    width = qkv.shape[1] // 3
    pairs = width // LANES
    rows = min(256, length)
    keys = rows + WINDOW
    blocks = length // rows
    span = WINDOW + length

    def column(count, offset):
        return pl.BlockSpec((count, LANES), lambda p: (0, offset + p))

    return pl.pallas_call(
        functools.partial(attention_backward_kernel, rows, keys, blocks),
        grid=(pairs,),
        in_specs=[
            column(length, 0),
            column(length, pairs),
            column(length, 2 * pairs),
            column(WINDOW, 0),
            column(WINDOW, pairs),
            column(length, 0),
            column(length, 0),
            pl.BlockSpec((16, length), lambda p: (0, 0)),
            pl.BlockSpec((1, length), lambda p: (0, 0)),
            pl.BlockSpec((span, 1), lambda p: (0, 0)),
        ]
        + [ANY_SPEC] * len(after),
        out_specs=[column(length, 0), column(span, 0), column(span, 0)],
        out_shape=[
            jax.ShapeDtypeStruct((length, width), bf16),
            jax.ShapeDtypeStruct((span, width), bf16),
            jax.ShapeDtypeStruct((span, width), bf16),
        ],
        scratch_shapes=[
            pltpu.VMEM((blocks, keys, rows), f32),
            pltpu.VMEM((span, LANES), bf16),
            pltpu.VMEM((span, LANES), bf16),
            pltpu.VMEM((span, LANES), f32),
            pltpu.VMEM((span, LANES), f32),
        ],
        compiler_params=pltpu.CompilerParams(vmem_limit_bytes=60 * MIB),
        cost_estimate=cost(48),
        name="attention_backward",
    )(
        qkv, qkv, qkv, kv_earlier, kv_earlier, grad_att, attended, lse, seg_query, seg_key, *after
    )


def sigmoid(values):
    return 1.0 / (1.0 + jnp.exp(-values))


def gathered(rows_ref, block_refs):
    count = block_refs[0].shape[0]
    width = rows_ref.shape[1]
    for index, block_ref in enumerate(block_refs):
        rows_ref[index * count : (index + 1) * count, :] = block_ref[:, :width]


def scattered(block_refs, rows, which=0):
    count = block_refs[0].shape[1]
    for index, block_ref in enumerate(block_refs):
        block_ref[which] = rows[index * count : (index + 1) * count, :].astype(bf16)


def experts_forward_kernel(groups, *refs):
    block_refs, (gate_w_ref, up_w_ref, down_w_ref) = refs[:groups], refs[groups : groups + 3]
    out_refs, (gate_ref, up_ref, rows_ref) = refs[-groups - 3 : -3], refs[-3:]
    gathered(rows_ref, block_refs)
    rows_in = rows_ref[...]
    gate_pre = dot_on(rows_in, gate_w_ref[0], 1, 0)
    up_pre = dot_on(rows_in, up_w_ref[0], 1, 0)
    activated = (gate_pre * sigmoid(gate_pre) * up_pre).astype(bf16)
    gate_ref[0] = gate_pre.astype(bf16)
    up_ref[0] = up_pre.astype(bf16)
    scattered(out_refs, dot_on(activated, down_w_ref[0], 1, 0))


def experts_forward(blocks, gate_up_w, down_w, after):
    groups = len(blocks)
    count = down_w.shape[0]
    width, hidden = gate_up_w.shape[1:]
    part = blocks[0].shape[0] // count
    rows = groups * part
    block_spec = pl.BlockSpec((part, width), lambda j: (j, 0))
    hidden_spec = pl.BlockSpec((1, rows, hidden), lambda j: (j, 0, 0))
    hidden_shape = jax.ShapeDtypeStruct((count, rows, hidden), bf16)
    *produced, gate_pre, up_pre = pl.pallas_call(
        functools.partial(experts_forward_kernel, groups),
        grid=(count,),
        in_specs=[block_spec] * groups
        + [
            pl.BlockSpec((1, width, hidden), lambda j: (j, 0, 0)),
            pl.BlockSpec((1, width, hidden), lambda j: (count + j, 0, 0)),
            pl.BlockSpec((1, hidden, width), lambda j: (j, 0, 0)),
        ]
        + [ANY_SPEC] * len(after),
        out_specs=[pl.BlockSpec((1, part, width), lambda j: (0, j, 0))] * groups
        + [hidden_spec, hidden_spec],
        out_shape=[jax.ShapeDtypeStruct((1, count * part, width), bf16)] * groups
        + [hidden_shape, hidden_shape],
        scratch_shapes=[pltpu.VMEM((rows, width), bf16)],
        compiler_params=pltpu.CompilerParams(vmem_limit_bytes=60 * MIB),
        cost_estimate=cost(26),
        name="experts_forward",
    )(*blocks, gate_up_w, gate_up_w, down_w, *after)
    return produced, gate_pre, up_pre


def experts_backward_kernel(groups, chunks, whole, has_sums, *refs):
    block_refs, d_refs, given = refs[:groups], refs[groups : 2 * groups], refs[2 * groups :]
    gate_w_ref, up_w_ref, down_w_ref = given[:3]
    if whole:
        share_refs, given = given[3 : 3 + groups], given[3 + groups :]
        *refs, produced_ref = refs
    else:
        (gate_ref, up_ref), given = given[3:5], given[5:]
    out_refs = refs[-5 - groups : -5]
    gate_up_grad_ref, down_grad_ref, total_ref, rows_ref, d_ref = refs[-5:]
    chunk = pl.program_id(1)

    @pl.when(chunk == 0)
    def _():
        gathered(rows_ref, block_refs)
        if whole:
            count = d_refs[0].shape[0]
            for index in range(groups):
                share = share_refs[index][...].astype(f32)
                share = share[:, 0:1] + share[:, 1:2]
                d_ref[index * count : (index + 1) * count, :] = (
                    d_refs[index][...].astype(f32) * share
                ).astype(bf16)
        else:
            gathered(d_ref, d_refs)

    rows_in = rows_ref[...]
    d_out = d_ref[...]
    if whole:
        gate_pre = dot_on(rows_in, gate_w_ref[0], 1, 0)
        up_pre = dot_on(rows_in, up_w_ref[0], 1, 0)
    else:
        gate_pre = gate_ref[0].astype(f32)
        up_pre = up_ref[0].astype(f32)
    share = sigmoid(gate_pre)
    swish = gate_pre * share
    activated = (swish * up_pre).astype(bf16)
    d_act = dot_on(d_out, down_w_ref[0], 1, 1)
    d_gate = (d_act * up_pre * (share * (1.0 + gate_pre * (1.0 - share)))).astype(bf16)
    d_up = (d_act * swish).astype(bf16)
    part = dot_on(d_gate, gate_w_ref[0], 1, 1) + dot_on(d_up, up_w_ref[0], 1, 1)
    gate_grad = dot_on(rows_in, d_gate, 0, 0)
    up_grad = dot_on(rows_in, d_up, 0, 0)
    down_grad = dot_on(activated, d_out, 0, 0)
    if has_sums:
        gate_up_sum_ref, down_sum_ref = given[:2]
        gate_grad += gate_up_sum_ref[0, 0].astype(f32)
        up_grad += gate_up_sum_ref[1, 0].astype(f32)
        down_grad += down_sum_ref[0].astype(f32)
    gate_up_grad_ref[0, 0] = gate_grad.astype(bf16)
    gate_up_grad_ref[1, 0] = up_grad.astype(bf16)
    down_grad_ref[0] = down_grad.astype(bf16)
    sums = [(total_ref, part)]
    if whole:
        sums.append((produced_ref, dot_on(activated, down_w_ref[0], 1, 0)))

    @pl.when(chunk == 0)
    def _():
        for sum_ref, value in sums:
            sum_ref[...] = value

    @pl.when(chunk > 0)
    def _():
        for sum_ref, value in sums:
            sum_ref[...] += value

    @pl.when(chunk == chunks - 1)
    def _():
        scattered(out_refs, total_ref[...], len(sums) - 1)
        if whole:
            scattered(out_refs, produced_ref[...])


def experts_backward(blocks, d_blocks, pre, gate_up_w, down_w, sums, after):
    groups = len(blocks)
    count, hidden, width = down_w.shape
    part = blocks[0].shape[0] // count
    rows = groups * part
    whole = pre is None
    chunk = min(512, hidden)
    chunks = hidden // chunk
    block_spec = pl.BlockSpec((part, width), lambda j, f: (j, 0))
    hidden_spec = pl.BlockSpec((1, rows, chunk), lambda j, f: (j, 0, f))
    wide_spec = pl.BlockSpec((1, width, chunk), lambda j, f: (j, 0, f))
    up_spec = pl.BlockSpec((1, width, chunk), lambda j, f: (count + j, 0, f))
    tall_spec = pl.BlockSpec((1, chunk, width), lambda j, f: (j, f, 0))
    both_spec = pl.BlockSpec((2, 1, width, chunk), lambda j, f: (0, j, 0, f))
    operands = [*blocks, *d_blocks, gate_up_w, gate_up_w, down_w]
    specs = [block_spec] * (2 * groups) + [wide_spec, up_spec, tall_spec]
    if whole:
        operands.extend(blocks)
        specs += [pl.BlockSpec((part, LANES), lambda j, f: (j, width // LANES))] * groups
    else:
        operands.extend(pre)
        specs += [hidden_spec, hidden_spec]
    if sums is not None:
        operands.extend(sums)
        specs.extend([both_spec, tall_spec])
    outs = 2 if whole else 1
    *out, gate_up_grad, down_grad = pl.pallas_call(
        functools.partial(experts_backward_kernel, groups, chunks, whole, sums is not None),
        grid=(count, chunks),
        in_specs=specs + [ANY_SPEC] * len(after),
        out_specs=[pl.BlockSpec((outs, part, width), lambda j, f: (0, j, 0))] * groups
        + [both_spec, tall_spec],
        out_shape=[jax.ShapeDtypeStruct((outs, count * part, width), bf16)] * groups
        + [
            jax.ShapeDtypeStruct((2, count, width, hidden), bf16),
            jax.ShapeDtypeStruct((count, hidden, width), bf16),
        ],
        scratch_shapes=[
            pltpu.VMEM((rows, width), f32),
            pltpu.VMEM((rows, width), bf16),
            pltpu.VMEM((rows, width), bf16),
        ]
        + ([pltpu.VMEM((rows, width), f32)] if whole else []),
        compiler_params=pltpu.CompilerParams(vmem_limit_bytes=60 * MIB),
        cost_estimate=cost(75 if whole else 52),
        name="experts_whole" if whole else "experts_backward",
    )(*operands, *after)
    return out, (gate_up_grad, down_grad)


def passed_along(block, axis, distance):
    devices = range(lax.axis_size(axis))
    route = [(i - distance, i) for i in devices if i - distance in devices]
    return lax.ppermute(block, axis, route)


def earlier_rows(block, hop_count):
    pieces = [passed_along(block, "context", hop) for hop in range(hop_count, 0, -1)]
    missing = WINDOW - hop_count * block.shape[-2]
    if missing > 0:
        shape = block.shape[:-2] + (missing, block.shape[-1])
        pieces = [jnp.zeros(shape, block.dtype)] + pieces
    rows = pieces[0] if len(pieces) == 1 else jnp.concatenate(pieces, axis=-2)
    return rows[..., rows.shape[-2] - WINDOW :, :]


def returned_rows(block, length, hop_count):
    total = None
    for hop in range(1, hop_count + 1):
        first = WINDOW - hop * length
        part = block[max(first, 0) : first + length]
        if first < 0:
            part = jnp.concatenate([jnp.zeros((-first, block.shape[1]), block.dtype), part])
        part = passed_along(part, "context", -hop).astype(f32)
        total = part if total is None else total + part
    return total


def exchange(blocks, direction):
    groups = lax.axis_size("expert")
    out = []
    for d, block in enumerate(blocks):
        step = d * direction
        route = [(i, (i + step) % groups) for i in range(groups)]
        out.append(block if d == 0 else lax.ppermute(block, "expert", route))
    return out


GATE, OF_NORMED, NORMED_SHARE, VECTOR_SHARE, MIX, SCALE, CHOSEN = 0, 2, 4, 5, 7, 9, 10
GAINS_LANE = 2 * ROUTED + 8
VECTOR_ROW, ATTN_GAIN_ROW, MOE_GAIN_ROW = 0, 2, 3


def inverse_rms(rows):
    return lax.rsqrt(jnp.mean(rows * rows, axis=-1, keepdims=True) + norm_eps)


def lane_iota(rows):
    return lax.broadcasted_iota(jnp.int32, (rows, LANES), 1)


def placed_on_lanes(rows, values):
    lane = lane_iota(rows)
    total = jnp.zeros((rows, LANES), f32)
    for index, value in values.items():
        total = jnp.where(lane == index, value, total)
    return total


def routing_kernel(routes_ref, base_ref, columns_ref, rows_ref):
    length = routes_ref.shape[1]
    lane = lane_iota(length)
    onehots = [(lane == routes_ref[0, :, k : k + 1]).astype(f32) for k in range(TOP)]
    counts = (onehots[0] + onehots[1]).astype(bf16)
    earlier = lax.broadcasted_iota(jnp.int32, (length, length), 0) > lax.broadcasted_iota(
        jnp.int32, (length, length), 1
    )
    rank = dot_on(jnp.where(earlier, 1.0, 0.0).astype(bf16), counts, 1, 0)
    place = base_ref[...] + jnp.where(lane < EXPERTS, rank, 0.0)
    slots = placed_on_lanes(
        length,
        {k: jnp.sum(onehots[k] * place, axis=1, keepdims=True) for k in range(TOP)},
    )
    columns_ref[0] = slots.astype(jnp.int32)
    rows_ref[0] = jnp.round(rows_of(slots, range(TOP))).astype(jnp.int32)


def routing_slots(routes, groups, capacity):
    count, length, _ = routes.shape
    per_dev = EXPERTS // groups
    expert = jnp.arange(LANES)
    place = (expert // per_dev - lax.axis_index("expert")) % groups
    base = (place * per_dev + expert % per_dev) * capacity
    base = jnp.where(expert < EXPERTS, base, -1).astype(f32)[None, :]
    return pl.pallas_call(
        routing_kernel,
        grid=(count,),
        in_specs=[
            pl.BlockSpec((1, length, TOP), lambda m: (m, 0, 0)),
            pl.BlockSpec((1, LANES), lambda m: (0, 0)),
        ],
        out_specs=[
            pl.BlockSpec((1, length, LANES), lambda m: (m, 0, 0)),
            pl.BlockSpec((1, 8, length), lambda m: (m, 0, 0)),
        ],
        out_shape=[
            jax.ShapeDtypeStruct((count, length, LANES), jnp.int32),
            jax.ShapeDtypeStruct((count, 8, length), jnp.int32),
        ],
        compiler_params=pltpu.CompilerParams(vmem_limit_bytes=60 * MIB),
        cost_estimate=cost(4),
        name="routing",
    )(routes, base)


def dispatch_kernel(mode, per_group, groups, rows_ref, slots_ref, gates_ref, *rest):
    out_refs = rest[-groups:]
    count, length = out_refs[0].shape[0], rows_ref.shape[0]
    width = rows_ref.shape[1]
    rows = rows_ref[...].astype(bf16)
    for group, out_ref in enumerate(out_refs):
        first = group * per_group + pl.program_id(0) * count
        slot = first + lax.broadcasted_iota(jnp.int32, (count, length), 0)
        hits = [slot == slots_ref[k : k + 1, :] for k in range(TOP)]
        table = jnp.where(hits[0] | hits[1], 1.0, 0.0).astype(bf16)
        found = dot_on(table, rows, 1, 0)
        if mode == "plain":
            out_ref[...] = found.astype(bf16)
            continue
        gate = jnp.sum(
            jnp.where(hits[0], gates_ref[0:1, :], 0.0)
            + jnp.where(hits[1], gates_ref[1:2, :], 0.0),
            axis=1,
            keepdims=True,
        )
        if mode == "scaled":
            out_ref[...] = (found * gate).astype(bf16)
            continue
        out_ref[:, :width] = found.astype(bf16)
        coarse = gate.astype(bf16).astype(f32)
        out_ref[:, width:] = placed_on_lanes(count, {0: coarse, 1: gate - coarse}).astype(bf16)


def dispatch(rows, slot_rows, gate_rows, mode, slots, groups, after=()):
    length, width = rows.shape
    per_group = slots // groups
    count = min(256, per_group)
    out_width = width + LANES if mode == "with gate" else width
    return pl.pallas_call(
        functools.partial(dispatch_kernel, mode, per_group, groups),
        grid=(per_group // count,),
        in_specs=[
            pl.BlockSpec((length, width), lambda s: (0, 0)),
            pl.BlockSpec((8, length), lambda s: (0, 0)),
            pl.BlockSpec((8, length), lambda s: (0, 0)),
        ]
        + [ANY_SPEC] * len(after),
        out_specs=[pl.BlockSpec((count, out_width), lambda s: (s, 0))] * groups,
        out_shape=[jax.ShapeDtypeStruct((per_group, out_width), bf16)] * groups,
        compiler_params=pltpu.CompilerParams(vmem_limit_bytes=60 * MIB),
        cost_estimate=cost(6),
        name="dispatch",
    )(rows, slot_rows, gate_rows, *after)


def attention_output_kernel(
    hidden_ref, attended_ref, out_w_ref, small_w_ref, vectors_ref, prior_ref, residual_ref,
    routes_ref, mid_ref, low_ref, logits_ref, scalars_ref, gates_ref,
):
    rows = hidden_ref.shape[0]
    mid = hidden_ref[...] + dot_on(attended_ref[...], out_w_ref[...], 1, 0)
    mid_ref[...] = mid
    scale = inverse_rms(mid)
    low = (mid * scale * vectors_ref[MOE_GAIN_ROW : MOE_GAIN_ROW + 1, :]).astype(bf16)
    low_ref[...] = low
    logits = dot_on(low, small_w_ref[...], 1, 0) + jnp.dot(
        prior_ref[...], residual_ref[...], precision=highest
    )
    logits_ref[...] = logits
    lane = lane_iota(rows)
    onehots = [lane == routes_ref[:, k : k + 1] for k in range(TOP)]

    def lane_sum(values):
        return jnp.sum(values, axis=1, keepdims=True)

    difference = lane_sum(jnp.where(onehots[0], logits, jnp.where(onehots[1], -logits, 0.0)))
    gates = (sigmoid(difference), sigmoid(-difference))
    chosen = [
        [jnp.where(routes_ref[:, k : k + 1] == EXPERTS + 2 + j, 1.0, 0.0) for j in range(2)]
        for k in range(TOP)
    ]
    alphas = []
    for j in range(2):
        at = ROUTED + 2 * j
        gap = lane_sum(jnp.where(lane == at, logits, jnp.where(lane == at + 1, -logits, 0.0)))
        alphas.append((sigmoid(gap), sigmoid(-gap)))
    of_normed = [
        jnp.where(routes_ref[:, k : k + 1] == EXPERTS + 1, 1.0, 0.0)
        + chosen[k][0] * alphas[0][0]
        + chosen[k][1] * alphas[1][0]
        for k in range(TOP)
    ]
    vector_gate = [gates[0] * chosen[0][j] + gates[1] * chosen[1][j] for j in range(2)]
    values = {
        GATE: gates[0], GATE + 1: gates[1],
        OF_NORMED: of_normed[0], OF_NORMED + 1: of_normed[1],
        NORMED_SHARE: gates[0] * of_normed[0] + gates[1] * of_normed[1],
        SCALE: scale,
    }
    for j in range(2):
        values[VECTOR_SHARE + j] = vector_gate[j] * alphas[j][1]
        values[MIX + j] = vector_gate[j] * alphas[j][0] * alphas[j][1]
        for k in range(TOP):
            values[CHOSEN + 2 * k + j] = chosen[k][j] * alphas[j][1]
    scalars = placed_on_lanes(rows, values)
    scalars_ref[...] = scalars
    gates_ref[...] = rows_of(scalars, (GATE, GATE + 1))


def attention_output(hidden, attended, weights, prior, routes):
    length, width = hidden.shape
    rows = min(256, length)
    wide = pl.BlockSpec((rows, width), lambda t: (t, 0))
    lanes = pl.BlockSpec((rows, LANES), lambda t: (t, 0))
    return pl.pallas_call(
        attention_output_kernel,
        grid=(length // rows,),
        in_specs=[
            wide,
            wide,
            pl.BlockSpec((width, width), lambda t: (0, 3)),
            pl.BlockSpec((width, LANES), lambda t: (0, 4 * width // LANES)),
            pl.BlockSpec((8, width), lambda t: (0, 0)),
            lanes,
            pl.BlockSpec((LANES, LANES), lambda t: (0, 0)),
            pl.BlockSpec((rows, TOP), lambda t: (t, 0)),
        ],
        out_specs=[wide, wide, lanes, lanes, pl.BlockSpec((8, rows), lambda t: (0, t))],
        out_shape=[
            jax.ShapeDtypeStruct((length, width), f32),
            jax.ShapeDtypeStruct((length, width), bf16),
            jax.ShapeDtypeStruct((length, LANES), f32),
            jax.ShapeDtypeStruct((length, LANES), f32),
            jax.ShapeDtypeStruct((8, length), f32),
        ],
        compiler_params=pltpu.CompilerParams(vmem_limit_bytes=60 * MIB),
        cost_estimate=cost(8),
        name="attention_output",
    )(
        hidden, attended, weights["dense"], weights["dense"], weights["vectors"], prior,
        weights["residual"], routes,
    )


def selected(columns, block_refs, which):
    per_group = block_refs[0].shape[0]
    total = None
    for group, block_ref in enumerate(block_refs):
        slot = group * per_group + lax.broadcasted_iota(
            jnp.int32, (columns.shape[0], per_group), 1
        )
        hit = slot == columns[:, which[0] : which[0] + 1]
        for k in which[1:]:
            hit = hit | (slot == columns[:, k : k + 1])
        part = dot_on(jnp.where(hit, 1.0, 0.0).astype(bf16), block_ref[...], 1, 0)
        total = part if total is None else total + part
    return total


def combine_kernel(last, groups, waits, *refs):
    back_refs, (columns_ref, mid_ref, scalars_ref, vectors_ref, next_ref) = (
        refs[:groups], refs[groups : groups + 5],
    )
    out_refs = refs[groups + 5 + waits :]
    columns, scalars = columns_ref[...], scalars_ref[...]
    mid = mid_ref[...]
    normed = mid * scalars[:, SCALE : SCALE + 1] * vectors_ref[MOE_GAIN_ROW : MOE_GAIN_ROW + 1, :]
    total = mid + scalars[:, NORMED_SHARE : NORMED_SHARE + 1] * normed
    for j in range(2):
        row = vectors_ref[VECTOR_ROW + j : VECTOR_ROW + j + 1, :]
        total += scalars[:, VECTOR_SHARE + j : VECTOR_SHARE + j + 1] * row
    for k in range(TOP):
        branch = selected(columns, back_refs, (k,))
        out_refs[k][...] = branch.astype(bf16)
        total += scalars[:, GATE + k : GATE + k + 1] * branch
    if last:
        out_refs[TOP][...] = total.astype(bf16)
    else:
        out_refs[TOP][...] = total
        out_refs[TOP + 1][...] = (
            total * inverse_rms(total) * next_ref[ATTN_GAIN_ROW : ATTN_GAIN_ROW + 1, :]
        ).astype(bf16)


def combine(back, columns, mid, scalars, vectors, next_vectors, after):
    last = next_vectors is None
    length, width = mid.shape
    back, which = back
    groups, per_group = len(back), back[0].shape[1]
    rows = min(256, length)
    wide = pl.BlockSpec((rows, width), lambda t: (t, 0))
    lanes = pl.BlockSpec((rows, LANES), lambda t: (t, 0))
    vector_spec = pl.BlockSpec((8, width), lambda t: (0, 0))
    low = jax.ShapeDtypeStruct((length, width), bf16)
    return pl.pallas_call(
        functools.partial(combine_kernel, last, groups, len(after)),
        grid=(length // rows,),
        in_specs=[pl.BlockSpec((None, per_group, width), lambda t: (which, 0, 0))] * groups
        + [lanes, wide, lanes, vector_spec, vector_spec]
        + [ANY_SPEC] * len(after),
        out_specs=[wide] * (TOP + 1 if last else TOP + 2),
        out_shape=[low, low, low]
        if last
        else [low, low, jax.ShapeDtypeStruct((length, width), f32), low],
        compiler_params=pltpu.CompilerParams(vmem_limit_bytes=60 * MIB),
        cost_estimate=cost(8),
        name="combine",
    )(*back, columns, mid, scalars, vectors, vectors if last else next_vectors, *after)


def token_backward_kernel(
    has_prior, groups, *refs
):
    back_refs, rest = refs[:groups], refs[groups:]
    (
        columns_ref, grad_ref, mid_ref, scalars_ref, branch0_ref, branch1_ref, low_ref, prior_ref,
        attended_ref, routes_ref, out_w_ref, small_w_ref, vectors_ref, residual_ref,
    ) = rest[:14]
    rest = rest[14:]
    d_mid_ref, d_att_ref, d_prior_ref, g_out_ref, g_small_ref, g_residual_ref, g_gain_ref = (
        rest[-7:]
    )
    step = pl.program_id(0)
    rows = mid_ref.shape[0]
    columns, scalars = columns_ref[...], scalars_ref[...]
    grad = grad_ref[...].astype(f32)
    mid = mid_ref[...]
    gain = vectors_ref[MOE_GAIN_ROW : MOE_GAIN_ROW + 1, :]
    scale = scalars[:, SCALE : SCALE + 1]
    unit = mid * scale
    lane = lane_iota(rows)

    def scalar(index):
        return scalars[:, index : index + 1]

    def row_sum(values):
        return jnp.sum(values, axis=1, keepdims=True)

    along = row_sum(grad * (unit * gain))
    along_vector = [
        row_sum(grad * vectors_ref[VECTOR_ROW + j : VECTOR_ROW + j + 1, :]) for j in range(2)
    ]
    d_gate = []
    for k, branch_ref in enumerate((branch0_ref, branch1_ref)):
        value = row_sum(grad * branch_ref[...].astype(f32)) + scalar(OF_NORMED + k) * along
        for j in range(2):
            value += scalar(CHOSEN + 2 * k + j) * along_vector[j]
        d_gate.append(value)
    d_choice = scalar(GATE) * scalar(GATE + 1) * (d_gate[0] - d_gate[1])
    d_small = jnp.where(
        lane == routes_ref[:, 0:1], d_choice, jnp.where(lane == routes_ref[:, 1:2], -d_choice, 0.0)
    )
    if has_prior:
        d_small += jnp.where(lane < ROUTED, rest[0][...], 0.0)
    d_logits = d_small
    for j in range(2):
        value = scalar(MIX + j) * (along - along_vector[j])
        at = ROUTED + 2 * j
        d_small = jnp.where(lane == at, value, jnp.where(lane == at + 1, -value, d_small))
    d_small_low = d_small.astype(bf16)
    d_prior_ref[...] = lax.dot_general(
        d_logits, residual_ref[...], (((1,), (1,)), ((), ())), precision=highest
    )
    vector_shares = placed_on_lanes(
        rows, {ROUTED + 4 + j: scalar(VECTOR_SHARE + j) for j in range(2)}
    ).astype(bf16)
    g_small = dot_on(low_ref[...], d_small_low, 0, 0) + dot_on(
        grad.astype(bf16), vector_shares, 0, 0
    )
    g_residual = lax.dot_general(
        prior_ref[...], d_logits, (((0,), (0,)), ((), ())), precision=highest
    )
    d_normed = (
        selected(columns, back_refs, (0, 1))
        + scalar(NORMED_SHARE) * grad
        + dot_on(d_small_low, small_w_ref[...], 1, 1)
    )
    g_gain = jnp.sum(d_normed * unit, axis=0, keepdims=True)
    d_unit = d_normed * gain
    d_mid = grad + (d_unit - unit * jnp.mean(d_unit * unit, axis=-1, keepdims=True)) * scale
    d_mid_ref[...] = d_mid
    d_mid_low = d_mid.astype(bf16)
    d_att_ref[...] = dot_on(d_mid_low, out_w_ref[...], 1, 1).astype(bf16)
    g_out = dot_on(attended_ref[...], d_mid_low, 0, 0)

    @pl.when(step == 0)
    def _():
        g_out_ref[...] = g_out
        g_small_ref[...] = g_small
        g_residual_ref[...] = g_residual
        g_gain_ref[...] = jnp.broadcast_to(g_gain, g_gain_ref.shape)

    @pl.when(step > 0)
    def _():
        g_out_ref[...] += g_out
        g_small_ref[...] += g_small
        g_residual_ref[...] += g_residual
        g_gain_ref[...] += jnp.broadcast_to(g_gain, g_gain_ref.shape)


def token_backward(back, kept, grad, weights, columns, routes, d_prior, after):
    length, width = grad.shape
    back, which = back
    groups, per_group = len(back), back[0].shape[1]
    rows = min(256, length)
    wide = pl.BlockSpec((rows, width), lambda t: (t, 0))
    lanes = pl.BlockSpec((rows, LANES), lambda t: (t, 0))

    def fixed(*shape, at=0):
        return pl.BlockSpec(shape, lambda t: (0, at))

    operands = [
        *back, columns, grad, kept["mid"], kept["scalars"], kept["branch"][0], kept["branch"][1],
        kept["low"], kept["prior"], kept["attended"], routes, weights["dense"], weights["dense"],
        weights["vectors"], weights["residual"],
    ]
    specs = [
        *[pl.BlockSpec((None, per_group, width), lambda t: (which, 0, 0))] * groups,
        lanes, wide, wide, lanes, wide, wide, wide, lanes, wide,
        pl.BlockSpec((rows, TOP), lambda t: (t, 0)), fixed(width, width, at=3),
        fixed(width, LANES, at=4 * width // LANES), fixed(8, width), fixed(LANES, LANES),
    ]
    if d_prior is not None:
        operands.append(d_prior)
        specs.append(lanes)
    return pl.pallas_call(
        functools.partial(token_backward_kernel, d_prior is not None, groups),
        grid=(length // rows,),
        in_specs=specs + [ANY_SPEC] * len(after),
        out_specs=[
            wide, wide, lanes, fixed(width, width), fixed(width, LANES), fixed(LANES, LANES),
            fixed(8, width),
        ],
        out_shape=[
            jax.ShapeDtypeStruct((length, width), f32),
            jax.ShapeDtypeStruct((length, width), bf16),
            jax.ShapeDtypeStruct((length, LANES), f32),
            jax.ShapeDtypeStruct((width, width), f32),
            jax.ShapeDtypeStruct((width, LANES), f32),
            jax.ShapeDtypeStruct((LANES, LANES), f32),
            jax.ShapeDtypeStruct((8, width), f32),
        ],
        compiler_params=pltpu.CompilerParams(vmem_limit_bytes=60 * MIB),
        cost_estimate=cost(25),
        name="token_backward",
    )(*operands, *after)


def finish_backward_kernel(
    has_later, hidden_ref, d_mid_ref, d_attn_ref, vectors_ref, *rest
):
    out_ref, g_gain_ref = rest[-2:]
    hidden = hidden_ref[...]
    d_attn = d_attn_ref[...]
    if has_later:
        d_attn += rest[0][...].astype(f32)
    scale = inverse_rms(hidden)
    unit = hidden * scale
    g_gain = jnp.broadcast_to(jnp.sum(d_attn * unit, axis=0, keepdims=True), g_gain_ref.shape)
    d_unit = d_attn * vectors_ref[ATTN_GAIN_ROW : ATTN_GAIN_ROW + 1, :]
    out_ref[...] = (
        d_mid_ref[...] + (d_unit - unit * jnp.mean(d_unit * unit, axis=-1, keepdims=True)) * scale
    ).astype(out_ref.dtype)

    @pl.when(pl.program_id(0) == 0)
    def _():
        g_gain_ref[...] = g_gain

    @pl.when(pl.program_id(0) > 0)
    def _():
        g_gain_ref[...] += g_gain


def finish_backward(hidden, d_mid, d_attn, vectors, later, out_type, after):
    length, width = hidden.shape
    rows = min(256, length)
    wide = pl.BlockSpec((rows, width), lambda t: (t, 0))
    vector_spec = pl.BlockSpec((8, width), lambda t: (0, 0))
    extra = [] if later is None else [later]
    return pl.pallas_call(
        functools.partial(finish_backward_kernel, later is not None),
        grid=(length // rows,),
        in_specs=[wide, wide, wide, vector_spec] + [wide] * len(extra) + [ANY_SPEC] * len(after),
        out_specs=[wide, vector_spec],
        out_shape=[
            jax.ShapeDtypeStruct((length, width), out_type),
            jax.ShapeDtypeStruct((8, width), f32),
        ],
        compiler_params=pltpu.CompilerParams(vmem_limit_bytes=60 * MIB),
        cost_estimate=cost(6),
        name="finish_backward",
    )(hidden, d_mid, d_attn, vectors, *extra, *after)


def fetch_layer(layer, local, first_arrived):
    width = local["w_query"].shape[2]
    shard = local["w_query"].shape[1]
    const_w = jnp.transpose(local["w_const"][layer], (1, 0, 2)).reshape(shard, 4)
    small = jnp.concatenate(
        [
            local["w_router"][layer], const_w, local["const_vec"][layer].T,
            local["norm_attn"][layer][:, None], local["norm_moe"][layer][:, None],
            jnp.zeros((shard, LANES - ROUTED - 8), bf16),
        ],
        axis=1,
    )
    packed = jnp.concatenate(
        [local["w_query"][layer], local["w_key"][layer], local["w_value"][layer],
         local["w_out"][layer], small],
        axis=1,
    )
    dense = lax.all_gather(packed, SHARDED, axis=0, tiled=True)
    gate_up = jnp.concatenate([local["w_gate"][layer], local["w_up"][layer]], axis=0)
    if layer == 0:
        (gate_up,) = held([gate_up], first_arrived)
    gate_up = lax.all_gather(gate_up, SHARDED, axis=1, tiled=True)
    down = lax.all_gather(local["w_down"][layer], SHARDED, axis=1, tiled=True)
    at = 4 * width + ROUTED + 4
    vectors = dense[:, at : at + 8].T.astype(f32)
    residual = local["w_res"][layer].astype(f32)
    blank = LANES - ROUTED
    return dict(
        dense=dense, vectors=vectors, gate_up=gate_up, down=down,
        residual=jnp.pad(residual, ((0, blank), (0, blank))),
    )


def per_device(
    hidden_in, segments, routes, prev_logits, out_grad, norm_attn, w_query, w_key, w_value,
    w_out, norm_moe, w_router, w_res, w_const, const_vec, w_gate, w_up, w_down,
):
    local = dict(
        norm_attn=norm_attn, w_query=w_query, w_key=w_key, w_value=w_value, w_out=w_out,
        norm_moe=norm_moe, w_router=w_router, w_res=w_res, w_const=w_const,
        const_vec=const_vec, w_gate=w_gate, w_up=w_up, w_down=w_down,
    )
    micro_count, _, length, width = hidden_in.shape
    micros = range(micro_count)
    layers = norm_attn.shape[0]
    groups = lax.axis_size("expert")
    hop_count = min((WINDOW + length - 2) // length, lax.axis_size("context") - 1)
    capacity = length // 4
    slots = EXPERTS * capacity
    block_start = lax.axis_index("context") * length
    hidden_earlier = []
    for micro in micros:
        block = hidden_in[micro, 0]
        if micro > 0 and hop_count > 0:
            (block,) = held([block], (hidden_earlier[-1],))
        hidden_earlier.append(earlier_rows(block, hop_count))
    routes = routes[:, 0]
    columns, slot_rows = routing_slots(routes, groups, capacity)
    blank_gates = jnp.zeros((8, length), f32)

    def normed(hidden, gain):
        return (hidden * inverse_rms(hidden) * gain).astype(bf16)

    last_arrived = []

    def in_turn(blocks, micro):
        others = held(list(blocks[1:]), tuple(last_arrived[1:]) if micro > 0 else ())
        last_arrived[:] = exchange(list(blocks[:1]) + others, -1)
        return list(last_arrived)

    early, sents = [], []
    for micro in micros:
        sent = dispatch(
            out_grad[micro, 0], slot_rows[micro], blank_gates, "plain", slots, groups,
        )
        sents.append(sent[-1])
        early.append(exchange(sent, 1))
    first_ready = (hidden_earlier[0], *sents)
    fetched = [fetch_layer(layer, local, first_ready) for layer in range(layers)]
    segs, state = [], []
    for micro in micros:
        whole = segments[micro, 0]
        padded = jnp.concatenate([jnp.full((WINDOW,), -1, jnp.int32), whole])
        query = lax.dynamic_slice_in_dim(whole, block_start, length, 0)
        key = lax.dynamic_slice_in_dim(padded, block_start, WINDOW + length, 0)
        segs.append((query, key))
        hidden = hidden_in[micro, 0].astype(f32)
        gain = fetched[0]["vectors"][ATTN_GAIN_ROW : ATTN_GAIN_ROW + 1]
        prior = jnp.pad(prev_logits[micro, 0], ((0, 0), (0, LANES - ROUTED)))
        state.append(
            (
                hidden, normed(hidden, gain),
                hidden_earlier[micro], prior,
            )
        )

    saved = [[None] * layers for _ in micros]
    expert_sums = [None] * layers

    def attention_part(layer, micro, after, after_output):
        weights = fetched[layer]
        hidden, attn_in, attn_earlier, prior = state[micro]
        if layer == 0:
            (attn_earlier,) = held([attn_earlier], after)
            attn_earlier = normed(attn_earlier.astype(f32), weights["vectors"][ATTN_GAIN_ROW][None])
        qkv = dot_on(attn_in, weights["dense"][:, : 3 * width], 1, 0).astype(bf16)
        kv_earlier = dot_on(attn_earlier, weights["dense"][:, width : 3 * width], 1, 0).astype(bf16)
        query, key = segs[micro]
        attended, lse = attention_forward(qkv, kv_earlier, query[:, None], key[None, :], after)
        mid, low, logits, scalars, gate_rows = attention_output(
            hidden, attended, weights, prior, routes[micro]
        )
        mode = "with gate" if layer == layers - 1 else "plain"
        sent = dispatch(low, slot_rows[micro], gate_rows, mode, slots, groups, after_output)
        saved[micro][layer] = dict(
            hidden=hidden, attn_in=attn_in, attn_earlier=attn_earlier, prior=prior, qkv=qkv,
            kv_earlier=kv_earlier, attended=attended, lse=lse, mid=mid, low=low,
            scalars=scalars, gate_rows=gate_rows, logits=logits, arrived=exchange(sent, 1),
        )
        return sent[-1]

    def experts_part(layer, micro, after):
        kept = saved[micro][layer]
        gate_up_w, down_w = fetched[layer]["gate_up"], fetched[layer]["down"]
        if layer == layers - 1:
            out, expert_sums[layer] = experts_backward(
                kept["arrived"], early[micro], None, gate_up_w, down_w, expert_sums[layer], after
            )
            arrived = in_turn(out, 0)
            kept["returned"], kept["back"] = (arrived, 0), (arrived, 1)
        else:
            out, *kept["pre"] = experts_forward(kept["arrived"], gate_up_w, down_w, after)
            kept["returned"] = (in_turn(out, 0), 0)
        return out[-1]

    def combine_part(layer, micro, after):
        kept = saved[micro][layer]
        last = layer == layers - 1
        outs = combine(
            kept["returned"], columns[micro], kept["mid"], kept["scalars"],
            fetched[layer]["vectors"], None if last else fetched[layer + 1]["vectors"], after,
        )
        kept["branch"] = outs[:TOP]
        if last:
            return outs[TOP]
        state[micro] = (
            outs[TOP], outs[TOP + 1], earlier_rows(outs[TOP + 1], hop_count), kept["logits"],
        )
        return outs[TOP]

    def experts_back_part(layer, micro, d_rows, after):
        kept = saved[micro][layer]
        dx, expert_sums[layer] = experts_backward(
            kept["arrived"], d_rows, kept["pre"], fetched[layer]["gate_up"],
            fetched[layer]["down"], expert_sums[layer], after,
        )
        kept["back"] = (in_turn(dx, 0), 0)
        return dx[-1]

    def token_back_part(layer, micro, grad, d_prior, after):
        kept = saved[micro][layer]
        (
            kept["d_mid"], kept["d_att"], d_prior, kept["g_out"], kept["g_small"],
            kept["g_residual"], g_moe_gain,
        ) = token_backward(
            kept["back"], kept, grad, fetched[layer], columns[micro], routes[micro], d_prior, after
        )
        kept["g_moe_gain"] = g_moe_gain[0]
        return d_prior

    def attention_back_part(layer, micro, after):
        kept, dense = saved[micro][layer], fetched[layer]["dense"]
        query, key = segs[micro]
        dq, dk, dv = attention_backward(
            kept["qkv"], kept["kv_earlier"], kept["d_att"], kept["attended"], kept["lse"],
            query[None, :], key[:, None], after,
        )
        query_w, key_w, value_w = (dense[:, i * width : (i + 1) * width] for i in range(3))
        kept["later"] = None
        if hop_count > 0:
            d_earlier = (
                dot_on(dk[:WINDOW], key_w, 1, 1) + dot_on(dv[:WINDOW], value_w, 1, 1)
            ).astype(bf16)
            kept["later"] = returned_rows(d_earlier, length, hop_count)
        kept["d_attn"] = (
            dot_on(dq, query_w, 1, 1)
            + dot_on(dk[WINDOW:], key_w, 1, 1)
            + dot_on(dv[WINDOW:], value_w, 1, 1)
        )
        kept["grads"] = [
            dot_on(kept["attn_in"], dq, 0, 0),
            dot_on(kept["attn_in"], dk[WINDOW:], 0, 0)
            + dot_on(kept["attn_earlier"], dk[:WINDOW], 0, 0),
            dot_on(kept["attn_in"], dv[WINDOW:], 0, 0)
            + dot_on(kept["attn_earlier"], dv[:WINDOW], 0, 0),
            kept["g_out"],
            kept["g_small"],
        ]
        return dq

    def finish_back_part(layer, micro, after):
        kept = saved[micro][layer]
        d_hidden, g_attn_gain = finish_backward(
            kept["hidden"], kept["d_mid"], kept["d_attn"], fetched[layer]["vectors"],
            kept["later"], f32 if layer > 0 else bf16, after,
        )
        kept["g_attn_gain"] = g_attn_gain[0]
        return d_hidden

    expert_shares, dense_shares = [None] * layers, [None] * layers

    def reduce_experts(layer):
        gate_up, down = held(expert_sums[layer], saved[0][layer]["back"][0][1:])
        gate_up = gate_up.reshape((-1,) + gate_up.shape[2:])
        expert_shares[layer] = (
            lax.psum_scatter(gate_up, SHARDED, scatter_dimension=1, tiled=True),
            lax.psum_scatter(down, SHARDED, scatter_dimension=1, tiled=True),
        )
        return expert_shares[layer]

    def total_of(layer, name):
        parts = [saved[micro][layer][name] for micro in micros]
        return sum(parts[1:], parts[0])

    def packed_dense(layer):
        parts = [saved[micro][layer]["grads"] for micro in micros]
        sums = [sum(values[1:], values[0]) for values in zip(*parts)]
        shards = lax.axis_size("context") * lax.axis_size("dp")
        at = ROUTED + 8
        residual = jnp.pad(
            total_of(layer, "g_residual")[:ROUTED, :ROUTED],
            ((0, width // shards - ROUTED), (at, LANES - at - ROUTED)),
        )
        small = sums[-1] + jnp.tile(residual, (shards, 1))
        if layer == 0:
            gains = [total_of(l, "g_moe_gain") for l in range(layers)]
            gains += [total_of(l, "g_attn_gain") for l in range(layers)]
            blank = jnp.zeros((LANES - GAINS_LANE - len(gains), width), f32)
            above = jnp.zeros((GAINS_LANE, width), f32)
            small = small + jnp.concatenate([above, jnp.stack(gains), blank]).T
        return jnp.concatenate([total.astype(bf16) for total in sums[:-1] + [small]], axis=1)

    def reduce_dense(layer, packed):
        shards = lax.axis_size("context") * lax.axis_size("dp")
        parts = packed.reshape(shards, width // shards, packed.shape[1])
        parts = lax.all_to_all(parts, SHARDED, split_axis=0, concat_axis=0, tiled=True)
        share = jnp.sum(parts.astype(f32), axis=0)
        if layer > 0:
            share = lax.psum(share.astype(bf16), "expert").astype(f32)
        else:
            span = 1
            while span < groups:
                sent = share.astype(bf16)
                route = [(i, i ^ span) for i in range(groups)]
                share = sent.astype(f32) + lax.ppermute(sent, "expert", route).astype(f32)
                span *= 2
        dense_shares[layer] = share
        return (share,)

    last = layers - 1
    d_rows = [None] * micro_count

    def send_back(layer, micro, after):
        grads[micro] = finish_back_part(layer, micro, after)
        sent = dispatch(
            grads[micro], slot_rows[micro], saved[micro][layer - 1]["gate_rows"], "scaled", slots,
            groups,
        )
        d_rows[micro] = exchange(sent, 1)
        return sent[-1]

    before = ()
    for layer in range(layers):
        for micro in micros:
            if layer > 0:
                before = (combine_part(layer - 1, micro, before),)
        for micro in micros:
            waits = tuple(early[micro][1:]) if layer == 0 else ()
            before = (attention_part(layer, micro, before, waits),)
        for micro in micros:
            before = (experts_part(layer, micro, before),)
    hidden_out = []

    grads = [out_grad[micro, 0] for micro in micros]
    d_priors = [None] * micro_count
    dense_wait = ()
    for layer in range(last, -1, -1):
        experts_ready = reduce_experts(layer)
        for micro in micros:
            if layer == last:
                hidden_out.append(combine_part(last, micro, before))
                before = (hidden_out[-1],)
            d_priors[micro] = token_back_part(layer, micro, grads[micro], d_priors[micro], before)
            before = (saved[micro][layer]["d_att"],)
            before = (attention_back_part(layer, micro, before),)
            if layer > 0:
                before = (send_back(layer, micro, before),)
        if layer > 0:
            dense_wait = reduce_dense(layer, packed_dense(layer))
            for micro in micros:
                if micro < len(experts_ready):
                    before += (experts_ready[micro],)
                before = (experts_back_part(layer - 1, micro, d_rows[micro], before),)
        else:
            for micro in micros:
                grads[micro] = finish_back_part(layer, micro, tuple(experts_ready) + dense_wait)
    reduce_dense(0, packed_dense(0))
    hidden_out = jnp.stack(hidden_out)[:, None]
    hidden_grad = jnp.stack(grads)[:, None]

    dense = jnp.stack(dense_shares)
    small = dense[:, :, 4 * width :]
    shard = small.shape[1]
    experts_total = [jnp.stack(parts).astype(f32) for parts in zip(*expert_shares)]
    per_dev = EXPERTS // groups
    return (
        hidden_out,
        hidden_grad,
        jnp.stack([small[0, :, GAINS_LANE + layers + l] for l in range(layers)]),
        dense[:, :, :width],
        dense[:, :, width : 2 * width],
        dense[:, :, 2 * width : 3 * width],
        dense[:, :, 3 * width : 4 * width],
        jnp.stack([small[0, :, GAINS_LANE + l] for l in range(layers)]),
        small[:, :, :ROUTED],
        small[:, :ROUTED, ROUTED + 8 : 2 * ROUTED + 8],
        jnp.transpose(
            small[:, :, ROUTED : ROUTED + 4].reshape(layers, shard, 2, 2), (0, 2, 1, 3)
        ),
        jnp.transpose(small[:, :, ROUTED + 4 : ROUTED + 6], (0, 2, 1)),
        experts_total[0][:, :per_dev],
        experts_total[0][:, per_dev:],
        experts_total[1],
    )

def solution(mesh):
    tokens = P(None, ("expert", "dp"), "context", None)
    rows = P(None, SHARDED, None)
    vector = P(None, SHARDED)
    experts = P(None, "expert", SHARDED, None)
    const = P(None, None, SHARDED, None)
    const_vector = P(None, None, SHARDED)
    return jax.shard_map(
        per_device,
        mesh=mesh,
        in_specs=(
            tokens, P(None, ("expert", "dp"), None), tokens, tokens, tokens, vector, rows, rows,
            rows, rows, vector, rows, P(), const, const_vector, experts, experts, experts,
        ),
        out_specs=(
            tokens, tokens, vector, rows, rows, rows, rows, vector, rows, P(), const,
            const_vector, experts, experts, experts,
        ),
        check_vma=False,
    )
```

```python
import functools

import jax
import jax.numpy as jnp
from jax import lax
from jax.experimental import pallas as pl
from jax.experimental.pallas import tpu as pltpu
from jax.sharding import PartitionSpec as P

HEADS = 12
HEAD_DIM = 64
EXPERTS = 8
TOP = 2
WINDOW = 1024
ROUTED = 12
LANES = 128
MIB = 1 << 20

norm_eps = 1e-05
masked = -1000000000.0
highest = lax.Precision.HIGHEST
f32 = jnp.float32
bf16 = jnp.bfloat16
SHARDED = ("context", "dp")


COST_SHARE = 0.3


def cost(microseconds):
    return pl.CostEstimate(
        flops=int(microseconds * COST_SHARE * 1.15e9), bytes_accessed=1, transcendentals=0
    )


ANY_SPEC = pl.BlockSpec(memory_space=pl.ANY)


def dot_on(left_op, right_op, left_dim, right_dim):
    return lax.dot_general(
        left_op,
        right_op,
        (((left_dim,), (right_dim,)), ((), ())),
        preferred_element_type=f32,
    )


def held(arrays, after):
    count = len(arrays)
    if not after:
        return list(arrays)
    return list(
        pl.pallas_call(
            lambda *refs: None,
            in_specs=[ANY_SPEC] * (count + len(after)),
            out_specs=[ANY_SPEC] * count,
            out_shape=[jax.ShapeDtypeStruct(array.shape, array.dtype) for array in arrays],
            input_output_aliases={index: index for index in range(count)},
            name="held",
        )(*arrays, *after)
    )


def rows_of(values, picks):
    count = 8 if len(picks) <= 8 else 16
    row = lax.broadcasted_iota(jnp.int32, (count, LANES), 0)
    lane = lax.broadcasted_iota(jnp.int32, (count, LANES), 1)
    pick = jnp.zeros((count, LANES), f32)
    for index, source in enumerate(picks):
        pick = jnp.where((row == index) & (lane == source), 1.0, pick)
    return lax.dot_general(
        pick, values, (((1,), (1,)), ((), ())), precision=highest, preferred_element_type=f32
    )


def join_spans(buffer_ref, earlier_ref, own_ref):
    buffer_ref[:WINDOW, :] = earlier_ref[...]
    buffer_ref[WINDOW:, :] = own_ref[...]


def attention_forward_kernel(
    rows, keys, blocks, q_ref, ko_ref, vo_ref, kp_ref, vp_ref, sq_ref, sk_ref, *rest
):
    out_ref, lse_rows_ref, lse_ref, bias_ref, k_ref, v_ref = rest[-6:]
    pair = pl.program_id(0)

    @pl.when(pair == 0)
    def _():
        lse_ref[...] = jnp.zeros_like(lse_ref)
        rel = lax.broadcasted_iota(jnp.int32, (rows, keys), 1) - lax.broadcasted_iota(
            jnp.int32, (rows, keys), 0
        )
        inside = (rel > 0) & (rel <= WINDOW)
        for block in range(blocks):
            first = block * rows
            same = sq_ref[first : first + rows, :] == sk_ref[:, first : first + keys]
            bias_ref[block] = jnp.where(inside & same, 0.0, masked)

    join_spans(k_ref, kp_ref, ko_ref)
    join_spans(v_ref, vp_ref, vo_ref)
    lane = lax.broadcasted_iota(jnp.int32, (rows, LANES), 1)
    low = lane < HEAD_DIM
    for block in range(blocks):
        own = slice(block * rows, (block + 1) * rows)
        span = slice(block * rows, block * rows + keys)
        query = q_ref[own, :] * (HEAD_DIM ** -0.5)
        key = k_ref[span, :]
        value = v_ref[span, :]
        heads_out = []
        for half in range(2):
            mine = low if half == 0 else ~low
            scores = (
                dot_on(jnp.where(mine, query, jnp.zeros_like(query)), key, 1, 1) + bias_ref[block]
            )
            row_max = jnp.max(scores, axis=1, keepdims=True)
            exponent = jnp.exp(scores - row_max)
            row_sum = jnp.sum(exponent, axis=1, keepdims=True)
            heads_out.append(dot_on(exponent.astype(bf16), value, 1, 0) * (1.0 / row_sum))
            lse_ref[own, :] = jnp.where(
                lane == 2 * pair + half, row_max + jnp.log(row_sum), lse_ref[own, :]
            )
        out_ref[own, :] = jnp.where(low, heads_out[0], heads_out[1]).astype(bf16)

    @pl.when(pair == pl.num_programs(0) - 1)
    def _():
        lse_rows_ref[...] = rows_of(lse_ref[...], range(HEADS))


def attention_forward(qkv, kv_earlier, seg_query, seg_key, after):
    length = qkv.shape[0]
    width = qkv.shape[1] // 3
    pairs = width // LANES
    rows = min(256, length)
    keys = rows + WINDOW
    blocks = length // rows
    span = WINDOW + length

    def column(count, offset):
        return pl.BlockSpec((count, LANES), lambda p: (0, offset + p))

    return pl.pallas_call(
        functools.partial(attention_forward_kernel, rows, keys, blocks),
        grid=(pairs,),
        in_specs=[
            column(length, 0),
            column(length, pairs),
            column(length, 2 * pairs),
            column(WINDOW, 0),
            column(WINDOW, pairs),
            pl.BlockSpec((length, 1), lambda p: (0, 0)),
            pl.BlockSpec((1, span), lambda p: (0, 0)),
        ]
        + [ANY_SPEC] * len(after),
        out_specs=[column(length, 0), pl.BlockSpec((16, length), lambda p: (0, 0))],
        out_shape=[
            jax.ShapeDtypeStruct((length, width), bf16),
            jax.ShapeDtypeStruct((16, length), f32),
        ],
        scratch_shapes=[
            pltpu.VMEM((length, LANES), f32),
            pltpu.VMEM((blocks, rows, keys), f32),
            pltpu.VMEM((span, LANES), bf16),
            pltpu.VMEM((span, LANES), bf16),
        ],
        compiler_params=pltpu.CompilerParams(vmem_limit_bytes=40 * MIB),
        cost_estimate=cost(32),
        name="attention_forward",
    )(qkv, qkv, qkv, kv_earlier, kv_earlier, seg_query, seg_key, *after)


def attention_backward_kernel(
    rows, keys, blocks, q_ref, ko_ref, vo_ref, kp_ref, vp_ref, do_ref, out_ref, lse_ref,
    sq_ref, sk_ref, *rest
):
    dq_ref, dk_ref, dv_ref, bias_ref, k_ref, v_ref, dk_sum, dv_sum = rest[-8:]
    pair = pl.program_id(0)

    @pl.when(pair == 0)
    def _():
        rel = lax.broadcasted_iota(jnp.int32, (keys, rows), 0) - lax.broadcasted_iota(
            jnp.int32, (keys, rows), 1
        )
        inside = (rel > 0) & (rel <= WINDOW)
        for block in range(blocks):
            first = block * rows
            same = sk_ref[first : first + keys, :] == sq_ref[:, first : first + rows]
            bias_ref[block] = jnp.where(inside & same, 0.0, masked)

    join_spans(k_ref, kp_ref, ko_ref)
    join_spans(v_ref, vp_ref, vo_ref)
    dk_sum[...] = jnp.zeros_like(dk_sum)
    dv_sum[...] = jnp.zeros_like(dv_sum)
    low = lax.broadcasted_iota(jnp.int32, (rows, LANES), 1) < HEAD_DIM
    ones = jnp.ones((8, LANES), bf16)
    for block in range(blocks):
        own = slice(block * rows, (block + 1) * rows)
        span = slice(block * rows, block * rows + keys)
        query = q_ref[own, :] * (HEAD_DIM ** -0.5)
        grad = do_ref[own, :]
        key = k_ref[span, :]
        value = v_ref[span, :]
        product = grad.astype(f32) * out_ref[own, :].astype(f32)
        heads_dq = []
        for half in range(2):
            mine = low if half == 0 else ~low
            query_h = jnp.where(mine, query, jnp.zeros_like(query))
            grad_h = jnp.where(mine, grad, jnp.zeros_like(grad))
            product_h = jnp.where(mine, product, 0.0)
            coarse = product_h.astype(bf16)
            fine = (product_h - coarse.astype(f32)).astype(bf16)
            delta = (dot_on(ones, coarse, 1, 1) + dot_on(ones, fine, 1, 1))[0:1, :]
            scores = dot_on(key, query_h, 1, 1) + bias_ref[block]
            probs = jnp.exp(scores - lse_ref[pl.ds(2 * pair + half, 1), own])
            d_probs = dot_on(value, grad_h, 1, 1)
            d_scores = (probs * (d_probs - delta)).astype(bf16)
            dv_sum[span, :] += dot_on(probs.astype(bf16), grad_h, 1, 0)
            dk_sum[span, :] += dot_on(d_scores, query_h, 1, 0)
            heads_dq.append(dot_on(d_scores, key, 0, 0))
        dq_ref[own, :] = (
            jnp.where(low, heads_dq[0], heads_dq[1]) * (HEAD_DIM ** -0.5)
        ).astype(bf16)
    dk_ref[...] = dk_sum[...].astype(bf16)
    dv_ref[...] = dv_sum[...].astype(bf16)


def attention_backward(qkv, kv_earlier, grad_att, attended, lse, seg_query, seg_key, after):
    length = qkv.shape[0]
    width = qkv.shape[1] // 3
    pairs = width // LANES
    rows = min(256, length)
    keys = rows + WINDOW
    blocks = length // rows
    span = WINDOW + length

    def column(count, offset):
        return pl.BlockSpec((count, LANES), lambda p: (0, offset + p))

    return pl.pallas_call(
        functools.partial(attention_backward_kernel, rows, keys, blocks),
        grid=(pairs,),
        in_specs=[
            column(length, 0),
            column(length, pairs),
            column(length, 2 * pairs),
            column(WINDOW, 0),
            column(WINDOW, pairs),
            column(length, 0),
            column(length, 0),
            pl.BlockSpec((16, length), lambda p: (0, 0)),
            pl.BlockSpec((1, length), lambda p: (0, 0)),
            pl.BlockSpec((span, 1), lambda p: (0, 0)),
        ]
        + [ANY_SPEC] * len(after),
        out_specs=[column(length, 0), column(span, 0), column(span, 0)],
        out_shape=[
            jax.ShapeDtypeStruct((length, width), bf16),
            jax.ShapeDtypeStruct((span, width), bf16),
            jax.ShapeDtypeStruct((span, width), bf16),
        ],
        scratch_shapes=[
            pltpu.VMEM((blocks, keys, rows), f32),
            pltpu.VMEM((span, LANES), bf16),
            pltpu.VMEM((span, LANES), bf16),
            pltpu.VMEM((span, LANES), f32),
            pltpu.VMEM((span, LANES), f32),
        ],
        compiler_params=pltpu.CompilerParams(vmem_limit_bytes=48 * MIB),
        cost_estimate=cost(48),
        name="attention_backward",
    )(
        qkv, qkv, qkv, kv_earlier, kv_earlier, grad_att, attended, lse, seg_query, seg_key, *after
    )


def sigmoid(values):
    return 1.0 / (1.0 + jnp.exp(-values))


def gathered(rows_ref, block_refs):
    count = block_refs[0].shape[0]
    width = rows_ref.shape[1]
    for index, block_ref in enumerate(block_refs):
        rows_ref[index * count : (index + 1) * count, :] = block_ref[:, :width]


def scattered(block_refs, rows, which=0):
    count = block_refs[0].shape[1]
    for index, block_ref in enumerate(block_refs):
        block_ref[which] = rows[index * count : (index + 1) * count, :].astype(bf16)


def experts_forward_kernel(groups, *refs):
    block_refs, (gate_w_ref, up_w_ref, down_w_ref) = refs[:groups], refs[groups : groups + 3]
    out_refs, (gate_ref, up_ref, rows_ref) = refs[-groups - 3 : -3], refs[-3:]
    gathered(rows_ref, block_refs)
    rows_in = rows_ref[...]
    gate_pre = dot_on(rows_in, gate_w_ref[0], 1, 0)
    up_pre = dot_on(rows_in, up_w_ref[0], 1, 0)
    activated = (gate_pre * sigmoid(gate_pre) * up_pre).astype(bf16)
    gate_ref[0] = gate_pre.astype(bf16)
    up_ref[0] = up_pre.astype(bf16)
    scattered(out_refs, dot_on(activated, down_w_ref[0], 1, 0))


def experts_forward(blocks, gate_up_w, down_w, after):
    groups = len(blocks)
    count = down_w.shape[0]
    width, hidden = gate_up_w.shape[1:]
    part = blocks[0].shape[0] // count
    rows = groups * part
    block_spec = pl.BlockSpec((part, width), lambda j: (j, 0))
    hidden_spec = pl.BlockSpec((1, rows, hidden), lambda j: (j, 0, 0))
    hidden_shape = jax.ShapeDtypeStruct((count, rows, hidden), bf16)
    *produced, gate_pre, up_pre = pl.pallas_call(
        functools.partial(experts_forward_kernel, groups),
        grid=(count,),
        in_specs=[block_spec] * groups
        + [
            pl.BlockSpec((1, width, hidden), lambda j: (j, 0, 0)),
            pl.BlockSpec((1, width, hidden), lambda j: (count + j, 0, 0)),
            pl.BlockSpec((1, hidden, width), lambda j: (j, 0, 0)),
        ]
        + [ANY_SPEC] * len(after),
        out_specs=[pl.BlockSpec((1, part, width), lambda j: (0, j, 0))] * groups
        + [hidden_spec, hidden_spec],
        out_shape=[jax.ShapeDtypeStruct((1, count * part, width), bf16)] * groups
        + [hidden_shape, hidden_shape],
        scratch_shapes=[pltpu.VMEM((rows, width), bf16)],
        compiler_params=pltpu.CompilerParams(vmem_limit_bytes=48 * MIB),
        cost_estimate=cost(26),
        name="experts_forward",
    )(*blocks, gate_up_w, gate_up_w, down_w, *after)
    return produced, gate_pre, up_pre


def experts_backward_kernel(groups, chunks, whole, has_sums, *refs):
    block_refs, d_refs, given = refs[:groups], refs[groups : 2 * groups], refs[2 * groups :]
    gate_w_ref, up_w_ref, down_w_ref = given[:3]
    if whole:
        share_refs, given = given[3 : 3 + groups], given[3 + groups :]
        *refs, produced_ref = refs
    else:
        (gate_ref, up_ref), given = given[3:5], given[5:]
    out_refs = refs[-5 - groups : -5]
    gate_up_grad_ref, down_grad_ref, total_ref, rows_ref, d_ref = refs[-5:]
    chunk = pl.program_id(1)

    @pl.when(chunk == 0)
    def _():
        gathered(rows_ref, block_refs)
        if whole:
            count = d_refs[0].shape[0]
            for index in range(groups):
                share = share_refs[index][...].astype(f32)
                share = share[:, 0:1] + share[:, 1:2]
                d_ref[index * count : (index + 1) * count, :] = (
                    d_refs[index][...].astype(f32) * share
                ).astype(bf16)
        else:
            gathered(d_ref, d_refs)

    rows_in = rows_ref[...]
    d_out = d_ref[...]
    if whole:
        gate_pre = dot_on(rows_in, gate_w_ref[0], 1, 0)
        up_pre = dot_on(rows_in, up_w_ref[0], 1, 0)
    else:
        gate_pre = gate_ref[0].astype(f32)
        up_pre = up_ref[0].astype(f32)
    share = sigmoid(gate_pre)
    swish = gate_pre * share
    activated = (swish * up_pre).astype(bf16)
    d_act = dot_on(d_out, down_w_ref[0], 1, 1)
    d_gate = (d_act * up_pre * (share * (1.0 + gate_pre * (1.0 - share)))).astype(bf16)
    d_up = (d_act * swish).astype(bf16)
    part = dot_on(d_gate, gate_w_ref[0], 1, 1) + dot_on(d_up, up_w_ref[0], 1, 1)
    gate_grad = dot_on(rows_in, d_gate, 0, 0)
    up_grad = dot_on(rows_in, d_up, 0, 0)
    down_grad = dot_on(activated, d_out, 0, 0)
    if has_sums:
        gate_up_sum_ref, down_sum_ref = given[:2]
        gate_grad += gate_up_sum_ref[0, 0].astype(f32)
        up_grad += gate_up_sum_ref[1, 0].astype(f32)
        down_grad += down_sum_ref[0].astype(f32)
    gate_up_grad_ref[0, 0] = gate_grad.astype(bf16)
    gate_up_grad_ref[1, 0] = up_grad.astype(bf16)
    down_grad_ref[0] = down_grad.astype(bf16)
    sums = [(total_ref, part)]
    if whole:
        sums.append((produced_ref, dot_on(activated, down_w_ref[0], 1, 0)))

    @pl.when(chunk == 0)
    def _():
        for sum_ref, value in sums:
            sum_ref[...] = value

    @pl.when(chunk > 0)
    def _():
        for sum_ref, value in sums:
            sum_ref[...] += value

    @pl.when(chunk == chunks - 1)
    def _():
        scattered(out_refs, total_ref[...], len(sums) - 1)
        if whole:
            scattered(out_refs, produced_ref[...])


def experts_backward(blocks, d_blocks, pre, gate_up_w, down_w, sums, after):
    groups = len(blocks)
    count, hidden, width = down_w.shape
    part = blocks[0].shape[0] // count
    rows = groups * part
    whole = pre is None
    chunk = min(512, hidden)
    chunks = hidden // chunk
    block_spec = pl.BlockSpec((part, width), lambda j, f: (j, 0))
    hidden_spec = pl.BlockSpec((1, rows, chunk), lambda j, f: (j, 0, f))
    wide_spec = pl.BlockSpec((1, width, chunk), lambda j, f: (j, 0, f))
    up_spec = pl.BlockSpec((1, width, chunk), lambda j, f: (count + j, 0, f))
    tall_spec = pl.BlockSpec((1, chunk, width), lambda j, f: (j, f, 0))
    both_spec = pl.BlockSpec((2, 1, width, chunk), lambda j, f: (0, j, 0, f))
    operands = [*blocks, *d_blocks, gate_up_w, gate_up_w, down_w]
    specs = [block_spec] * (2 * groups) + [wide_spec, up_spec, tall_spec]
    if whole:
        operands.extend(blocks)
        specs += [pl.BlockSpec((part, LANES), lambda j, f: (j, width // LANES))] * groups
    else:
        operands.extend(pre)
        specs += [hidden_spec, hidden_spec]
    if sums is not None:
        operands.extend(sums)
        specs.extend([both_spec, tall_spec])
    outs = 2 if whole else 1
    *out, gate_up_grad, down_grad = pl.pallas_call(
        functools.partial(experts_backward_kernel, groups, chunks, whole, sums is not None),
        grid=(count, chunks),
        in_specs=specs + [ANY_SPEC] * len(after),
        out_specs=[pl.BlockSpec((outs, part, width), lambda j, f: (0, j, 0))] * groups
        + [both_spec, tall_spec],
        out_shape=[jax.ShapeDtypeStruct((outs, count * part, width), bf16)] * groups
        + [
            jax.ShapeDtypeStruct((2, count, width, hidden), bf16),
            jax.ShapeDtypeStruct((count, hidden, width), bf16),
        ],
        scratch_shapes=[
            pltpu.VMEM((rows, width), f32),
            pltpu.VMEM((rows, width), bf16),
            pltpu.VMEM((rows, width), bf16),
        ]
        + ([pltpu.VMEM((rows, width), f32)] if whole else []),
        compiler_params=pltpu.CompilerParams(vmem_limit_bytes=58 * MIB),
        cost_estimate=cost(75 if whole else 52),
        name="experts_whole" if whole else "experts_backward",
    )(*operands, *after)
    return out, (gate_up_grad, down_grad)


def passed_along(block, axis, distance):
    devices = range(lax.axis_size(axis))
    route = [(i - distance, i) for i in devices if i - distance in devices]
    return lax.ppermute(block, axis, route)


def earlier_rows(block, hop_count):
    pieces = [passed_along(block, "context", hop) for hop in range(hop_count, 0, -1)]
    missing = WINDOW - hop_count * block.shape[-2]
    if missing > 0:
        shape = block.shape[:-2] + (missing, block.shape[-1])
        pieces = [jnp.zeros(shape, block.dtype)] + pieces
    rows = pieces[0] if len(pieces) == 1 else jnp.concatenate(pieces, axis=-2)
    return rows[..., rows.shape[-2] - WINDOW :, :]


def returned_rows(block, length, hop_count):
    total = None
    for hop in range(1, hop_count + 1):
        first = WINDOW - hop * length
        part = block[max(first, 0) : first + length]
        if first < 0:
            part = jnp.concatenate([jnp.zeros((-first, block.shape[1]), block.dtype), part])
        part = passed_along(part, "context", -hop).astype(f32)
        total = part if total is None else total + part
    return total


def exchange(blocks, direction):
    groups = lax.axis_size("expert")
    out = []
    for d, block in enumerate(blocks):
        step = d * direction
        route = [(i, (i + step) % groups) for i in range(groups)]
        out.append(block if d == 0 else lax.ppermute(block, "expert", route))
    return out


GATE, OF_NORMED, NORMED_SHARE, VECTOR_SHARE, MIX, SCALE, CHOSEN = 0, 2, 4, 5, 7, 9, 10
GAINS_LANE = 2 * ROUTED + 8
VECTOR_ROW, ATTN_GAIN_ROW, MOE_GAIN_ROW = 0, 2, 3


def inverse_rms(rows):
    return lax.rsqrt(jnp.mean(rows * rows, axis=-1, keepdims=True) + norm_eps)


def lane_iota(rows):
    return lax.broadcasted_iota(jnp.int32, (rows, LANES), 1)


def placed_on_lanes(rows, values):
    lane = lane_iota(rows)
    total = jnp.zeros((rows, LANES), f32)
    for index, value in values.items():
        total = jnp.where(lane == index, value, total)
    return total


def routing_kernel(routes_ref, base_ref, columns_ref, rows_ref):
    length = routes_ref.shape[1]
    lane = lane_iota(length)
    onehots = [(lane == routes_ref[0, :, k : k + 1]).astype(f32) for k in range(TOP)]
    counts = (onehots[0] + onehots[1]).astype(bf16)
    earlier = lax.broadcasted_iota(jnp.int32, (length, length), 0) > lax.broadcasted_iota(
        jnp.int32, (length, length), 1
    )
    rank = dot_on(jnp.where(earlier, 1.0, 0.0).astype(bf16), counts, 1, 0)
    place = base_ref[...] + jnp.where(lane < EXPERTS, rank, 0.0)
    slots = placed_on_lanes(
        length,
        {k: jnp.sum(onehots[k] * place, axis=1, keepdims=True) for k in range(TOP)},
    )
    columns_ref[0] = slots.astype(jnp.int32)
    rows_ref[0] = jnp.round(rows_of(slots, range(TOP))).astype(jnp.int32)


def routing_slots(routes, groups, capacity):
    count, length, _ = routes.shape
    per_dev = EXPERTS // groups
    expert = jnp.arange(LANES)
    place = (expert // per_dev - lax.axis_index("expert")) % groups
    base = (place * per_dev + expert % per_dev) * capacity
    base = jnp.where(expert < EXPERTS, base, -1).astype(f32)[None, :]
    return pl.pallas_call(
        routing_kernel,
        grid=(count,),
        in_specs=[
            pl.BlockSpec((1, length, TOP), lambda m: (m, 0, 0)),
            pl.BlockSpec((1, LANES), lambda m: (0, 0)),
        ],
        out_specs=[
            pl.BlockSpec((1, length, LANES), lambda m: (m, 0, 0)),
            pl.BlockSpec((1, 8, length), lambda m: (m, 0, 0)),
        ],
        out_shape=[
            jax.ShapeDtypeStruct((count, length, LANES), jnp.int32),
            jax.ShapeDtypeStruct((count, 8, length), jnp.int32),
        ],
        compiler_params=pltpu.CompilerParams(vmem_limit_bytes=32 * MIB),
        cost_estimate=cost(4),
        name="routing",
    )(routes, base)


def dispatch_kernel(mode, per_group, groups, rows_ref, slots_ref, gates_ref, *rest):
    out_refs = rest[-groups:]
    count, length = out_refs[0].shape[0], rows_ref.shape[0]
    width = rows_ref.shape[1]
    rows = rows_ref[...].astype(bf16)
    for group, out_ref in enumerate(out_refs):
        first = group * per_group + pl.program_id(0) * count
        slot = first + lax.broadcasted_iota(jnp.int32, (count, length), 0)
        hits = [slot == slots_ref[k : k + 1, :] for k in range(TOP)]
        table = jnp.where(hits[0] | hits[1], 1.0, 0.0).astype(bf16)
        found = dot_on(table, rows, 1, 0)
        if mode == "plain":
            out_ref[...] = found.astype(bf16)
            continue
        gate = jnp.sum(
            jnp.where(hits[0], gates_ref[0:1, :], 0.0)
            + jnp.where(hits[1], gates_ref[1:2, :], 0.0),
            axis=1,
            keepdims=True,
        )
        if mode == "scaled":
            out_ref[...] = (found * gate).astype(bf16)
            continue
        out_ref[:, :width] = found.astype(bf16)
        coarse = gate.astype(bf16).astype(f32)
        out_ref[:, width:] = placed_on_lanes(count, {0: coarse, 1: gate - coarse}).astype(bf16)


def dispatch(rows, slot_rows, gate_rows, mode, slots, groups, after=()):
    length, width = rows.shape
    per_group = slots // groups
    count = min(256, per_group)
    out_width = width + LANES if mode == "with gate" else width
    return pl.pallas_call(
        functools.partial(dispatch_kernel, mode, per_group, groups),
        grid=(per_group // count,),
        in_specs=[
            pl.BlockSpec((length, width), lambda s: (0, 0)),
            pl.BlockSpec((8, length), lambda s: (0, 0)),
            pl.BlockSpec((8, length), lambda s: (0, 0)),
        ]
        + [ANY_SPEC] * len(after),
        out_specs=[pl.BlockSpec((count, out_width), lambda s: (s, 0))] * groups,
        out_shape=[jax.ShapeDtypeStruct((per_group, out_width), bf16)] * groups,
        compiler_params=pltpu.CompilerParams(vmem_limit_bytes=32 * MIB),
        cost_estimate=cost(6),
        name="dispatch",
    )(rows, slot_rows, gate_rows, *after)


def attention_output_kernel(
    hidden_ref, attended_ref, out_w_ref, small_w_ref, vectors_ref, prior_ref, residual_ref,
    routes_ref, mid_ref, low_ref, logits_ref, scalars_ref, gates_ref,
):
    rows = hidden_ref.shape[0]
    mid = hidden_ref[...] + dot_on(attended_ref[...], out_w_ref[...], 1, 0)
    mid_ref[...] = mid
    scale = inverse_rms(mid)
    low = (mid * scale * vectors_ref[MOE_GAIN_ROW : MOE_GAIN_ROW + 1, :]).astype(bf16)
    low_ref[...] = low
    logits = dot_on(low, small_w_ref[...], 1, 0) + jnp.dot(
        prior_ref[...], residual_ref[...], precision=highest
    )
    logits_ref[...] = logits
    lane = lane_iota(rows)
    onehots = [lane == routes_ref[:, k : k + 1] for k in range(TOP)]

    def lane_sum(values):
        return jnp.sum(values, axis=1, keepdims=True)

    difference = lane_sum(jnp.where(onehots[0], logits, jnp.where(onehots[1], -logits, 0.0)))
    gates = (sigmoid(difference), sigmoid(-difference))
    chosen = [
        [jnp.where(routes_ref[:, k : k + 1] == EXPERTS + 2 + j, 1.0, 0.0) for j in range(2)]
        for k in range(TOP)
    ]
    alphas = []
    for j in range(2):
        at = ROUTED + 2 * j
        gap = lane_sum(jnp.where(lane == at, logits, jnp.where(lane == at + 1, -logits, 0.0)))
        alphas.append((sigmoid(gap), sigmoid(-gap)))
    of_normed = [
        jnp.where(routes_ref[:, k : k + 1] == EXPERTS + 1, 1.0, 0.0)
        + chosen[k][0] * alphas[0][0]
        + chosen[k][1] * alphas[1][0]
        for k in range(TOP)
    ]
    vector_gate = [gates[0] * chosen[0][j] + gates[1] * chosen[1][j] for j in range(2)]
    values = {
        GATE: gates[0], GATE + 1: gates[1],
        OF_NORMED: of_normed[0], OF_NORMED + 1: of_normed[1],
        NORMED_SHARE: gates[0] * of_normed[0] + gates[1] * of_normed[1],
        SCALE: scale,
    }
    for j in range(2):
        values[VECTOR_SHARE + j] = vector_gate[j] * alphas[j][1]
        values[MIX + j] = vector_gate[j] * alphas[j][0] * alphas[j][1]
        for k in range(TOP):
            values[CHOSEN + 2 * k + j] = chosen[k][j] * alphas[j][1]
    scalars = placed_on_lanes(rows, values)
    scalars_ref[...] = scalars
    gates_ref[...] = rows_of(scalars, (GATE, GATE + 1))


def attention_output(hidden, attended, weights, prior, routes):
    length, width = hidden.shape
    rows = min(256, length)
    wide = pl.BlockSpec((rows, width), lambda t: (t, 0))
    lanes = pl.BlockSpec((rows, LANES), lambda t: (t, 0))
    return pl.pallas_call(
        attention_output_kernel,
        grid=(length // rows,),
        in_specs=[
            wide,
            wide,
            pl.BlockSpec((width, width), lambda t: (0, 3)),
            pl.BlockSpec((width, LANES), lambda t: (0, 4 * width // LANES)),
            pl.BlockSpec((8, width), lambda t: (0, 0)),
            lanes,
            pl.BlockSpec((LANES, LANES), lambda t: (0, 0)),
            pl.BlockSpec((rows, TOP), lambda t: (t, 0)),
        ],
        out_specs=[wide, wide, lanes, lanes, pl.BlockSpec((8, rows), lambda t: (0, t))],
        out_shape=[
            jax.ShapeDtypeStruct((length, width), f32),
            jax.ShapeDtypeStruct((length, width), bf16),
            jax.ShapeDtypeStruct((length, LANES), f32),
            jax.ShapeDtypeStruct((length, LANES), f32),
            jax.ShapeDtypeStruct((8, length), f32),
        ],
        compiler_params=pltpu.CompilerParams(vmem_limit_bytes=24 * MIB),
        cost_estimate=cost(8),
        name="attention_output",
    )(
        hidden, attended, weights["dense"], weights["dense"], weights["vectors"], prior,
        weights["residual"], routes,
    )


def selected(columns, block_refs, which):
    per_group = block_refs[0].shape[0]
    total = None
    for group, block_ref in enumerate(block_refs):
        slot = group * per_group + lax.broadcasted_iota(
            jnp.int32, (columns.shape[0], per_group), 1
        )
        hit = slot == columns[:, which[0] : which[0] + 1]
        for k in which[1:]:
            hit = hit | (slot == columns[:, k : k + 1])
        part = dot_on(jnp.where(hit, 1.0, 0.0).astype(bf16), block_ref[...], 1, 0)
        total = part if total is None else total + part
    return total


def combine_kernel(last, groups, waits, *refs):
    back_refs, (columns_ref, mid_ref, scalars_ref, vectors_ref, next_ref) = (
        refs[:groups], refs[groups : groups + 5],
    )
    out_refs = refs[groups + 5 + waits :]
    columns, scalars = columns_ref[...], scalars_ref[...]
    mid = mid_ref[...]
    normed = mid * scalars[:, SCALE : SCALE + 1] * vectors_ref[MOE_GAIN_ROW : MOE_GAIN_ROW + 1, :]
    total = mid + scalars[:, NORMED_SHARE : NORMED_SHARE + 1] * normed
    for j in range(2):
        row = vectors_ref[VECTOR_ROW + j : VECTOR_ROW + j + 1, :]
        total += scalars[:, VECTOR_SHARE + j : VECTOR_SHARE + j + 1] * row
    for k in range(TOP):
        branch = selected(columns, back_refs, (k,))
        out_refs[k][...] = branch.astype(bf16)
        total += scalars[:, GATE + k : GATE + k + 1] * branch
    if last:
        out_refs[TOP][...] = total.astype(bf16)
    else:
        out_refs[TOP][...] = total
        out_refs[TOP + 1][...] = (
            total * inverse_rms(total) * next_ref[ATTN_GAIN_ROW : ATTN_GAIN_ROW + 1, :]
        ).astype(bf16)


def combine(back, columns, mid, scalars, vectors, next_vectors, after):
    last = next_vectors is None
    length, width = mid.shape
    back, which = back
    groups, per_group = len(back), back[0].shape[1]
    rows = min(256, length)
    wide = pl.BlockSpec((rows, width), lambda t: (t, 0))
    lanes = pl.BlockSpec((rows, LANES), lambda t: (t, 0))
    vector_spec = pl.BlockSpec((8, width), lambda t: (0, 0))
    low = jax.ShapeDtypeStruct((length, width), bf16)
    return pl.pallas_call(
        functools.partial(combine_kernel, last, groups, len(after)),
        grid=(length // rows,),
        in_specs=[pl.BlockSpec((None, per_group, width), lambda t: (which, 0, 0))] * groups
        + [lanes, wide, lanes, vector_spec, vector_spec]
        + [ANY_SPEC] * len(after),
        out_specs=[wide] * (TOP + 1 if last else TOP + 2),
        out_shape=[low, low, low]
        if last
        else [low, low, jax.ShapeDtypeStruct((length, width), f32), low],
        compiler_params=pltpu.CompilerParams(vmem_limit_bytes=24 * MIB),
        cost_estimate=cost(8),
        name="combine",
    )(*back, columns, mid, scalars, vectors, vectors if last else next_vectors, *after)


def token_backward_kernel(
    has_prior, groups, *refs
):
    back_refs, rest = refs[:groups], refs[groups:]
    (
        columns_ref, grad_ref, mid_ref, scalars_ref, branch0_ref, branch1_ref, low_ref, prior_ref,
        attended_ref, routes_ref, out_w_ref, small_w_ref, vectors_ref, residual_ref,
    ) = rest[:14]
    rest = rest[14:]
    d_mid_ref, d_att_ref, d_prior_ref, g_out_ref, g_small_ref, g_residual_ref, g_gain_ref = (
        rest[-7:]
    )
    step = pl.program_id(0)
    rows = mid_ref.shape[0]
    columns, scalars = columns_ref[...], scalars_ref[...]
    grad = grad_ref[...].astype(f32)
    mid = mid_ref[...]
    gain = vectors_ref[MOE_GAIN_ROW : MOE_GAIN_ROW + 1, :]
    scale = scalars[:, SCALE : SCALE + 1]
    unit = mid * scale
    lane = lane_iota(rows)

    def scalar(index):
        return scalars[:, index : index + 1]

    def row_sum(values):
        return jnp.sum(values, axis=1, keepdims=True)

    along = row_sum(grad * (unit * gain))
    along_vector = [
        row_sum(grad * vectors_ref[VECTOR_ROW + j : VECTOR_ROW + j + 1, :]) for j in range(2)
    ]
    d_gate = []
    for k, branch_ref in enumerate((branch0_ref, branch1_ref)):
        value = row_sum(grad * branch_ref[...].astype(f32)) + scalar(OF_NORMED + k) * along
        for j in range(2):
            value += scalar(CHOSEN + 2 * k + j) * along_vector[j]
        d_gate.append(value)
    d_choice = scalar(GATE) * scalar(GATE + 1) * (d_gate[0] - d_gate[1])
    d_small = jnp.where(
        lane == routes_ref[:, 0:1], d_choice, jnp.where(lane == routes_ref[:, 1:2], -d_choice, 0.0)
    )
    if has_prior:
        d_small += jnp.where(lane < ROUTED, rest[0][...], 0.0)
    d_logits = d_small
    for j in range(2):
        value = scalar(MIX + j) * (along - along_vector[j])
        at = ROUTED + 2 * j
        d_small = jnp.where(lane == at, value, jnp.where(lane == at + 1, -value, d_small))
    d_small_low = d_small.astype(bf16)
    d_prior_ref[...] = lax.dot_general(
        d_logits, residual_ref[...], (((1,), (1,)), ((), ())), precision=highest
    )
    vector_shares = placed_on_lanes(
        rows, {ROUTED + 4 + j: scalar(VECTOR_SHARE + j) for j in range(2)}
    ).astype(bf16)
    g_small = dot_on(low_ref[...], d_small_low, 0, 0) + dot_on(
        grad.astype(bf16), vector_shares, 0, 0
    )
    g_residual = lax.dot_general(
        prior_ref[...], d_logits, (((0,), (0,)), ((), ())), precision=highest
    )
    d_normed = (
        selected(columns, back_refs, (0, 1))
        + scalar(NORMED_SHARE) * grad
        + dot_on(d_small_low, small_w_ref[...], 1, 1)
    )
    g_gain = jnp.sum(d_normed * unit, axis=0, keepdims=True)
    d_unit = d_normed * gain
    d_mid = grad + (d_unit - unit * jnp.mean(d_unit * unit, axis=-1, keepdims=True)) * scale
    d_mid_ref[...] = d_mid
    d_mid_low = d_mid.astype(bf16)
    d_att_ref[...] = dot_on(d_mid_low, out_w_ref[...], 1, 1).astype(bf16)
    g_out = dot_on(attended_ref[...], d_mid_low, 0, 0)

    @pl.when(step == 0)
    def _():
        g_out_ref[...] = g_out
        g_small_ref[...] = g_small
        g_residual_ref[...] = g_residual
        g_gain_ref[...] = jnp.broadcast_to(g_gain, g_gain_ref.shape)

    @pl.when(step > 0)
    def _():
        g_out_ref[...] += g_out
        g_small_ref[...] += g_small
        g_residual_ref[...] += g_residual
        g_gain_ref[...] += jnp.broadcast_to(g_gain, g_gain_ref.shape)


def token_backward(back, kept, grad, weights, columns, routes, d_prior, after):
    length, width = grad.shape
    back, which = back
    groups, per_group = len(back), back[0].shape[1]
    rows = min(256, length)
    wide = pl.BlockSpec((rows, width), lambda t: (t, 0))
    lanes = pl.BlockSpec((rows, LANES), lambda t: (t, 0))

    def fixed(*shape, at=0):
        return pl.BlockSpec(shape, lambda t: (0, at))

    operands = [
        *back, columns, grad, kept["mid"], kept["scalars"], kept["branch"][0], kept["branch"][1],
        kept["low"], kept["prior"], kept["attended"], routes, weights["dense"], weights["dense"],
        weights["vectors"], weights["residual"],
    ]
    specs = [
        *[pl.BlockSpec((None, per_group, width), lambda t: (which, 0, 0))] * groups,
        lanes, wide, wide, lanes, wide, wide, wide, lanes, wide,
        pl.BlockSpec((rows, TOP), lambda t: (t, 0)), fixed(width, width, at=3),
        fixed(width, LANES, at=4 * width // LANES), fixed(8, width), fixed(LANES, LANES),
    ]
    if d_prior is not None:
        operands.append(d_prior)
        specs.append(lanes)
    return pl.pallas_call(
        functools.partial(token_backward_kernel, d_prior is not None, groups),
        grid=(length // rows,),
        in_specs=specs + [ANY_SPEC] * len(after),
        out_specs=[
            wide, wide, lanes, fixed(width, width), fixed(width, LANES), fixed(LANES, LANES),
            fixed(8, width),
        ],
        out_shape=[
            jax.ShapeDtypeStruct((length, width), f32),
            jax.ShapeDtypeStruct((length, width), bf16),
            jax.ShapeDtypeStruct((length, LANES), f32),
            jax.ShapeDtypeStruct((width, width), f32),
            jax.ShapeDtypeStruct((width, LANES), f32),
            jax.ShapeDtypeStruct((LANES, LANES), f32),
            jax.ShapeDtypeStruct((8, width), f32),
        ],
        compiler_params=pltpu.CompilerParams(vmem_limit_bytes=48 * MIB),
        cost_estimate=cost(25),
        name="token_backward",
    )(*operands, *after)


def finish_backward_kernel(
    has_later, hidden_ref, d_mid_ref, d_attn_ref, vectors_ref, *rest
):
    out_ref, g_gain_ref = rest[-2:]
    hidden = hidden_ref[...]
    d_attn = d_attn_ref[...]
    if has_later:
        d_attn += rest[0][...].astype(f32)
    scale = inverse_rms(hidden)
    unit = hidden * scale
    g_gain = jnp.broadcast_to(jnp.sum(d_attn * unit, axis=0, keepdims=True), g_gain_ref.shape)
    d_unit = d_attn * vectors_ref[ATTN_GAIN_ROW : ATTN_GAIN_ROW + 1, :]
    out_ref[...] = (
        d_mid_ref[...] + (d_unit - unit * jnp.mean(d_unit * unit, axis=-1, keepdims=True)) * scale
    ).astype(out_ref.dtype)

    @pl.when(pl.program_id(0) == 0)
    def _():
        g_gain_ref[...] = g_gain

    @pl.when(pl.program_id(0) > 0)
    def _():
        g_gain_ref[...] += g_gain


def finish_backward(hidden, d_mid, d_attn, vectors, later, out_type, after):
    length, width = hidden.shape
    rows = min(256, length)
    wide = pl.BlockSpec((rows, width), lambda t: (t, 0))
    vector_spec = pl.BlockSpec((8, width), lambda t: (0, 0))
    extra = [] if later is None else [later]
    return pl.pallas_call(
        functools.partial(finish_backward_kernel, later is not None),
        grid=(length // rows,),
        in_specs=[wide, wide, wide, vector_spec] + [wide] * len(extra) + [ANY_SPEC] * len(after),
        out_specs=[wide, vector_spec],
        out_shape=[
            jax.ShapeDtypeStruct((length, width), out_type),
            jax.ShapeDtypeStruct((8, width), f32),
        ],
        compiler_params=pltpu.CompilerParams(vmem_limit_bytes=24 * MIB),
        cost_estimate=cost(6),
        name="finish_backward",
    )(hidden, d_mid, d_attn, vectors, *extra, *after)


def fetch_layer(layer, local):
    width = local["w_query"].shape[2]
    shard = local["w_query"].shape[1]
    const_w = jnp.transpose(local["w_const"][layer], (1, 0, 2)).reshape(shard, 4)
    small = jnp.concatenate(
        [
            local["w_router"][layer], const_w, local["const_vec"][layer].T,
            local["norm_attn"][layer][:, None], local["norm_moe"][layer][:, None],
            jnp.zeros((shard, LANES - ROUTED - 8), bf16),
        ],
        axis=1,
    )
    packed = jnp.concatenate(
        [local["w_query"][layer], local["w_key"][layer], local["w_value"][layer],
         local["w_out"][layer], small],
        axis=1,
    )
    dense = lax.all_gather(packed, SHARDED, axis=0, tiled=True)
    gate_up = jnp.concatenate([local["w_gate"][layer], local["w_up"][layer]], axis=0)
    gate_up = lax.all_gather(gate_up, SHARDED, axis=1, tiled=True)
    down = lax.all_gather(local["w_down"][layer], SHARDED, axis=1, tiled=True)
    at = 4 * width + ROUTED + 4
    vectors = dense[:, at : at + 8].T.astype(f32)
    residual = local["w_res"][layer].astype(f32)
    blank = LANES - ROUTED
    return dict(
        dense=dense, vectors=vectors, gate_up=gate_up, down=down,
        residual=jnp.pad(residual, ((0, blank), (0, blank))),
    )


def per_device(
    hidden_in, segments, routes, prev_logits, out_grad, norm_attn, w_query, w_key, w_value,
    w_out, norm_moe, w_router, w_res, w_const, const_vec, w_gate, w_up, w_down,
):
    local = dict(
        norm_attn=norm_attn, w_query=w_query, w_key=w_key, w_value=w_value, w_out=w_out,
        norm_moe=norm_moe, w_router=w_router, w_res=w_res, w_const=w_const,
        const_vec=const_vec, w_gate=w_gate, w_up=w_up, w_down=w_down,
    )
    micro_count, _, length, width = hidden_in.shape
    micros = range(micro_count)
    layers = norm_attn.shape[0]
    groups = lax.axis_size("expert")
    hop_count = min((WINDOW + length - 2) // length, lax.axis_size("context") - 1)
    capacity = length // 4
    slots = EXPERTS * capacity
    block_start = lax.axis_index("context") * length
    routes = routes[:, 0]
    columns, slot_rows = routing_slots(routes, groups, capacity)
    blank_gates = jnp.zeros((8, length), f32)

    def normed(hidden, gain):
        return (hidden * inverse_rms(hidden) * gain).astype(bf16)

    last_arrived = []

    def in_turn(blocks, micro):
        others = held(list(blocks[1:]), tuple(last_arrived[1:]) if micro > 0 else ())
        last_arrived[:] = exchange(list(blocks[:1]) + others, -1)
        return list(last_arrived)

    early = []

    def send_early(micro, after):
        sent = dispatch(
            out_grad[micro, 0], slot_rows[micro], blank_gates, "plain", slots, groups, after
        )
        early.append(exchange(sent, 1))

    send_early(0, ())
    fetched = [fetch_layer(layer, local) for layer in range(layers)]
    segs, state = [], []
    for micro in micros:
        whole = segments[micro, 0]
        padded = jnp.concatenate([jnp.full((WINDOW,), -1, jnp.int32), whole])
        query = lax.dynamic_slice_in_dim(whole, block_start, length, 0)
        key = lax.dynamic_slice_in_dim(padded, block_start, WINDOW + length, 0)
        segs.append((query, key))
        hidden = hidden_in[micro, 0].astype(f32)
        gain = fetched[0]["vectors"][ATTN_GAIN_ROW : ATTN_GAIN_ROW + 1]
        prior = jnp.pad(prev_logits[micro, 0], ((0, 0), (0, LANES - ROUTED)))
        state.append(
            (
                hidden, normed(hidden, gain),
                None if micro > 0 else earlier_rows(hidden_in[micro, 0], hop_count), prior,
            )
        )

    saved = [[None] * layers for _ in micros]
    expert_sums = [None] * layers

    def attention_part(layer, micro, after, after_output):
        weights = fetched[layer]
        hidden, attn_in, attn_earlier, prior = state[micro]
        if layer == 0:
            if micro > 0:
                (block,) = held([hidden_in[micro, 0]], (saved[micro - 1][0]["attended"],))
                attn_earlier = earlier_rows(block, hop_count)
            attn_earlier = normed(attn_earlier.astype(f32), weights["vectors"][ATTN_GAIN_ROW][None])
        qkv = dot_on(attn_in, weights["dense"][:, : 3 * width], 1, 0).astype(bf16)
        kv_earlier = dot_on(attn_earlier, weights["dense"][:, width : 3 * width], 1, 0).astype(bf16)
        query, key = segs[micro]
        attended, lse = attention_forward(qkv, kv_earlier, query[:, None], key[None, :], after)
        mid, low, logits, scalars, gate_rows = attention_output(
            hidden, attended, weights, prior, routes[micro]
        )
        mode = "with gate" if layer == layers - 1 else "plain"
        sent = dispatch(low, slot_rows[micro], gate_rows, mode, slots, groups, after_output)
        saved[micro][layer] = dict(
            hidden=hidden, attn_in=attn_in, attn_earlier=attn_earlier, prior=prior, qkv=qkv,
            kv_earlier=kv_earlier, attended=attended, lse=lse, mid=mid, low=low,
            scalars=scalars, gate_rows=gate_rows, logits=logits, arrived=exchange(sent, 1),
        )
        return sent[-1]

    def experts_part(layer, micro, after):
        kept = saved[micro][layer]
        gate_up_w, down_w = fetched[layer]["gate_up"], fetched[layer]["down"]
        if layer == layers - 1:
            out, expert_sums[layer] = experts_backward(
                kept["arrived"], early[micro], None, gate_up_w, down_w, expert_sums[layer], after
            )
            arrived = in_turn(out, 0)
            kept["returned"], kept["back"] = (arrived, 0), (arrived, 1)
        else:
            out, *kept["pre"] = experts_forward(kept["arrived"], gate_up_w, down_w, after)
            kept["returned"] = (in_turn(out, 0), 0)
        return out[-1]

    def combine_part(layer, micro, after):
        kept = saved[micro][layer]
        last = layer == layers - 1
        outs = combine(
            kept["returned"], columns[micro], kept["mid"], kept["scalars"],
            fetched[layer]["vectors"], None if last else fetched[layer + 1]["vectors"], after,
        )
        kept["branch"] = outs[:TOP]
        if last:
            return outs[TOP]
        state[micro] = (
            outs[TOP], outs[TOP + 1], earlier_rows(outs[TOP + 1], hop_count), kept["logits"],
        )
        return outs[TOP]

    def experts_back_part(layer, micro, d_rows, after):
        kept = saved[micro][layer]
        dx, expert_sums[layer] = experts_backward(
            kept["arrived"], d_rows, kept["pre"], fetched[layer]["gate_up"],
            fetched[layer]["down"], expert_sums[layer], after,
        )
        kept["back"] = (in_turn(dx, 0), 0)
        return dx[-1]

    def token_back_part(layer, micro, grad, d_prior, after):
        kept = saved[micro][layer]
        (
            kept["d_mid"], kept["d_att"], d_prior, kept["g_out"], kept["g_small"],
            kept["g_residual"], g_moe_gain,
        ) = token_backward(
            kept["back"], kept, grad, fetched[layer], columns[micro], routes[micro], d_prior, after
        )
        kept["g_moe_gain"] = g_moe_gain[0]
        return d_prior

    def attention_back_part(layer, micro, after):
        kept, dense = saved[micro][layer], fetched[layer]["dense"]
        query, key = segs[micro]
        dq, dk, dv = attention_backward(
            kept["qkv"], kept["kv_earlier"], kept["d_att"], kept["attended"], kept["lse"],
            query[None, :], key[:, None], after,
        )
        query_w, key_w, value_w = (dense[:, i * width : (i + 1) * width] for i in range(3))
        kept["later"] = None
        if hop_count > 0:
            d_earlier = (
                dot_on(dk[:WINDOW], key_w, 1, 1) + dot_on(dv[:WINDOW], value_w, 1, 1)
            ).astype(bf16)
            kept["later"] = returned_rows(d_earlier, length, hop_count)
        kept["d_attn"] = (
            dot_on(dq, query_w, 1, 1)
            + dot_on(dk[WINDOW:], key_w, 1, 1)
            + dot_on(dv[WINDOW:], value_w, 1, 1)
        )
        kept["grads"] = [
            dot_on(kept["attn_in"], dq, 0, 0),
            dot_on(kept["attn_in"], dk[WINDOW:], 0, 0)
            + dot_on(kept["attn_earlier"], dk[:WINDOW], 0, 0),
            dot_on(kept["attn_in"], dv[WINDOW:], 0, 0)
            + dot_on(kept["attn_earlier"], dv[:WINDOW], 0, 0),
            kept["g_out"],
            kept["g_small"],
        ]
        return dq

    def finish_back_part(layer, micro, after):
        kept = saved[micro][layer]
        d_hidden, g_attn_gain = finish_backward(
            kept["hidden"], kept["d_mid"], kept["d_attn"], fetched[layer]["vectors"],
            kept["later"], f32 if layer > 0 else bf16, after,
        )
        kept["g_attn_gain"] = g_attn_gain[0]
        return d_hidden

    expert_shares, dense_shares = [None] * layers, [None] * layers

    def reduce_experts(layer):
        gate_up, down = held(expert_sums[layer], saved[0][layer]["back"][0][1:])
        gate_up = gate_up.reshape((-1,) + gate_up.shape[2:])
        expert_shares[layer] = (
            lax.psum_scatter(gate_up, SHARDED, scatter_dimension=1, tiled=True),
            lax.psum_scatter(down, SHARDED, scatter_dimension=1, tiled=True),
        )
        return expert_shares[layer]

    def total_of(layer, name):
        parts = [saved[micro][layer][name] for micro in micros]
        return sum(parts[1:], parts[0])

    def packed_dense(layer):
        parts = [saved[micro][layer]["grads"] for micro in micros]
        sums = [sum(values[1:], values[0]) for values in zip(*parts)]
        shards = lax.axis_size("context") * lax.axis_size("dp")
        at = ROUTED + 8
        residual = jnp.pad(
            total_of(layer, "g_residual")[:ROUTED, :ROUTED],
            ((0, width // shards - ROUTED), (at, LANES - at - ROUTED)),
        )
        small = sums[-1] + jnp.tile(residual, (shards, 1))
        if layer == 0:
            gains = [total_of(l, "g_moe_gain") for l in range(layers)]
            gains += [total_of(l, "g_attn_gain") for l in range(layers)]
            blank = jnp.zeros((LANES - GAINS_LANE - len(gains), width), f32)
            above = jnp.zeros((GAINS_LANE, width), f32)
            small = small + jnp.concatenate([above, jnp.stack(gains), blank]).T
        return jnp.concatenate([total.astype(bf16) for total in sums[:-1] + [small]], axis=1)

    def reduce_dense(layer, packed):
        shards = lax.axis_size("context") * lax.axis_size("dp")
        parts = packed.reshape(shards, width // shards, packed.shape[1])
        parts = lax.all_to_all(parts, SHARDED, split_axis=0, concat_axis=0, tiled=True)
        share = jnp.sum(parts.astype(f32), axis=0)
        if layer > 0:
            share = lax.psum(share.astype(bf16), "expert").astype(f32)
        else:
            span = 1
            while span < groups:
                sent = share.astype(bf16)
                route = [(i, i ^ span) for i in range(groups)]
                share = sent.astype(f32) + lax.ppermute(sent, "expert", route).astype(f32)
                span *= 2
        dense_shares[layer] = share
        return (share,)

    last = layers - 1
    d_rows = [None] * micro_count

    def send_back(layer, micro, after):
        grads[micro] = finish_back_part(layer, micro, after)
        sent = dispatch(
            grads[micro], slot_rows[micro], saved[micro][layer - 1]["gate_rows"], "scaled", slots,
            groups,
        )
        d_rows[micro] = exchange(sent, 1)
        return sent[-1]

    before = ()
    for layer in range(layers):
        for micro in micros:
            if layer > 0:
                before = (combine_part(layer - 1, micro, before),)
        if layer == last:
            for micro in micros[1:]:
                send_early(micro, before)
        for micro in micros:
            waits = tuple(early[-1][1:]) if micro == 0 else ()
            before = (attention_part(layer, micro, before, waits),)
        for micro in micros:
            before = (experts_part(layer, micro, before),)
    hidden_out = []

    grads = [out_grad[micro, 0] for micro in micros]
    d_priors = [None] * micro_count
    dense_wait = ()
    for layer in range(last, -1, -1):
        experts_ready = reduce_experts(layer)
        for micro in micros:
            if layer == last:
                hidden_out.append(combine_part(last, micro, before))
                before = (hidden_out[-1],)
            d_priors[micro] = token_back_part(layer, micro, grads[micro], d_priors[micro], before)
            before = (saved[micro][layer]["d_att"],)
            before = (attention_back_part(layer, micro, before),)
            if layer > 0:
                before = (send_back(layer, micro, before),)
        if layer > 0:
            (packed,) = held([packed_dense(layer)], before)
            dense_wait = reduce_dense(layer, packed)
            for micro in micros:
                if micro < len(experts_ready):
                    before += (experts_ready[micro],)
                before = (experts_back_part(layer - 1, micro, d_rows[micro], before),)
        else:
            for micro in micros:
                grads[micro] = finish_back_part(layer, micro, tuple(experts_ready) + dense_wait)
    reduce_dense(0, packed_dense(0))
    hidden_out = jnp.stack(hidden_out)[:, None]
    hidden_grad = jnp.stack(grads)[:, None]

    dense = jnp.stack(dense_shares)
    small = dense[:, :, 4 * width :]
    shard = small.shape[1]
    experts_total = [jnp.stack(parts).astype(f32) for parts in zip(*expert_shares)]
    per_dev = EXPERTS // groups
    return (
        hidden_out,
        hidden_grad,
        jnp.stack([small[0, :, GAINS_LANE + layers + l] for l in range(layers)]),
        dense[:, :, :width],
        dense[:, :, width : 2 * width],
        dense[:, :, 2 * width : 3 * width],
        dense[:, :, 3 * width : 4 * width],
        jnp.stack([small[0, :, GAINS_LANE + l] for l in range(layers)]),
        small[:, :, :ROUTED],
        small[:, :ROUTED, ROUTED + 8 : 2 * ROUTED + 8],
        jnp.transpose(
            small[:, :, ROUTED : ROUTED + 4].reshape(layers, shard, 2, 2), (0, 2, 1, 3)
        ),
        jnp.transpose(small[:, :, ROUTED + 4 : ROUTED + 6], (0, 2, 1)),
        experts_total[0][:, :per_dev],
        experts_total[0][:, per_dev:],
        experts_total[1],
    )

def solution(mesh):
    tokens = P(None, ("expert", "dp"), "context", None)
    rows = P(None, SHARDED, None)
    vector = P(None, SHARDED)
    experts = P(None, "expert", SHARDED, None)
    const = P(None, None, SHARDED, None)
    const_vector = P(None, None, SHARDED)
    return jax.shard_map(
        per_device,
        mesh=mesh,
        in_specs=(
            tokens, P(None, ("expert", "dp"), None), tokens, tokens, tokens, vector, rows, rows,
            rows, rows, vector, rows, P(), const, const_vector, experts, experts, experts,
        ),
        out_specs=(
            tokens, tokens, vector, rows, rows, rows, rows, vector, rows, P(), const,
            const_vector, experts, experts, experts,
        ),
        check_vma=False,
    )
```

```python
import functools

import jax
import jax.numpy as jnp
from jax import lax
from jax.experimental import pallas as pl
from jax.experimental.pallas import tpu as pltpu
from jax.sharding import PartitionSpec as P

HEADS = 12
HEAD_DIM = 64
EXPERTS = 8
TOP = 2
WINDOW = 1024
ROUTED = 12
LANES = 128
MIB = 1 << 20

norm_eps = 1e-05
masked = -1000000000.0
highest = lax.Precision.HIGHEST
f32 = jnp.float32
bf16 = jnp.bfloat16
SHARDED = ("context", "dp")


COST_SHARE = 0.3


def cost(microseconds):
    return pl.CostEstimate(
        flops=int(microseconds * COST_SHARE * 1.15e9), bytes_accessed=1, transcendentals=0
    )


ANY_SPEC = pl.BlockSpec(memory_space=pl.ANY)


def dot_on(left_op, right_op, left_dim, right_dim):
    return lax.dot_general(
        left_op,
        right_op,
        (((left_dim,), (right_dim,)), ((), ())),
        preferred_element_type=f32,
    )


def held(arrays, after):
    count = len(arrays)
    if not after:
        return list(arrays)
    return list(
        pl.pallas_call(
            lambda *refs: None,
            in_specs=[ANY_SPEC] * (count + len(after)),
            out_specs=[ANY_SPEC] * count,
            out_shape=[jax.ShapeDtypeStruct(array.shape, array.dtype) for array in arrays],
            input_output_aliases={index: index for index in range(count)},
            name="held",
        )(*arrays, *after)
    )


def rows_of(values, picks):
    count = 8 if len(picks) <= 8 else 16
    row = lax.broadcasted_iota(jnp.int32, (count, LANES), 0)
    lane = lax.broadcasted_iota(jnp.int32, (count, LANES), 1)
    pick = jnp.zeros((count, LANES), f32)
    for index, source in enumerate(picks):
        pick = jnp.where((row == index) & (lane == source), 1.0, pick)
    return lax.dot_general(
        pick, values, (((1,), (1,)), ((), ())), precision=highest, preferred_element_type=f32
    )


def join_spans(buffer_ref, earlier_ref, own_ref):
    buffer_ref[:WINDOW, :] = earlier_ref[...]
    buffer_ref[WINDOW:, :] = own_ref[...]


def attention_forward_kernel(
    rows, keys, blocks, q_ref, ko_ref, vo_ref, kp_ref, vp_ref, sq_ref, sk_ref, *rest
):
    out_ref, lse_rows_ref, lse_ref, bias_ref, k_ref, v_ref = rest[-6:]
    pair = pl.program_id(0)

    @pl.when(pair == 0)
    def _():
        lse_ref[...] = jnp.zeros_like(lse_ref)
        rel = lax.broadcasted_iota(jnp.int32, (rows, keys), 1) - lax.broadcasted_iota(
            jnp.int32, (rows, keys), 0
        )
        inside = (rel > 0) & (rel <= WINDOW)
        for block in range(blocks):
            first = block * rows
            same = sq_ref[first : first + rows, :] == sk_ref[:, first : first + keys]
            bias_ref[block] = jnp.where(inside & same, 0.0, masked)

    join_spans(k_ref, kp_ref, ko_ref)
    join_spans(v_ref, vp_ref, vo_ref)
    lane = lax.broadcasted_iota(jnp.int32, (rows, LANES), 1)
    low = lane < HEAD_DIM
    for block in range(blocks):
        own = slice(block * rows, (block + 1) * rows)
        span = slice(block * rows, block * rows + keys)
        query = q_ref[own, :] * (HEAD_DIM ** -0.5)
        key = k_ref[span, :]
        value = v_ref[span, :]
        heads_out = []
        for half in range(2):
            mine = low if half == 0 else ~low
            scores = (
                dot_on(jnp.where(mine, query, jnp.zeros_like(query)), key, 1, 1) + bias_ref[block]
            )
            row_max = jnp.max(scores, axis=1, keepdims=True)
            exponent = jnp.exp(scores - row_max)
            row_sum = jnp.sum(exponent, axis=1, keepdims=True)
            heads_out.append(dot_on(exponent.astype(bf16), value, 1, 0) * (1.0 / row_sum))
            lse_ref[own, :] = jnp.where(
                lane == 2 * pair + half, row_max + jnp.log(row_sum), lse_ref[own, :]
            )
        out_ref[own, :] = jnp.where(low, heads_out[0], heads_out[1]).astype(bf16)

    @pl.when(pair == pl.num_programs(0) - 1)
    def _():
        lse_rows_ref[...] = rows_of(lse_ref[...], range(HEADS))


def attention_forward(qkv, kv_earlier, seg_query, seg_key, after):
    length = qkv.shape[0]
    width = qkv.shape[1] // 3
    pairs = width // LANES
    rows = min(256, length)
    keys = rows + WINDOW
    blocks = length // rows
    span = WINDOW + length

    def column(count, offset):
        return pl.BlockSpec((count, LANES), lambda p: (0, offset + p))

    return pl.pallas_call(
        functools.partial(attention_forward_kernel, rows, keys, blocks),
        grid=(pairs,),
        in_specs=[
            column(length, 0),
            column(length, pairs),
            column(length, 2 * pairs),
            column(WINDOW, 0),
            column(WINDOW, pairs),
            pl.BlockSpec((length, 1), lambda p: (0, 0)),
            pl.BlockSpec((1, span), lambda p: (0, 0)),
        ]
        + [ANY_SPEC] * len(after),
        out_specs=[column(length, 0), pl.BlockSpec((16, length), lambda p: (0, 0))],
        out_shape=[
            jax.ShapeDtypeStruct((length, width), bf16),
            jax.ShapeDtypeStruct((16, length), f32),
        ],
        scratch_shapes=[
            pltpu.VMEM((length, LANES), f32),
            pltpu.VMEM((blocks, rows, keys), f32),
            pltpu.VMEM((span, LANES), bf16),
            pltpu.VMEM((span, LANES), bf16),
        ],
        compiler_params=pltpu.CompilerParams(vmem_limit_bytes=40 * MIB),
        cost_estimate=cost(32),
        name="attention_forward",
    )(qkv, qkv, qkv, kv_earlier, kv_earlier, seg_query, seg_key, *after)


def attention_backward_kernel(
    rows, keys, blocks, q_ref, ko_ref, vo_ref, kp_ref, vp_ref, do_ref, out_ref, lse_ref,
    sq_ref, sk_ref, *rest
):
    dq_ref, dk_ref, dv_ref, bias_ref, k_ref, v_ref, dk_sum, dv_sum = rest[-8:]
    pair = pl.program_id(0)

    @pl.when(pair == 0)
    def _():
        rel = lax.broadcasted_iota(jnp.int32, (keys, rows), 0) - lax.broadcasted_iota(
            jnp.int32, (keys, rows), 1
        )
        inside = (rel > 0) & (rel <= WINDOW)
        for block in range(blocks):
            first = block * rows
            same = sk_ref[first : first + keys, :] == sq_ref[:, first : first + rows]
            bias_ref[block] = jnp.where(inside & same, 0.0, masked)

    join_spans(k_ref, kp_ref, ko_ref)
    join_spans(v_ref, vp_ref, vo_ref)
    dk_sum[...] = jnp.zeros_like(dk_sum)
    dv_sum[...] = jnp.zeros_like(dv_sum)
    low = lax.broadcasted_iota(jnp.int32, (rows, LANES), 1) < HEAD_DIM
    ones = jnp.ones((8, LANES), bf16)
    for block in range(blocks):
        own = slice(block * rows, (block + 1) * rows)
        span = slice(block * rows, block * rows + keys)
        query = q_ref[own, :] * (HEAD_DIM ** -0.5)
        grad = do_ref[own, :]
        key = k_ref[span, :]
        value = v_ref[span, :]
        product = grad.astype(f32) * out_ref[own, :].astype(f32)
        heads_dq = []
        for half in range(2):
            mine = low if half == 0 else ~low
            query_h = jnp.where(mine, query, jnp.zeros_like(query))
            grad_h = jnp.where(mine, grad, jnp.zeros_like(grad))
            product_h = jnp.where(mine, product, 0.0)
            coarse = product_h.astype(bf16)
            fine = (product_h - coarse.astype(f32)).astype(bf16)
            delta = (dot_on(ones, coarse, 1, 1) + dot_on(ones, fine, 1, 1))[0:1, :]
            scores = dot_on(key, query_h, 1, 1) + bias_ref[block]
            probs = jnp.exp(scores - lse_ref[pl.ds(2 * pair + half, 1), own])
            d_probs = dot_on(value, grad_h, 1, 1)
            d_scores = (probs * (d_probs - delta)).astype(bf16)
            dv_sum[span, :] += dot_on(probs.astype(bf16), grad_h, 1, 0)
            dk_sum[span, :] += dot_on(d_scores, query_h, 1, 0)
            heads_dq.append(dot_on(d_scores, key, 0, 0))
        dq_ref[own, :] = (
            jnp.where(low, heads_dq[0], heads_dq[1]) * (HEAD_DIM ** -0.5)
        ).astype(bf16)
    dk_ref[...] = dk_sum[...].astype(bf16)
    dv_ref[...] = dv_sum[...].astype(bf16)


def attention_backward(qkv, kv_earlier, grad_att, attended, lse, seg_query, seg_key, after):
    length = qkv.shape[0]
    width = qkv.shape[1] // 3
    pairs = width // LANES
    rows = min(256, length)
    keys = rows + WINDOW
    blocks = length // rows
    span = WINDOW + length

    def column(count, offset):
        return pl.BlockSpec((count, LANES), lambda p: (0, offset + p))

    return pl.pallas_call(
        functools.partial(attention_backward_kernel, rows, keys, blocks),
        grid=(pairs,),
        in_specs=[
            column(length, 0),
            column(length, pairs),
            column(length, 2 * pairs),
            column(WINDOW, 0),
            column(WINDOW, pairs),
            column(length, 0),
            column(length, 0),
            pl.BlockSpec((16, length), lambda p: (0, 0)),
            pl.BlockSpec((1, length), lambda p: (0, 0)),
            pl.BlockSpec((span, 1), lambda p: (0, 0)),
        ]
        + [ANY_SPEC] * len(after),
        out_specs=[column(length, 0), column(span, 0), column(span, 0)],
        out_shape=[
            jax.ShapeDtypeStruct((length, width), bf16),
            jax.ShapeDtypeStruct((span, width), bf16),
            jax.ShapeDtypeStruct((span, width), bf16),
        ],
        scratch_shapes=[
            pltpu.VMEM((blocks, keys, rows), f32),
            pltpu.VMEM((span, LANES), bf16),
            pltpu.VMEM((span, LANES), bf16),
            pltpu.VMEM((span, LANES), f32),
            pltpu.VMEM((span, LANES), f32),
        ],
        compiler_params=pltpu.CompilerParams(vmem_limit_bytes=48 * MIB),
        cost_estimate=cost(48),
        name="attention_backward",
    )(
        qkv, qkv, qkv, kv_earlier, kv_earlier, grad_att, attended, lse, seg_query, seg_key, *after
    )


def sigmoid(values):
    return 1.0 / (1.0 + jnp.exp(-values))


def gathered(rows_ref, block_refs):
    count = block_refs[0].shape[0]
    width = rows_ref.shape[1]
    for index, block_ref in enumerate(block_refs):
        rows_ref[index * count : (index + 1) * count, :] = block_ref[:, :width]


def scattered(block_refs, rows, which=0):
    count = block_refs[0].shape[1]
    for index, block_ref in enumerate(block_refs):
        block_ref[which] = rows[index * count : (index + 1) * count, :].astype(bf16)


def experts_forward_kernel(groups, *refs):
    block_refs, (gate_w_ref, up_w_ref, down_w_ref) = refs[:groups], refs[groups : groups + 3]
    out_refs, (gate_ref, up_ref, rows_ref) = refs[-groups - 3 : -3], refs[-3:]
    gathered(rows_ref, block_refs)
    rows_in = rows_ref[...]
    gate_pre = dot_on(rows_in, gate_w_ref[0], 1, 0)
    up_pre = dot_on(rows_in, up_w_ref[0], 1, 0)
    activated = (gate_pre * sigmoid(gate_pre) * up_pre).astype(bf16)
    gate_ref[0] = gate_pre.astype(bf16)
    up_ref[0] = up_pre.astype(bf16)
    scattered(out_refs, dot_on(activated, down_w_ref[0], 1, 0))


def experts_forward(blocks, gate_up_w, down_w, after):
    groups = len(blocks)
    count = down_w.shape[0]
    width, hidden = gate_up_w.shape[1:]
    part = blocks[0].shape[0] // count
    rows = groups * part
    block_spec = pl.BlockSpec((part, width), lambda j: (j, 0))
    hidden_spec = pl.BlockSpec((1, rows, hidden), lambda j: (j, 0, 0))
    hidden_shape = jax.ShapeDtypeStruct((count, rows, hidden), bf16)
    *produced, gate_pre, up_pre = pl.pallas_call(
        functools.partial(experts_forward_kernel, groups),
        grid=(count,),
        in_specs=[block_spec] * groups
        + [
            pl.BlockSpec((1, width, hidden), lambda j: (j, 0, 0)),
            pl.BlockSpec((1, width, hidden), lambda j: (count + j, 0, 0)),
            pl.BlockSpec((1, hidden, width), lambda j: (j, 0, 0)),
        ]
        + [ANY_SPEC] * len(after),
        out_specs=[pl.BlockSpec((1, part, width), lambda j: (0, j, 0))] * groups
        + [hidden_spec, hidden_spec],
        out_shape=[jax.ShapeDtypeStruct((1, count * part, width), bf16)] * groups
        + [hidden_shape, hidden_shape],
        scratch_shapes=[pltpu.VMEM((rows, width), bf16)],
        compiler_params=pltpu.CompilerParams(vmem_limit_bytes=48 * MIB),
        cost_estimate=cost(26),
        name="experts_forward",
    )(*blocks, gate_up_w, gate_up_w, down_w, *after)
    return produced, gate_pre, up_pre


def experts_backward_kernel(groups, chunks, whole, has_sums, *refs):
    block_refs, d_refs, given = refs[:groups], refs[groups : 2 * groups], refs[2 * groups :]
    gate_w_ref, up_w_ref, down_w_ref = given[:3]
    if whole:
        share_refs, given = given[3 : 3 + groups], given[3 + groups :]
        *refs, produced_ref = refs
    else:
        (gate_ref, up_ref), given = given[3:5], given[5:]
    out_refs = refs[-5 - groups : -5]
    gate_up_grad_ref, down_grad_ref, total_ref, rows_ref, d_ref = refs[-5:]
    chunk = pl.program_id(1)

    @pl.when(chunk == 0)
    def _():
        gathered(rows_ref, block_refs)
        if whole:
            count = d_refs[0].shape[0]
            for index in range(groups):
                share = share_refs[index][...].astype(f32)
                share = share[:, 0:1] + share[:, 1:2]
                d_ref[index * count : (index + 1) * count, :] = (
                    d_refs[index][...].astype(f32) * share
                ).astype(bf16)
        else:
            gathered(d_ref, d_refs)

    rows_in = rows_ref[...]
    d_out = d_ref[...]
    if whole:
        gate_pre = dot_on(rows_in, gate_w_ref[0], 1, 0)
        up_pre = dot_on(rows_in, up_w_ref[0], 1, 0)
    else:
        gate_pre = gate_ref[0].astype(f32)
        up_pre = up_ref[0].astype(f32)
    share = sigmoid(gate_pre)
    swish = gate_pre * share
    activated = (swish * up_pre).astype(bf16)
    d_act = dot_on(d_out, down_w_ref[0], 1, 1)
    d_gate = (d_act * up_pre * (share * (1.0 + gate_pre * (1.0 - share)))).astype(bf16)
    d_up = (d_act * swish).astype(bf16)
    part = dot_on(d_gate, gate_w_ref[0], 1, 1) + dot_on(d_up, up_w_ref[0], 1, 1)
    gate_grad = dot_on(rows_in, d_gate, 0, 0)
    up_grad = dot_on(rows_in, d_up, 0, 0)
    down_grad = dot_on(activated, d_out, 0, 0)
    if has_sums:
        gate_up_sum_ref, down_sum_ref = given[:2]
        gate_grad += gate_up_sum_ref[0, 0].astype(f32)
        up_grad += gate_up_sum_ref[1, 0].astype(f32)
        down_grad += down_sum_ref[0].astype(f32)
    gate_up_grad_ref[0, 0] = gate_grad.astype(bf16)
    gate_up_grad_ref[1, 0] = up_grad.astype(bf16)
    down_grad_ref[0] = down_grad.astype(bf16)
    sums = [(total_ref, part)]
    if whole:
        sums.append((produced_ref, dot_on(activated, down_w_ref[0], 1, 0)))

    @pl.when(chunk == 0)
    def _():
        for sum_ref, value in sums:
            sum_ref[...] = value

    @pl.when(chunk > 0)
    def _():
        for sum_ref, value in sums:
            sum_ref[...] += value

    @pl.when(chunk == chunks - 1)
    def _():
        scattered(out_refs, total_ref[...], len(sums) - 1)
        if whole:
            scattered(out_refs, produced_ref[...])


def experts_backward(blocks, d_blocks, pre, gate_up_w, down_w, sums, after):
    groups = len(blocks)
    count, hidden, width = down_w.shape
    part = blocks[0].shape[0] // count
    rows = groups * part
    whole = pre is None
    chunk = min(512, hidden)
    chunks = hidden // chunk
    block_spec = pl.BlockSpec((part, width), lambda j, f: (j, 0))
    hidden_spec = pl.BlockSpec((1, rows, chunk), lambda j, f: (j, 0, f))
    wide_spec = pl.BlockSpec((1, width, chunk), lambda j, f: (j, 0, f))
    up_spec = pl.BlockSpec((1, width, chunk), lambda j, f: (count + j, 0, f))
    tall_spec = pl.BlockSpec((1, chunk, width), lambda j, f: (j, f, 0))
    both_spec = pl.BlockSpec((2, 1, width, chunk), lambda j, f: (0, j, 0, f))
    operands = [*blocks, *d_blocks, gate_up_w, gate_up_w, down_w]
    specs = [block_spec] * (2 * groups) + [wide_spec, up_spec, tall_spec]
    if whole:
        operands.extend(blocks)
        specs += [pl.BlockSpec((part, LANES), lambda j, f: (j, width // LANES))] * groups
    else:
        operands.extend(pre)
        specs += [hidden_spec, hidden_spec]
    if sums is not None:
        operands.extend(sums)
        specs.extend([both_spec, tall_spec])
    outs = 2 if whole else 1
    *out, gate_up_grad, down_grad = pl.pallas_call(
        functools.partial(experts_backward_kernel, groups, chunks, whole, sums is not None),
        grid=(count, chunks),
        in_specs=specs + [ANY_SPEC] * len(after),
        out_specs=[pl.BlockSpec((outs, part, width), lambda j, f: (0, j, 0))] * groups
        + [both_spec, tall_spec],
        out_shape=[jax.ShapeDtypeStruct((outs, count * part, width), bf16)] * groups
        + [
            jax.ShapeDtypeStruct((2, count, width, hidden), bf16),
            jax.ShapeDtypeStruct((count, hidden, width), bf16),
        ],
        scratch_shapes=[
            pltpu.VMEM((rows, width), f32),
            pltpu.VMEM((rows, width), bf16),
            pltpu.VMEM((rows, width), bf16),
        ]
        + ([pltpu.VMEM((rows, width), f32)] if whole else []),
        compiler_params=pltpu.CompilerParams(vmem_limit_bytes=58 * MIB),
        cost_estimate=cost(75 if whole else 52),
        name="experts_whole" if whole else "experts_backward",
    )(*operands, *after)
    return out, (gate_up_grad, down_grad)


def passed_along(block, axis, distance):
    devices = range(lax.axis_size(axis))
    route = [(i - distance, i) for i in devices if i - distance in devices]
    return lax.ppermute(block, axis, route)


def earlier_rows(block, hop_count):
    pieces = [passed_along(block, "context", hop) for hop in range(hop_count, 0, -1)]
    missing = WINDOW - hop_count * block.shape[-2]
    if missing > 0:
        shape = block.shape[:-2] + (missing, block.shape[-1])
        pieces = [jnp.zeros(shape, block.dtype)] + pieces
    rows = pieces[0] if len(pieces) == 1 else jnp.concatenate(pieces, axis=-2)
    return rows[..., rows.shape[-2] - WINDOW :, :]


def returned_rows(block, length, hop_count):
    total = None
    for hop in range(1, hop_count + 1):
        first = WINDOW - hop * length
        part = block[max(first, 0) : first + length]
        if first < 0:
            part = jnp.concatenate([jnp.zeros((-first, block.shape[1]), block.dtype), part])
        part = passed_along(part, "context", -hop).astype(f32)
        total = part if total is None else total + part
    return total


def exchange(blocks, direction):
    groups = lax.axis_size("expert")
    out = []
    for d, block in enumerate(blocks):
        step = d * direction
        route = [(i, (i + step) % groups) for i in range(groups)]
        out.append(block if d == 0 else lax.ppermute(block, "expert", route))
    return out


GATE, OF_NORMED, NORMED_SHARE, VECTOR_SHARE, MIX, SCALE, CHOSEN = 0, 2, 4, 5, 7, 9, 10
GAINS_LANE = 2 * ROUTED + 8
VECTOR_ROW, ATTN_GAIN_ROW, MOE_GAIN_ROW = 0, 2, 3


def inverse_rms(rows):
    return lax.rsqrt(jnp.mean(rows * rows, axis=-1, keepdims=True) + norm_eps)


def lane_iota(rows):
    return lax.broadcasted_iota(jnp.int32, (rows, LANES), 1)


def placed_on_lanes(rows, values):
    lane = lane_iota(rows)
    total = jnp.zeros((rows, LANES), f32)
    for index, value in values.items():
        total = jnp.where(lane == index, value, total)
    return total


def routing_kernel(routes_ref, base_ref, columns_ref, rows_ref):
    length = routes_ref.shape[1]
    lane = lane_iota(length)
    onehots = [(lane == routes_ref[0, :, k : k + 1]).astype(f32) for k in range(TOP)]
    counts = (onehots[0] + onehots[1]).astype(bf16)
    earlier = lax.broadcasted_iota(jnp.int32, (length, length), 0) > lax.broadcasted_iota(
        jnp.int32, (length, length), 1
    )
    rank = dot_on(jnp.where(earlier, 1.0, 0.0).astype(bf16), counts, 1, 0)
    place = base_ref[...] + jnp.where(lane < EXPERTS, rank, 0.0)
    slots = placed_on_lanes(
        length,
        {k: jnp.sum(onehots[k] * place, axis=1, keepdims=True) for k in range(TOP)},
    )
    columns_ref[0] = slots.astype(jnp.int32)
    rows_ref[0] = jnp.round(rows_of(slots, range(TOP))).astype(jnp.int32)


def routing_slots(routes, groups, capacity):
    count, length, _ = routes.shape
    per_dev = EXPERTS // groups
    expert = jnp.arange(LANES)
    place = (expert // per_dev - lax.axis_index("expert")) % groups
    base = (place * per_dev + expert % per_dev) * capacity
    base = jnp.where(expert < EXPERTS, base, -1).astype(f32)[None, :]
    return pl.pallas_call(
        routing_kernel,
        grid=(count,),
        in_specs=[
            pl.BlockSpec((1, length, TOP), lambda m: (m, 0, 0)),
            pl.BlockSpec((1, LANES), lambda m: (0, 0)),
        ],
        out_specs=[
            pl.BlockSpec((1, length, LANES), lambda m: (m, 0, 0)),
            pl.BlockSpec((1, 8, length), lambda m: (m, 0, 0)),
        ],
        out_shape=[
            jax.ShapeDtypeStruct((count, length, LANES), jnp.int32),
            jax.ShapeDtypeStruct((count, 8, length), jnp.int32),
        ],
        compiler_params=pltpu.CompilerParams(vmem_limit_bytes=32 * MIB),
        cost_estimate=cost(4),
        name="routing",
    )(routes, base)


def dispatch_kernel(mode, per_group, groups, rows_ref, slots_ref, gates_ref, *rest):
    out_refs = rest[-groups:]
    count, length = out_refs[0].shape[0], rows_ref.shape[0]
    width = rows_ref.shape[1]
    rows = rows_ref[...].astype(bf16)
    for group, out_ref in enumerate(out_refs):
        first = group * per_group + pl.program_id(0) * count
        slot = first + lax.broadcasted_iota(jnp.int32, (count, length), 0)
        hits = [slot == slots_ref[k : k + 1, :] for k in range(TOP)]
        table = jnp.where(hits[0] | hits[1], 1.0, 0.0).astype(bf16)
        found = dot_on(table, rows, 1, 0)
        if mode == "plain":
            out_ref[...] = found.astype(bf16)
            continue
        gate = jnp.sum(
            jnp.where(hits[0], gates_ref[0:1, :], 0.0)
            + jnp.where(hits[1], gates_ref[1:2, :], 0.0),
            axis=1,
            keepdims=True,
        )
        if mode == "scaled":
            out_ref[...] = (found * gate).astype(bf16)
            continue
        out_ref[:, :width] = found.astype(bf16)
        coarse = gate.astype(bf16).astype(f32)
        out_ref[:, width:] = placed_on_lanes(count, {0: coarse, 1: gate - coarse}).astype(bf16)


def dispatch(rows, slot_rows, gate_rows, mode, slots, groups, after=()):
    length, width = rows.shape
    per_group = slots // groups
    count = min(256, per_group)
    out_width = width + LANES if mode == "with gate" else width
    return pl.pallas_call(
        functools.partial(dispatch_kernel, mode, per_group, groups),
        grid=(per_group // count,),
        in_specs=[
            pl.BlockSpec((length, width), lambda s: (0, 0)),
            pl.BlockSpec((8, length), lambda s: (0, 0)),
            pl.BlockSpec((8, length), lambda s: (0, 0)),
        ]
        + [ANY_SPEC] * len(after),
        out_specs=[pl.BlockSpec((count, out_width), lambda s: (s, 0))] * groups,
        out_shape=[jax.ShapeDtypeStruct((per_group, out_width), bf16)] * groups,
        compiler_params=pltpu.CompilerParams(vmem_limit_bytes=32 * MIB),
        cost_estimate=cost(6),
        name="dispatch",
    )(rows, slot_rows, gate_rows, *after)


def attention_output_kernel(
    hidden_ref, attended_ref, out_w_ref, small_w_ref, vectors_ref, prior_ref, residual_ref,
    routes_ref, mid_ref, low_ref, logits_ref, scalars_ref, gates_ref,
):
    rows = hidden_ref.shape[0]
    mid = hidden_ref[...] + dot_on(attended_ref[...], out_w_ref[...], 1, 0)
    mid_ref[...] = mid
    scale = inverse_rms(mid)
    low = (mid * scale * vectors_ref[MOE_GAIN_ROW : MOE_GAIN_ROW + 1, :]).astype(bf16)
    low_ref[...] = low
    logits = dot_on(low, small_w_ref[...], 1, 0) + jnp.dot(
        prior_ref[...], residual_ref[...], precision=highest
    )
    logits_ref[...] = logits
    lane = lane_iota(rows)
    onehots = [lane == routes_ref[:, k : k + 1] for k in range(TOP)]

    def lane_sum(values):
        return jnp.sum(values, axis=1, keepdims=True)

    difference = lane_sum(jnp.where(onehots[0], logits, jnp.where(onehots[1], -logits, 0.0)))
    gates = (sigmoid(difference), sigmoid(-difference))
    chosen = [
        [jnp.where(routes_ref[:, k : k + 1] == EXPERTS + 2 + j, 1.0, 0.0) for j in range(2)]
        for k in range(TOP)
    ]
    alphas = []
    for j in range(2):
        at = ROUTED + 2 * j
        gap = lane_sum(jnp.where(lane == at, logits, jnp.where(lane == at + 1, -logits, 0.0)))
        alphas.append((sigmoid(gap), sigmoid(-gap)))
    of_normed = [
        jnp.where(routes_ref[:, k : k + 1] == EXPERTS + 1, 1.0, 0.0)
        + chosen[k][0] * alphas[0][0]
        + chosen[k][1] * alphas[1][0]
        for k in range(TOP)
    ]
    vector_gate = [gates[0] * chosen[0][j] + gates[1] * chosen[1][j] for j in range(2)]
    values = {
        GATE: gates[0], GATE + 1: gates[1],
        OF_NORMED: of_normed[0], OF_NORMED + 1: of_normed[1],
        NORMED_SHARE: gates[0] * of_normed[0] + gates[1] * of_normed[1],
        SCALE: scale,
    }
    for j in range(2):
        values[VECTOR_SHARE + j] = vector_gate[j] * alphas[j][1]
        values[MIX + j] = vector_gate[j] * alphas[j][0] * alphas[j][1]
        for k in range(TOP):
            values[CHOSEN + 2 * k + j] = chosen[k][j] * alphas[j][1]
    scalars = placed_on_lanes(rows, values)
    scalars_ref[...] = scalars
    gates_ref[...] = rows_of(scalars, (GATE, GATE + 1))


def attention_output(hidden, attended, weights, prior, routes):
    length, width = hidden.shape
    rows = min(256, length)
    wide = pl.BlockSpec((rows, width), lambda t: (t, 0))
    lanes = pl.BlockSpec((rows, LANES), lambda t: (t, 0))
    return pl.pallas_call(
        attention_output_kernel,
        grid=(length // rows,),
        in_specs=[
            wide,
            wide,
            pl.BlockSpec((width, width), lambda t: (0, 3)),
            pl.BlockSpec((width, LANES), lambda t: (0, 4 * width // LANES)),
            pl.BlockSpec((8, width), lambda t: (0, 0)),
            lanes,
            pl.BlockSpec((LANES, LANES), lambda t: (0, 0)),
            pl.BlockSpec((rows, TOP), lambda t: (t, 0)),
        ],
        out_specs=[wide, wide, lanes, lanes, pl.BlockSpec((8, rows), lambda t: (0, t))],
        out_shape=[
            jax.ShapeDtypeStruct((length, width), f32),
            jax.ShapeDtypeStruct((length, width), bf16),
            jax.ShapeDtypeStruct((length, LANES), f32),
            jax.ShapeDtypeStruct((length, LANES), f32),
            jax.ShapeDtypeStruct((8, length), f32),
        ],
        compiler_params=pltpu.CompilerParams(vmem_limit_bytes=24 * MIB),
        cost_estimate=cost(8),
        name="attention_output",
    )(
        hidden, attended, weights["dense"], weights["dense"], weights["vectors"], prior,
        weights["residual"], routes,
    )


def selected(columns, block_refs, which):
    per_group = block_refs[0].shape[0]
    total = None
    for group, block_ref in enumerate(block_refs):
        slot = group * per_group + lax.broadcasted_iota(
            jnp.int32, (columns.shape[0], per_group), 1
        )
        hit = slot == columns[:, which[0] : which[0] + 1]
        for k in which[1:]:
            hit = hit | (slot == columns[:, k : k + 1])
        part = dot_on(jnp.where(hit, 1.0, 0.0).astype(bf16), block_ref[...], 1, 0)
        total = part if total is None else total + part
    return total


def combine_kernel(last, groups, waits, *refs):
    back_refs, (columns_ref, mid_ref, scalars_ref, vectors_ref, next_ref) = (
        refs[:groups], refs[groups : groups + 5],
    )
    out_refs = refs[groups + 5 + waits :]
    columns, scalars = columns_ref[...], scalars_ref[...]
    mid = mid_ref[...]
    normed = mid * scalars[:, SCALE : SCALE + 1] * vectors_ref[MOE_GAIN_ROW : MOE_GAIN_ROW + 1, :]
    total = mid + scalars[:, NORMED_SHARE : NORMED_SHARE + 1] * normed
    for j in range(2):
        row = vectors_ref[VECTOR_ROW + j : VECTOR_ROW + j + 1, :]
        total += scalars[:, VECTOR_SHARE + j : VECTOR_SHARE + j + 1] * row
    for k in range(TOP):
        branch = selected(columns, back_refs, (k,))
        out_refs[k][...] = branch.astype(bf16)
        total += scalars[:, GATE + k : GATE + k + 1] * branch
    if last:
        out_refs[TOP][...] = total.astype(bf16)
    else:
        out_refs[TOP][...] = total
        out_refs[TOP + 1][...] = (
            total * inverse_rms(total) * next_ref[ATTN_GAIN_ROW : ATTN_GAIN_ROW + 1, :]
        ).astype(bf16)


def combine(back, columns, mid, scalars, vectors, next_vectors, after):
    last = next_vectors is None
    length, width = mid.shape
    back, which = back
    groups, per_group = len(back), back[0].shape[1]
    rows = min(256, length)
    wide = pl.BlockSpec((rows, width), lambda t: (t, 0))
    lanes = pl.BlockSpec((rows, LANES), lambda t: (t, 0))
    vector_spec = pl.BlockSpec((8, width), lambda t: (0, 0))
    low = jax.ShapeDtypeStruct((length, width), bf16)
    return pl.pallas_call(
        functools.partial(combine_kernel, last, groups, len(after)),
        grid=(length // rows,),
        in_specs=[pl.BlockSpec((None, per_group, width), lambda t: (which, 0, 0))] * groups
        + [lanes, wide, lanes, vector_spec, vector_spec]
        + [ANY_SPEC] * len(after),
        out_specs=[wide] * (TOP + 1 if last else TOP + 2),
        out_shape=[low, low, low]
        if last
        else [low, low, jax.ShapeDtypeStruct((length, width), f32), low],
        compiler_params=pltpu.CompilerParams(vmem_limit_bytes=24 * MIB),
        cost_estimate=cost(8),
        name="combine",
    )(*back, columns, mid, scalars, vectors, vectors if last else next_vectors, *after)


def token_backward_kernel(
    has_prior, groups, *refs
):
    back_refs, rest = refs[:groups], refs[groups:]
    (
        columns_ref, grad_ref, mid_ref, scalars_ref, branch0_ref, branch1_ref, low_ref, prior_ref,
        attended_ref, routes_ref, out_w_ref, small_w_ref, vectors_ref, residual_ref,
    ) = rest[:14]
    rest = rest[14:]
    d_mid_ref, d_att_ref, d_prior_ref, g_out_ref, g_small_ref, g_residual_ref, g_gain_ref = (
        rest[-7:]
    )
    step = pl.program_id(0)
    rows = mid_ref.shape[0]
    columns, scalars = columns_ref[...], scalars_ref[...]
    grad = grad_ref[...].astype(f32)
    mid = mid_ref[...]
    gain = vectors_ref[MOE_GAIN_ROW : MOE_GAIN_ROW + 1, :]
    scale = scalars[:, SCALE : SCALE + 1]
    unit = mid * scale
    lane = lane_iota(rows)

    def scalar(index):
        return scalars[:, index : index + 1]

    def row_sum(values):
        return jnp.sum(values, axis=1, keepdims=True)

    along = row_sum(grad * (unit * gain))
    along_vector = [
        row_sum(grad * vectors_ref[VECTOR_ROW + j : VECTOR_ROW + j + 1, :]) for j in range(2)
    ]
    d_gate = []
    for k, branch_ref in enumerate((branch0_ref, branch1_ref)):
        value = row_sum(grad * branch_ref[...].astype(f32)) + scalar(OF_NORMED + k) * along
        for j in range(2):
            value += scalar(CHOSEN + 2 * k + j) * along_vector[j]
        d_gate.append(value)
    d_choice = scalar(GATE) * scalar(GATE + 1) * (d_gate[0] - d_gate[1])
    d_small = jnp.where(
        lane == routes_ref[:, 0:1], d_choice, jnp.where(lane == routes_ref[:, 1:2], -d_choice, 0.0)
    )
    if has_prior:
        d_small += jnp.where(lane < ROUTED, rest[0][...], 0.0)
    d_logits = d_small
    for j in range(2):
        value = scalar(MIX + j) * (along - along_vector[j])
        at = ROUTED + 2 * j
        d_small = jnp.where(lane == at, value, jnp.where(lane == at + 1, -value, d_small))
    d_small_low = d_small.astype(bf16)
    d_prior_ref[...] = lax.dot_general(
        d_logits, residual_ref[...], (((1,), (1,)), ((), ())), precision=highest
    )
    vector_shares = placed_on_lanes(
        rows, {ROUTED + 4 + j: scalar(VECTOR_SHARE + j) for j in range(2)}
    ).astype(bf16)
    g_small = dot_on(low_ref[...], d_small_low, 0, 0) + dot_on(
        grad.astype(bf16), vector_shares, 0, 0
    )
    g_residual = lax.dot_general(
        prior_ref[...], d_logits, (((0,), (0,)), ((), ())), precision=highest
    )
    d_normed = (
        selected(columns, back_refs, (0, 1))
        + scalar(NORMED_SHARE) * grad
        + dot_on(d_small_low, small_w_ref[...], 1, 1)
    )
    g_gain = jnp.sum(d_normed * unit, axis=0, keepdims=True)
    d_unit = d_normed * gain
    d_mid = grad + (d_unit - unit * jnp.mean(d_unit * unit, axis=-1, keepdims=True)) * scale
    d_mid_ref[...] = d_mid
    d_mid_low = d_mid.astype(bf16)
    d_att_ref[...] = dot_on(d_mid_low, out_w_ref[...], 1, 1).astype(bf16)
    g_out = dot_on(attended_ref[...], d_mid_low, 0, 0)

    @pl.when(step == 0)
    def _():
        g_out_ref[...] = g_out
        g_small_ref[...] = g_small
        g_residual_ref[...] = g_residual
        g_gain_ref[...] = jnp.broadcast_to(g_gain, g_gain_ref.shape)

    @pl.when(step > 0)
    def _():
        g_out_ref[...] += g_out
        g_small_ref[...] += g_small
        g_residual_ref[...] += g_residual
        g_gain_ref[...] += jnp.broadcast_to(g_gain, g_gain_ref.shape)


def token_backward(back, kept, grad, weights, columns, routes, d_prior, after):
    length, width = grad.shape
    back, which = back
    groups, per_group = len(back), back[0].shape[1]
    rows = min(256, length)
    wide = pl.BlockSpec((rows, width), lambda t: (t, 0))
    lanes = pl.BlockSpec((rows, LANES), lambda t: (t, 0))

    def fixed(*shape, at=0):
        return pl.BlockSpec(shape, lambda t: (0, at))

    operands = [
        *back, columns, grad, kept["mid"], kept["scalars"], kept["branch"][0], kept["branch"][1],
        kept["low"], kept["prior"], kept["attended"], routes, weights["dense"], weights["dense"],
        weights["vectors"], weights["residual"],
    ]
    specs = [
        *[pl.BlockSpec((None, per_group, width), lambda t: (which, 0, 0))] * groups,
        lanes, wide, wide, lanes, wide, wide, wide, lanes, wide,
        pl.BlockSpec((rows, TOP), lambda t: (t, 0)), fixed(width, width, at=3),
        fixed(width, LANES, at=4 * width // LANES), fixed(8, width), fixed(LANES, LANES),
    ]
    if d_prior is not None:
        operands.append(d_prior)
        specs.append(lanes)
    return pl.pallas_call(
        functools.partial(token_backward_kernel, d_prior is not None, groups),
        grid=(length // rows,),
        in_specs=specs + [ANY_SPEC] * len(after),
        out_specs=[
            wide, wide, lanes, fixed(width, width), fixed(width, LANES), fixed(LANES, LANES),
            fixed(8, width),
        ],
        out_shape=[
            jax.ShapeDtypeStruct((length, width), f32),
            jax.ShapeDtypeStruct((length, width), bf16),
            jax.ShapeDtypeStruct((length, LANES), f32),
            jax.ShapeDtypeStruct((width, width), f32),
            jax.ShapeDtypeStruct((width, LANES), f32),
            jax.ShapeDtypeStruct((LANES, LANES), f32),
            jax.ShapeDtypeStruct((8, width), f32),
        ],
        compiler_params=pltpu.CompilerParams(vmem_limit_bytes=48 * MIB),
        cost_estimate=cost(25),
        name="token_backward",
    )(*operands, *after)


def finish_backward_kernel(
    has_later, hidden_ref, d_mid_ref, d_attn_ref, vectors_ref, *rest
):
    out_ref, g_gain_ref = rest[-2:]
    hidden = hidden_ref[...]
    d_attn = d_attn_ref[...]
    if has_later:
        d_attn += rest[0][...].astype(f32)
    scale = inverse_rms(hidden)
    unit = hidden * scale
    g_gain = jnp.broadcast_to(jnp.sum(d_attn * unit, axis=0, keepdims=True), g_gain_ref.shape)
    d_unit = d_attn * vectors_ref[ATTN_GAIN_ROW : ATTN_GAIN_ROW + 1, :]
    out_ref[...] = (
        d_mid_ref[...] + (d_unit - unit * jnp.mean(d_unit * unit, axis=-1, keepdims=True)) * scale
    ).astype(out_ref.dtype)

    @pl.when(pl.program_id(0) == 0)
    def _():
        g_gain_ref[...] = g_gain

    @pl.when(pl.program_id(0) > 0)
    def _():
        g_gain_ref[...] += g_gain


def finish_backward(hidden, d_mid, d_attn, vectors, later, out_type, after):
    length, width = hidden.shape
    rows = min(256, length)
    wide = pl.BlockSpec((rows, width), lambda t: (t, 0))
    vector_spec = pl.BlockSpec((8, width), lambda t: (0, 0))
    extra = [] if later is None else [later]
    return pl.pallas_call(
        functools.partial(finish_backward_kernel, later is not None),
        grid=(length // rows,),
        in_specs=[wide, wide, wide, vector_spec] + [wide] * len(extra) + [ANY_SPEC] * len(after),
        out_specs=[wide, vector_spec],
        out_shape=[
            jax.ShapeDtypeStruct((length, width), out_type),
            jax.ShapeDtypeStruct((8, width), f32),
        ],
        compiler_params=pltpu.CompilerParams(vmem_limit_bytes=24 * MIB),
        cost_estimate=cost(6),
        name="finish_backward",
    )(hidden, d_mid, d_attn, vectors, *extra, *after)


def fetch_layer(layer, local):
    width = local["w_query"].shape[2]
    shard = local["w_query"].shape[1]
    const_w = jnp.transpose(local["w_const"][layer], (1, 0, 2)).reshape(shard, 4)
    small = jnp.concatenate(
        [
            local["w_router"][layer], const_w, local["const_vec"][layer].T,
            local["norm_attn"][layer][:, None], local["norm_moe"][layer][:, None],
            jnp.zeros((shard, LANES - ROUTED - 8), bf16),
        ],
        axis=1,
    )
    packed = jnp.concatenate(
        [local["w_query"][layer], local["w_key"][layer], local["w_value"][layer],
         local["w_out"][layer], small],
        axis=1,
    )
    dense = lax.all_gather(packed, SHARDED, axis=0, tiled=True)
    gate_up = jnp.concatenate([local["w_gate"][layer], local["w_up"][layer]], axis=0)
    gate_up = lax.all_gather(gate_up, SHARDED, axis=1, tiled=True)
    down = lax.all_gather(local["w_down"][layer], SHARDED, axis=1, tiled=True)
    at = 4 * width + ROUTED + 4
    vectors = dense[:, at : at + 8].T.astype(f32)
    residual = local["w_res"][layer].astype(f32)
    blank = LANES - ROUTED
    return dict(
        dense=dense, vectors=vectors, gate_up=gate_up, down=down,
        residual=jnp.pad(residual, ((0, blank), (0, blank))),
    )


def per_device(
    hidden_in, segments, routes, prev_logits, out_grad, norm_attn, w_query, w_key, w_value,
    w_out, norm_moe, w_router, w_res, w_const, const_vec, w_gate, w_up, w_down,
):
    local = dict(
        norm_attn=norm_attn, w_query=w_query, w_key=w_key, w_value=w_value, w_out=w_out,
        norm_moe=norm_moe, w_router=w_router, w_res=w_res, w_const=w_const,
        const_vec=const_vec, w_gate=w_gate, w_up=w_up, w_down=w_down,
    )
    micro_count, _, length, width = hidden_in.shape
    micros = range(micro_count)
    layers = norm_attn.shape[0]
    groups = lax.axis_size("expert")
    hop_count = min((WINDOW + length - 2) // length, lax.axis_size("context") - 1)
    capacity = length // 4
    slots = EXPERTS * capacity
    block_start = lax.axis_index("context") * length
    routes = routes[:, 0]
    columns, slot_rows = routing_slots(routes, groups, capacity)
    blank_gates = jnp.zeros((8, length), f32)

    def normed(hidden, gain):
        return (hidden * inverse_rms(hidden) * gain).astype(bf16)

    last_arrived = []

    def in_turn(blocks, micro):
        others = held(list(blocks[1:]), tuple(last_arrived[1:]) if micro > 0 else ())
        last_arrived[:] = exchange(list(blocks[:1]) + others, -1)
        return list(last_arrived)

    early = []

    def send_early(micro, after):
        sent = dispatch(
            out_grad[micro, 0], slot_rows[micro], blank_gates, "plain", slots, groups, after
        )
        early.append(exchange(sent, 1))

    send_early(0, ())
    fetched = [fetch_layer(layer, local) for layer in range(layers)]
    segs, state = [], []
    for micro in micros:
        whole = segments[micro, 0]
        padded = jnp.concatenate([jnp.full((WINDOW,), -1, jnp.int32), whole])
        query = lax.dynamic_slice_in_dim(whole, block_start, length, 0)
        key = lax.dynamic_slice_in_dim(padded, block_start, WINDOW + length, 0)
        segs.append((query, key))
        hidden = hidden_in[micro, 0].astype(f32)
        gain = fetched[0]["vectors"][ATTN_GAIN_ROW : ATTN_GAIN_ROW + 1]
        prior = jnp.pad(prev_logits[micro, 0], ((0, 0), (0, LANES - ROUTED)))
        state.append(
            (
                hidden, normed(hidden, gain),
                None if micro > 0 else earlier_rows(hidden_in[micro, 0], hop_count), prior,
            )
        )

    saved = [[None] * layers for _ in micros]
    expert_sums = [None] * layers

    def attention_part(layer, micro, after, after_output):
        weights = fetched[layer]
        hidden, attn_in, attn_earlier, prior = state[micro]
        if layer == 0:
            if micro > 0:
                (block,) = held([hidden_in[micro, 0]], (saved[micro - 1][0]["attended"],))
                attn_earlier = earlier_rows(block, hop_count)
            attn_earlier = normed(attn_earlier.astype(f32), weights["vectors"][ATTN_GAIN_ROW][None])
        qkv = dot_on(attn_in, weights["dense"][:, : 3 * width], 1, 0).astype(bf16)
        kv_earlier = dot_on(attn_earlier, weights["dense"][:, width : 3 * width], 1, 0).astype(bf16)
        query, key = segs[micro]
        attended, lse = attention_forward(qkv, kv_earlier, query[:, None], key[None, :], after)
        mid, low, logits, scalars, gate_rows = attention_output(
            hidden, attended, weights, prior, routes[micro]
        )
        mode = "with gate" if layer == layers - 1 else "plain"
        sent = dispatch(low, slot_rows[micro], gate_rows, mode, slots, groups, after_output)
        saved[micro][layer] = dict(
            hidden=hidden, attn_in=attn_in, attn_earlier=attn_earlier, prior=prior, qkv=qkv,
            kv_earlier=kv_earlier, attended=attended, lse=lse, mid=mid, low=low,
            scalars=scalars, gate_rows=gate_rows, logits=logits, arrived=exchange(sent, 1),
        )
        return sent[-1]

    def experts_part(layer, micro, after):
        kept = saved[micro][layer]
        gate_up_w, down_w = fetched[layer]["gate_up"], fetched[layer]["down"]
        if layer == layers - 1:
            out, expert_sums[layer] = experts_backward(
                kept["arrived"], early[micro], None, gate_up_w, down_w, expert_sums[layer], after
            )
            arrived = in_turn(out, 0)
            kept["returned"], kept["back"] = (arrived, 0), (arrived, 1)
        else:
            out, *kept["pre"] = experts_forward(kept["arrived"], gate_up_w, down_w, after)
            kept["returned"] = (in_turn(out, 0), 0)
        return out[-1]

    def combine_part(layer, micro, after):
        kept = saved[micro][layer]
        last = layer == layers - 1
        outs = combine(
            kept["returned"], columns[micro], kept["mid"], kept["scalars"],
            fetched[layer]["vectors"], None if last else fetched[layer + 1]["vectors"], after,
        )
        kept["branch"] = outs[:TOP]
        if last:
            return outs[TOP]
        state[micro] = (
            outs[TOP], outs[TOP + 1], earlier_rows(outs[TOP + 1], hop_count), kept["logits"],
        )
        return outs[TOP]

    def experts_back_part(layer, micro, d_rows, after):
        kept = saved[micro][layer]
        dx, expert_sums[layer] = experts_backward(
            kept["arrived"], d_rows, kept["pre"], fetched[layer]["gate_up"],
            fetched[layer]["down"], expert_sums[layer], after,
        )
        kept["back"] = (in_turn(dx, 0), 0)
        return dx[-1]

    def token_back_part(layer, micro, grad, d_prior, after):
        kept = saved[micro][layer]
        (
            kept["d_mid"], kept["d_att"], d_prior, kept["g_out"], kept["g_small"],
            kept["g_residual"], g_moe_gain,
        ) = token_backward(
            kept["back"], kept, grad, fetched[layer], columns[micro], routes[micro], d_prior, after
        )
        kept["g_moe_gain"] = g_moe_gain[0]
        return d_prior

    def attention_back_part(layer, micro, after):
        kept, dense = saved[micro][layer], fetched[layer]["dense"]
        query, key = segs[micro]
        dq, dk, dv = attention_backward(
            kept["qkv"], kept["kv_earlier"], kept["d_att"], kept["attended"], kept["lse"],
            query[None, :], key[:, None], after,
        )
        query_w, key_w, value_w = (dense[:, i * width : (i + 1) * width] for i in range(3))
        kept["later"] = None
        if hop_count > 0:
            d_earlier = (
                dot_on(dk[:WINDOW], key_w, 1, 1) + dot_on(dv[:WINDOW], value_w, 1, 1)
            ).astype(bf16)
            kept["later"] = returned_rows(d_earlier, length, hop_count)
        kept["d_attn"] = (
            dot_on(dq, query_w, 1, 1)
            + dot_on(dk[WINDOW:], key_w, 1, 1)
            + dot_on(dv[WINDOW:], value_w, 1, 1)
        )
        kept["grads"] = [
            dot_on(kept["attn_in"], dq, 0, 0),
            dot_on(kept["attn_in"], dk[WINDOW:], 0, 0)
            + dot_on(kept["attn_earlier"], dk[:WINDOW], 0, 0),
            dot_on(kept["attn_in"], dv[WINDOW:], 0, 0)
            + dot_on(kept["attn_earlier"], dv[:WINDOW], 0, 0),
            kept["g_out"],
            kept["g_small"],
        ]
        return dq

    def finish_back_part(layer, micro, after):
        kept = saved[micro][layer]
        d_hidden, g_attn_gain = finish_backward(
            kept["hidden"], kept["d_mid"], kept["d_attn"], fetched[layer]["vectors"],
            kept["later"], f32 if layer > 0 else bf16, after,
        )
        kept["g_attn_gain"] = g_attn_gain[0]
        return d_hidden

    expert_shares, dense_shares = [None] * layers, [None] * layers

    def reduce_experts(layer):
        gate_up, down = held(expert_sums[layer], saved[0][layer]["back"][0][1:])
        gate_up = gate_up.reshape((-1,) + gate_up.shape[2:])
        expert_shares[layer] = (
            lax.psum_scatter(gate_up, SHARDED, scatter_dimension=1, tiled=True),
            lax.psum_scatter(down, SHARDED, scatter_dimension=1, tiled=True),
        )
        return expert_shares[layer]

    def total_of(layer, name):
        parts = [saved[micro][layer][name] for micro in micros]
        return sum(parts[1:], parts[0])

    def packed_dense(layer):
        parts = [saved[micro][layer]["grads"] for micro in micros]
        sums = [sum(values[1:], values[0]) for values in zip(*parts)]
        shards = lax.axis_size("context") * lax.axis_size("dp")
        at = ROUTED + 8
        residual = jnp.pad(
            total_of(layer, "g_residual")[:ROUTED, :ROUTED],
            ((0, width // shards - ROUTED), (at, LANES - at - ROUTED)),
        )
        small = sums[-1] + jnp.tile(residual, (shards, 1))
        if layer == 0:
            gains = [total_of(l, "g_moe_gain") for l in range(layers)]
            gains += [total_of(l, "g_attn_gain") for l in range(1, layers)]
            blank = jnp.zeros((LANES - GAINS_LANE - len(gains), width), f32)
            above = jnp.zeros((GAINS_LANE, width), f32)
            small = small + jnp.concatenate([above, jnp.stack(gains), blank]).T
        return jnp.concatenate([total.astype(bf16) for total in sums[:-1] + [small]], axis=1)

    def reduce_dense(layer, packed, after):
        shards = lax.axis_size("context") * lax.axis_size("dp")
        parts = packed.reshape(shards, width // shards, packed.shape[1])
        parts = lax.all_to_all(parts, SHARDED, split_axis=0, concat_axis=0, tiled=True)
        share = jnp.sum(parts.astype(f32), axis=0)
        if layer > 0:
            (share,) = held([share.astype(bf16)], after)
            share = lax.psum(share, "expert").astype(f32)
        else:
            span = 1
            while span < groups:
                sent = share.astype(bf16)
                route = [(i, i ^ span) for i in range(groups)]
                share = sent.astype(f32) + lax.ppermute(sent, "expert", route).astype(f32)
                span *= 2
        dense_shares[layer] = share
        return (share,)

    last = layers - 1
    d_rows = [None] * micro_count

    def send_back(layer, micro, after):
        grads[micro] = finish_back_part(layer, micro, after)
        sent = dispatch(
            grads[micro], slot_rows[micro], saved[micro][layer - 1]["gate_rows"], "scaled", slots,
            groups,
        )
        d_rows[micro] = exchange(sent, 1)
        return sent[-1]

    before = ()
    for layer in range(layers):
        for micro in micros:
            if layer > 0:
                before = (combine_part(layer - 1, micro, before),)
        if layer == last:
            for micro in micros[1:]:
                send_early(micro, before)
        for micro in micros:
            waits = tuple(early[-1][1:]) if micro == 0 else ()
            before = (attention_part(layer, micro, before, waits),)
        for micro in micros:
            before = (experts_part(layer, micro, before),)
    hidden_out = []

    grads = [out_grad[micro, 0] for micro in micros]
    d_priors = [None] * micro_count
    dense_wait = ()
    for layer in range(last, -1, -1):
        experts_ready = reduce_experts(layer)
        for micro in micros:
            if layer == last:
                hidden_out.append(combine_part(last, micro, before))
                before = (hidden_out[-1],)
            d_priors[micro] = token_back_part(layer, micro, grads[micro], d_priors[micro], before)
            before = (saved[micro][layer]["d_att"],)
            before = (attention_back_part(layer, micro, before),)
            if layer > 0:
                before = (send_back(layer, micro, before),)
        if layer > 0:
            for micro in micros:
                if micro < len(experts_ready):
                    before += (experts_ready[micro],)
                before = (experts_back_part(layer - 1, micro, d_rows[micro], before),)
                if micro == 0:
                    first = before
            (packed,) = held([packed_dense(layer)], first)
            dense_wait = reduce_dense(layer, packed, before)
        else:
            packed = packed_dense(layer)
            for micro in micros:
                grads[micro] = finish_back_part(layer, micro, tuple(experts_ready) + dense_wait)
    reduce_dense(0, packed, ())
    first_gain = lax.psum(
        total_of(0, "g_attn_gain").astype(bf16), ("expert", "context", "dp")
    ).astype(f32)
    first_gain = lax.dynamic_slice_in_dim(
        first_gain, lax.axis_index(SHARDED) * w_query.shape[1], w_query.shape[1], 0
    )
    hidden_out = jnp.stack(hidden_out)[:, None]
    hidden_grad = jnp.stack(grads)[:, None]

    dense = jnp.stack(dense_shares)
    small = dense[:, :, 4 * width :]
    shard = small.shape[1]
    experts_total = [jnp.stack(parts).astype(f32) for parts in zip(*expert_shares)]
    per_dev = EXPERTS // groups
    return (
        hidden_out,
        hidden_grad,
        jnp.stack(
            [first_gain]
            + [small[0, :, GAINS_LANE + layers + l - 1] for l in range(1, layers)]
        ),
        dense[:, :, :width],
        dense[:, :, width : 2 * width],
        dense[:, :, 2 * width : 3 * width],
        dense[:, :, 3 * width : 4 * width],
        jnp.stack([small[0, :, GAINS_LANE + l] for l in range(layers)]),
        small[:, :, :ROUTED],
        small[:, :ROUTED, ROUTED + 8 : 2 * ROUTED + 8],
        jnp.transpose(
            small[:, :, ROUTED : ROUTED + 4].reshape(layers, shard, 2, 2), (0, 2, 1, 3)
        ),
        jnp.transpose(small[:, :, ROUTED + 4 : ROUTED + 6], (0, 2, 1)),
        experts_total[0][:, :per_dev],
        experts_total[0][:, per_dev:],
        experts_total[1],
    )

def solution(mesh):
    tokens = P(None, ("expert", "dp"), "context", None)
    rows = P(None, SHARDED, None)
    vector = P(None, SHARDED)
    experts = P(None, "expert", SHARDED, None)
    const = P(None, None, SHARDED, None)
    const_vector = P(None, None, SHARDED)
    return jax.shard_map(
        per_device,
        mesh=mesh,
        in_specs=(
            tokens, P(None, ("expert", "dp"), None), tokens, tokens, tokens, vector, rows, rows,
            rows, rows, vector, rows, P(), const, const_vector, experts, experts, experts,
        ),
        out_specs=(
            tokens, tokens, vector, rows, rows, rows, rows, vector, rows, P(), const,
            const_vector, experts, experts, experts,
        ),
        check_vma=False,
    )
```

```python
import functools

import jax
import jax.numpy as jnp
from jax import lax
from jax.experimental import pallas as pl
from jax.experimental.pallas import tpu as pltpu
from jax.sharding import PartitionSpec as P

HEADS = 12
HEAD_DIM = 64
EXPERTS = 8
TOP = 2
WINDOW = 1024
ROUTED = 12
LANES = 128
MIB = 1 << 20

norm_eps = 1e-05
masked = -1000000000.0
highest = lax.Precision.HIGHEST
f32 = jnp.float32
bf16 = jnp.bfloat16
SHARDED = ("context", "dp")


COST_SHARE = 0.3


def cost(microseconds):
    return pl.CostEstimate(
        flops=int(microseconds * COST_SHARE * 1.15e9), bytes_accessed=1, transcendentals=0
    )


ANY_SPEC = pl.BlockSpec(memory_space=pl.ANY)


def dot_on(left_op, right_op, left_dim, right_dim):
    return lax.dot_general(
        left_op,
        right_op,
        (((left_dim,), (right_dim,)), ((), ())),
        preferred_element_type=f32,
    )


def held(arrays, after):
    count = len(arrays)
    if not after:
        return list(arrays)
    return list(
        pl.pallas_call(
            lambda *refs: None,
            in_specs=[ANY_SPEC] * (count + len(after)),
            out_specs=[ANY_SPEC] * count,
            out_shape=[jax.ShapeDtypeStruct(array.shape, array.dtype) for array in arrays],
            input_output_aliases={index: index for index in range(count)},
            name="held",
        )(*arrays, *after)
    )


def rows_of(values, picks):
    count = 8 if len(picks) <= 8 else 16
    row = lax.broadcasted_iota(jnp.int32, (count, LANES), 0)
    lane = lax.broadcasted_iota(jnp.int32, (count, LANES), 1)
    pick = jnp.zeros((count, LANES), f32)
    for index, source in enumerate(picks):
        pick = jnp.where((row == index) & (lane == source), 1.0, pick)
    return lax.dot_general(
        pick, values, (((1,), (1,)), ((), ())), precision=highest, preferred_element_type=f32
    )


def join_spans(buffer_ref, earlier_ref, own_ref):
    buffer_ref[:WINDOW, :] = earlier_ref[...]
    buffer_ref[WINDOW:, :] = own_ref[...]


def attention_forward_kernel(
    rows, keys, blocks, q_ref, ko_ref, vo_ref, kp_ref, vp_ref, sq_ref, sk_ref, *rest
):
    out_ref, lse_rows_ref, lse_ref, bias_ref, k_ref, v_ref = rest[-6:]
    pair = pl.program_id(0)

    @pl.when(pair == 0)
    def _():
        lse_ref[...] = jnp.zeros_like(lse_ref)
        rel = lax.broadcasted_iota(jnp.int32, (rows, keys), 1) - lax.broadcasted_iota(
            jnp.int32, (rows, keys), 0
        )
        inside = (rel > 0) & (rel <= WINDOW)
        for block in range(blocks):
            first = block * rows
            same = sq_ref[first : first + rows, :] == sk_ref[:, first : first + keys]
            bias_ref[block] = jnp.where(inside & same, 0.0, masked)

    join_spans(k_ref, kp_ref, ko_ref)
    join_spans(v_ref, vp_ref, vo_ref)
    lane = lax.broadcasted_iota(jnp.int32, (rows, LANES), 1)
    low = lane < HEAD_DIM
    for block in range(blocks):
        own = slice(block * rows, (block + 1) * rows)
        span = slice(block * rows, block * rows + keys)
        query = q_ref[own, :] * (HEAD_DIM ** -0.5)
        key = k_ref[span, :]
        value = v_ref[span, :]
        heads_out = []
        for half in range(2):
            mine = low if half == 0 else ~low
            scores = (
                dot_on(jnp.where(mine, query, jnp.zeros_like(query)), key, 1, 1) + bias_ref[block]
            )
            row_max = jnp.max(scores, axis=1, keepdims=True)
            exponent = jnp.exp(scores - row_max)
            row_sum = jnp.sum(exponent, axis=1, keepdims=True)
            heads_out.append(dot_on(exponent.astype(bf16), value, 1, 0) * (1.0 / row_sum))
            lse_ref[own, :] = jnp.where(
                lane == 2 * pair + half, row_max + jnp.log(row_sum), lse_ref[own, :]
            )
        out_ref[own, :] = jnp.where(low, heads_out[0], heads_out[1]).astype(bf16)

    @pl.when(pair == pl.num_programs(0) - 1)
    def _():
        lse_rows_ref[...] = rows_of(lse_ref[...], range(HEADS))


def attention_forward(qkv, kv_earlier, seg_query, seg_key, after):
    length = qkv.shape[0]
    width = qkv.shape[1] // 3
    pairs = width // LANES
    rows = min(256, length)
    keys = rows + WINDOW
    blocks = length // rows
    span = WINDOW + length

    def column(count, offset):
        return pl.BlockSpec((count, LANES), lambda p: (0, offset + p))

    return pl.pallas_call(
        functools.partial(attention_forward_kernel, rows, keys, blocks),
        grid=(pairs,),
        in_specs=[
            column(length, 0),
            column(length, pairs),
            column(length, 2 * pairs),
            column(WINDOW, 0),
            column(WINDOW, pairs),
            pl.BlockSpec((length, 1), lambda p: (0, 0)),
            pl.BlockSpec((1, span), lambda p: (0, 0)),
        ]
        + [ANY_SPEC] * len(after),
        out_specs=[column(length, 0), pl.BlockSpec((16, length), lambda p: (0, 0))],
        out_shape=[
            jax.ShapeDtypeStruct((length, width), bf16),
            jax.ShapeDtypeStruct((16, length), f32),
        ],
        scratch_shapes=[
            pltpu.VMEM((length, LANES), f32),
            pltpu.VMEM((blocks, rows, keys), f32),
            pltpu.VMEM((span, LANES), bf16),
            pltpu.VMEM((span, LANES), bf16),
        ],
        compiler_params=pltpu.CompilerParams(vmem_limit_bytes=40 * MIB),
        cost_estimate=cost(32),
        name="attention_forward",
    )(qkv, qkv, qkv, kv_earlier, kv_earlier, seg_query, seg_key, *after)


def attention_backward_kernel(
    rows, keys, blocks, q_ref, ko_ref, vo_ref, kp_ref, vp_ref, do_ref, out_ref, lse_ref,
    sq_ref, sk_ref, *rest
):
    dq_ref, dk_ref, dv_ref, bias_ref, k_ref, v_ref, dk_sum, dv_sum = rest[-8:]
    pair = pl.program_id(0)

    @pl.when(pair == 0)
    def _():
        rel = lax.broadcasted_iota(jnp.int32, (keys, rows), 0) - lax.broadcasted_iota(
            jnp.int32, (keys, rows), 1
        )
        inside = (rel > 0) & (rel <= WINDOW)
        for block in range(blocks):
            first = block * rows
            same = sk_ref[first : first + keys, :] == sq_ref[:, first : first + rows]
            bias_ref[block] = jnp.where(inside & same, 0.0, masked)

    join_spans(k_ref, kp_ref, ko_ref)
    join_spans(v_ref, vp_ref, vo_ref)
    dk_sum[...] = jnp.zeros_like(dk_sum)
    dv_sum[...] = jnp.zeros_like(dv_sum)
    low = lax.broadcasted_iota(jnp.int32, (rows, LANES), 1) < HEAD_DIM
    ones = jnp.ones((8, LANES), bf16)
    for block in range(blocks):
        own = slice(block * rows, (block + 1) * rows)
        span = slice(block * rows, block * rows + keys)
        query = q_ref[own, :] * (HEAD_DIM ** -0.5)
        grad = do_ref[own, :]
        key = k_ref[span, :]
        value = v_ref[span, :]
        product = grad.astype(f32) * out_ref[own, :].astype(f32)
        heads_dq = []
        for half in range(2):
            mine = low if half == 0 else ~low
            query_h = jnp.where(mine, query, jnp.zeros_like(query))
            grad_h = jnp.where(mine, grad, jnp.zeros_like(grad))
            product_h = jnp.where(mine, product, 0.0)
            coarse = product_h.astype(bf16)
            fine = (product_h - coarse.astype(f32)).astype(bf16)
            delta = (dot_on(ones, coarse, 1, 1) + dot_on(ones, fine, 1, 1))[0:1, :]
            scores = dot_on(key, query_h, 1, 1) + bias_ref[block]
            probs = jnp.exp(scores - lse_ref[pl.ds(2 * pair + half, 1), own])
            d_probs = dot_on(value, grad_h, 1, 1)
            d_scores = (probs * (d_probs - delta)).astype(bf16)
            dv_sum[span, :] += dot_on(probs.astype(bf16), grad_h, 1, 0)
            dk_sum[span, :] += dot_on(d_scores, query_h, 1, 0)
            heads_dq.append(dot_on(d_scores, key, 0, 0))
        dq_ref[own, :] = (
            jnp.where(low, heads_dq[0], heads_dq[1]) * (HEAD_DIM ** -0.5)
        ).astype(bf16)
    dk_ref[...] = dk_sum[...].astype(bf16)
    dv_ref[...] = dv_sum[...].astype(bf16)


def attention_backward(qkv, kv_earlier, grad_att, attended, lse, seg_query, seg_key, after):
    length = qkv.shape[0]
    width = qkv.shape[1] // 3
    pairs = width // LANES
    rows = min(256, length)
    keys = rows + WINDOW
    blocks = length // rows
    span = WINDOW + length

    def column(count, offset):
        return pl.BlockSpec((count, LANES), lambda p: (0, offset + p))

    return pl.pallas_call(
        functools.partial(attention_backward_kernel, rows, keys, blocks),
        grid=(pairs,),
        in_specs=[
            column(length, 0),
            column(length, pairs),
            column(length, 2 * pairs),
            column(WINDOW, 0),
            column(WINDOW, pairs),
            column(length, 0),
            column(length, 0),
            pl.BlockSpec((16, length), lambda p: (0, 0)),
            pl.BlockSpec((1, length), lambda p: (0, 0)),
            pl.BlockSpec((span, 1), lambda p: (0, 0)),
        ]
        + [ANY_SPEC] * len(after),
        out_specs=[column(length, 0), column(span, 0), column(span, 0)],
        out_shape=[
            jax.ShapeDtypeStruct((length, width), bf16),
            jax.ShapeDtypeStruct((span, width), bf16),
            jax.ShapeDtypeStruct((span, width), bf16),
        ],
        scratch_shapes=[
            pltpu.VMEM((blocks, keys, rows), f32),
            pltpu.VMEM((span, LANES), bf16),
            pltpu.VMEM((span, LANES), bf16),
            pltpu.VMEM((span, LANES), f32),
            pltpu.VMEM((span, LANES), f32),
        ],
        compiler_params=pltpu.CompilerParams(vmem_limit_bytes=48 * MIB),
        cost_estimate=cost(48),
        name="attention_backward",
    )(
        qkv, qkv, qkv, kv_earlier, kv_earlier, grad_att, attended, lse, seg_query, seg_key, *after
    )


def sigmoid(values):
    return 1.0 / (1.0 + jnp.exp(-values))


def gathered(rows_ref, block_refs):
    count = block_refs[0].shape[0]
    width = rows_ref.shape[1]
    for index, block_ref in enumerate(block_refs):
        rows_ref[index * count : (index + 1) * count, :] = block_ref[:, :width]


def scattered(block_refs, rows, which=0):
    count = block_refs[0].shape[1]
    for index, block_ref in enumerate(block_refs):
        block_ref[which] = rows[index * count : (index + 1) * count, :].astype(bf16)


def experts_forward_kernel(groups, *refs):
    block_refs, (gate_w_ref, up_w_ref, down_w_ref) = refs[:groups], refs[groups : groups + 3]
    out_refs, (gate_ref, up_ref, rows_ref) = refs[-groups - 3 : -3], refs[-3:]
    gathered(rows_ref, block_refs)
    rows_in = rows_ref[...]
    gate_pre = dot_on(rows_in, gate_w_ref[0], 1, 0)
    up_pre = dot_on(rows_in, up_w_ref[0], 1, 0)
    activated = (gate_pre * sigmoid(gate_pre) * up_pre).astype(bf16)
    gate_ref[0] = gate_pre.astype(bf16)
    up_ref[0] = up_pre.astype(bf16)
    scattered(out_refs, dot_on(activated, down_w_ref[0], 1, 0))


def experts_forward(blocks, gate_up_w, down_w, after):
    groups = len(blocks)
    count = down_w.shape[0]
    width, hidden = gate_up_w.shape[1:]
    part = blocks[0].shape[0] // count
    rows = groups * part
    block_spec = pl.BlockSpec((part, width), lambda j: (j, 0))
    hidden_spec = pl.BlockSpec((1, rows, hidden), lambda j: (j, 0, 0))
    hidden_shape = jax.ShapeDtypeStruct((count, rows, hidden), bf16)
    *produced, gate_pre, up_pre = pl.pallas_call(
        functools.partial(experts_forward_kernel, groups),
        grid=(count,),
        in_specs=[block_spec] * groups
        + [
            pl.BlockSpec((1, width, hidden), lambda j: (j, 0, 0)),
            pl.BlockSpec((1, width, hidden), lambda j: (count + j, 0, 0)),
            pl.BlockSpec((1, hidden, width), lambda j: (j, 0, 0)),
        ]
        + [ANY_SPEC] * len(after),
        out_specs=[pl.BlockSpec((1, part, width), lambda j: (0, j, 0))] * groups
        + [hidden_spec, hidden_spec],
        out_shape=[jax.ShapeDtypeStruct((1, count * part, width), bf16)] * groups
        + [hidden_shape, hidden_shape],
        scratch_shapes=[pltpu.VMEM((rows, width), bf16)],
        compiler_params=pltpu.CompilerParams(vmem_limit_bytes=48 * MIB),
        cost_estimate=cost(26),
        name="experts_forward",
    )(*blocks, gate_up_w, gate_up_w, down_w, *after)
    return produced, gate_pre, up_pre


def experts_backward_kernel(groups, chunks, whole, has_sums, *refs):
    block_refs, d_refs, given = refs[:groups], refs[groups : 2 * groups], refs[2 * groups :]
    gate_w_ref, up_w_ref, down_w_ref = given[:3]
    if whole:
        share_refs, given = given[3 : 3 + groups], given[3 + groups :]
        *refs, produced_ref = refs
    else:
        (gate_ref, up_ref), given = given[3:5], given[5:]
    out_refs = refs[-5 - groups : -5]
    gate_up_grad_ref, down_grad_ref, total_ref, rows_ref, d_ref = refs[-5:]
    chunk = pl.program_id(1)

    @pl.when(chunk == 0)
    def _():
        gathered(rows_ref, block_refs)
        if whole:
            count = d_refs[0].shape[0]
            for index in range(groups):
                share = share_refs[index][...].astype(f32)
                share = share[:, 0:1] + share[:, 1:2]
                d_ref[index * count : (index + 1) * count, :] = (
                    d_refs[index][...].astype(f32) * share
                ).astype(bf16)
        else:
            gathered(d_ref, d_refs)

    rows_in = rows_ref[...]
    d_out = d_ref[...]
    if whole:
        gate_pre = dot_on(rows_in, gate_w_ref[0], 1, 0)
        up_pre = dot_on(rows_in, up_w_ref[0], 1, 0)
    else:
        gate_pre = gate_ref[0].astype(f32)
        up_pre = up_ref[0].astype(f32)
    share = sigmoid(gate_pre)
    swish = gate_pre * share
    activated = (swish * up_pre).astype(bf16)
    d_act = dot_on(d_out, down_w_ref[0], 1, 1)
    d_gate = (d_act * up_pre * (share * (1.0 + gate_pre * (1.0 - share)))).astype(bf16)
    d_up = (d_act * swish).astype(bf16)
    part = dot_on(d_gate, gate_w_ref[0], 1, 1) + dot_on(d_up, up_w_ref[0], 1, 1)
    gate_grad = dot_on(rows_in, d_gate, 0, 0)
    up_grad = dot_on(rows_in, d_up, 0, 0)
    down_grad = dot_on(activated, d_out, 0, 0)
    if has_sums:
        gate_up_sum_ref, down_sum_ref = given[:2]
        gate_grad += gate_up_sum_ref[0, 0].astype(f32)
        up_grad += gate_up_sum_ref[1, 0].astype(f32)
        down_grad += down_sum_ref[0].astype(f32)
    gate_up_grad_ref[0, 0] = gate_grad.astype(bf16)
    gate_up_grad_ref[1, 0] = up_grad.astype(bf16)
    down_grad_ref[0] = down_grad.astype(bf16)
    sums = [(total_ref, part)]
    if whole:
        sums.append((produced_ref, dot_on(activated, down_w_ref[0], 1, 0)))

    @pl.when(chunk == 0)
    def _():
        for sum_ref, value in sums:
            sum_ref[...] = value

    @pl.when(chunk > 0)
    def _():
        for sum_ref, value in sums:
            sum_ref[...] += value

    @pl.when(chunk == chunks - 1)
    def _():
        scattered(out_refs, total_ref[...], len(sums) - 1)
        if whole:
            scattered(out_refs, produced_ref[...])


def experts_backward(blocks, d_blocks, pre, gate_up_w, down_w, sums, after):
    groups = len(blocks)
    count, hidden, width = down_w.shape
    part = blocks[0].shape[0] // count
    rows = groups * part
    whole = pre is None
    chunk = min(512, hidden)
    chunks = hidden // chunk
    block_spec = pl.BlockSpec((part, width), lambda j, f: (j, 0))
    hidden_spec = pl.BlockSpec((1, rows, chunk), lambda j, f: (j, 0, f))
    wide_spec = pl.BlockSpec((1, width, chunk), lambda j, f: (j, 0, f))
    up_spec = pl.BlockSpec((1, width, chunk), lambda j, f: (count + j, 0, f))
    tall_spec = pl.BlockSpec((1, chunk, width), lambda j, f: (j, f, 0))
    both_spec = pl.BlockSpec((2, 1, width, chunk), lambda j, f: (0, j, 0, f))
    operands = [*blocks, *d_blocks, gate_up_w, gate_up_w, down_w]
    specs = [block_spec] * (2 * groups) + [wide_spec, up_spec, tall_spec]
    if whole:
        operands.extend(blocks)
        specs += [pl.BlockSpec((part, LANES), lambda j, f: (j, width // LANES))] * groups
    else:
        operands.extend(pre)
        specs += [hidden_spec, hidden_spec]
    if sums is not None:
        operands.extend(sums)
        specs.extend([both_spec, tall_spec])
    outs = 2 if whole else 1
    *out, gate_up_grad, down_grad = pl.pallas_call(
        functools.partial(experts_backward_kernel, groups, chunks, whole, sums is not None),
        grid=(count, chunks),
        in_specs=specs + [ANY_SPEC] * len(after),
        out_specs=[pl.BlockSpec((outs, part, width), lambda j, f: (0, j, 0))] * groups
        + [both_spec, tall_spec],
        out_shape=[jax.ShapeDtypeStruct((outs, count * part, width), bf16)] * groups
        + [
            jax.ShapeDtypeStruct((2, count, width, hidden), bf16),
            jax.ShapeDtypeStruct((count, hidden, width), bf16),
        ],
        scratch_shapes=[
            pltpu.VMEM((rows, width), f32),
            pltpu.VMEM((rows, width), bf16),
            pltpu.VMEM((rows, width), bf16),
        ]
        + ([pltpu.VMEM((rows, width), f32)] if whole else []),
        compiler_params=pltpu.CompilerParams(vmem_limit_bytes=58 * MIB),
        cost_estimate=cost(75 if whole else 52),
        name="experts_whole" if whole else "experts_backward",
    )(*operands, *after)
    return out, (gate_up_grad, down_grad)


def passed_along(block, axis, distance):
    devices = range(lax.axis_size(axis))
    route = [(i - distance, i) for i in devices if i - distance in devices]
    return lax.ppermute(block, axis, route)


def earlier_rows(block, hop_count):
    pieces = [passed_along(block, "context", hop) for hop in range(hop_count, 0, -1)]
    missing = WINDOW - hop_count * block.shape[-2]
    if missing > 0:
        shape = block.shape[:-2] + (missing, block.shape[-1])
        pieces = [jnp.zeros(shape, block.dtype)] + pieces
    rows = pieces[0] if len(pieces) == 1 else jnp.concatenate(pieces, axis=-2)
    return rows[..., rows.shape[-2] - WINDOW :, :]


def returned_rows(block, length, hop_count):
    total = None
    for hop in range(1, hop_count + 1):
        first = WINDOW - hop * length
        part = block[max(first, 0) : first + length]
        if first < 0:
            part = jnp.concatenate([jnp.zeros((-first, block.shape[1]), block.dtype), part])
        part = passed_along(part, "context", -hop).astype(f32)
        total = part if total is None else total + part
    return total


def exchange(blocks, direction):
    groups = lax.axis_size("expert")
    out = []
    for d, block in enumerate(blocks):
        step = d * direction
        route = [(i, (i + step) % groups) for i in range(groups)]
        out.append(block if d == 0 else lax.ppermute(block, "expert", route))
    return out


GATE, OF_NORMED, NORMED_SHARE, VECTOR_SHARE, MIX, SCALE, CHOSEN = 0, 2, 4, 5, 7, 9, 10
GAINS_LANE = 2 * ROUTED + 8
VECTOR_ROW, ATTN_GAIN_ROW, MOE_GAIN_ROW = 0, 2, 3


def inverse_rms(rows):
    return lax.rsqrt(jnp.mean(rows * rows, axis=-1, keepdims=True) + norm_eps)


def lane_iota(rows):
    return lax.broadcasted_iota(jnp.int32, (rows, LANES), 1)


def placed_on_lanes(rows, values):
    lane = lane_iota(rows)
    total = jnp.zeros((rows, LANES), f32)
    for index, value in values.items():
        total = jnp.where(lane == index, value, total)
    return total


def routing_kernel(routes_ref, base_ref, columns_ref, rows_ref):
    length = routes_ref.shape[1]
    lane = lane_iota(length)
    onehots = [(lane == routes_ref[0, :, k : k + 1]).astype(f32) for k in range(TOP)]
    counts = (onehots[0] + onehots[1]).astype(bf16)
    earlier = lax.broadcasted_iota(jnp.int32, (length, length), 0) > lax.broadcasted_iota(
        jnp.int32, (length, length), 1
    )
    rank = dot_on(jnp.where(earlier, 1.0, 0.0).astype(bf16), counts, 1, 0)
    place = base_ref[...] + jnp.where(lane < EXPERTS, rank, 0.0)
    slots = placed_on_lanes(
        length,
        {k: jnp.sum(onehots[k] * place, axis=1, keepdims=True) for k in range(TOP)},
    )
    columns_ref[0] = slots.astype(jnp.int32)
    rows_ref[0] = jnp.round(rows_of(slots, range(TOP))).astype(jnp.int32)


def routing_slots(routes, groups, capacity):
    count, length, _ = routes.shape
    per_dev = EXPERTS // groups
    expert = jnp.arange(LANES)
    place = (expert // per_dev - lax.axis_index("expert")) % groups
    base = (place * per_dev + expert % per_dev) * capacity
    base = jnp.where(expert < EXPERTS, base, -1).astype(f32)[None, :]
    return pl.pallas_call(
        routing_kernel,
        grid=(count,),
        in_specs=[
            pl.BlockSpec((1, length, TOP), lambda m: (m, 0, 0)),
            pl.BlockSpec((1, LANES), lambda m: (0, 0)),
        ],
        out_specs=[
            pl.BlockSpec((1, length, LANES), lambda m: (m, 0, 0)),
            pl.BlockSpec((1, 8, length), lambda m: (m, 0, 0)),
        ],
        out_shape=[
            jax.ShapeDtypeStruct((count, length, LANES), jnp.int32),
            jax.ShapeDtypeStruct((count, 8, length), jnp.int32),
        ],
        compiler_params=pltpu.CompilerParams(vmem_limit_bytes=32 * MIB),
        cost_estimate=cost(4),
        name="routing",
    )(routes, base)


def dispatch_kernel(mode, per_group, groups, rows_ref, slots_ref, gates_ref, *rest):
    out_refs = rest[-groups:]
    count, length = out_refs[0].shape[0], rows_ref.shape[0]
    width = rows_ref.shape[1]
    rows = rows_ref[...].astype(bf16)
    for group, out_ref in enumerate(out_refs):
        first = group * per_group + pl.program_id(0) * count
        slot = first + lax.broadcasted_iota(jnp.int32, (count, length), 0)
        hits = [slot == slots_ref[k : k + 1, :] for k in range(TOP)]
        table = jnp.where(hits[0] | hits[1], 1.0, 0.0).astype(bf16)
        found = dot_on(table, rows, 1, 0)
        if mode == "plain":
            out_ref[...] = found.astype(bf16)
            continue
        gate = jnp.sum(
            jnp.where(hits[0], gates_ref[0:1, :], 0.0)
            + jnp.where(hits[1], gates_ref[1:2, :], 0.0),
            axis=1,
            keepdims=True,
        )
        if mode == "scaled":
            out_ref[...] = (found * gate).astype(bf16)
            continue
        out_ref[:, :width] = found.astype(bf16)
        coarse = gate.astype(bf16).astype(f32)
        out_ref[:, width:] = placed_on_lanes(count, {0: coarse, 1: gate - coarse}).astype(bf16)


def dispatch(rows, slot_rows, gate_rows, mode, slots, groups, after=()):
    length, width = rows.shape
    per_group = slots // groups
    count = min(256, per_group)
    out_width = width + LANES if mode == "with gate" else width
    return pl.pallas_call(
        functools.partial(dispatch_kernel, mode, per_group, groups),
        grid=(per_group // count,),
        in_specs=[
            pl.BlockSpec((length, width), lambda s: (0, 0)),
            pl.BlockSpec((8, length), lambda s: (0, 0)),
            pl.BlockSpec((8, length), lambda s: (0, 0)),
        ]
        + [ANY_SPEC] * len(after),
        out_specs=[pl.BlockSpec((count, out_width), lambda s: (s, 0))] * groups,
        out_shape=[jax.ShapeDtypeStruct((per_group, out_width), bf16)] * groups,
        compiler_params=pltpu.CompilerParams(vmem_limit_bytes=32 * MIB),
        cost_estimate=cost(6),
        name="dispatch",
    )(rows, slot_rows, gate_rows, *after)


def attention_output_kernel(
    hidden_ref, attended_ref, out_w_ref, small_w_ref, vectors_ref, prior_ref, residual_ref,
    routes_ref, mid_ref, low_ref, logits_ref, scalars_ref, gates_ref,
):
    rows = hidden_ref.shape[0]
    mid = hidden_ref[...] + dot_on(attended_ref[...], out_w_ref[...], 1, 0)
    mid_ref[...] = mid
    scale = inverse_rms(mid)
    low = (mid * scale * vectors_ref[MOE_GAIN_ROW : MOE_GAIN_ROW + 1, :]).astype(bf16)
    low_ref[...] = low
    logits = dot_on(low, small_w_ref[...], 1, 0) + jnp.dot(
        prior_ref[...], residual_ref[...], precision=highest
    )
    logits_ref[...] = logits
    lane = lane_iota(rows)
    onehots = [lane == routes_ref[:, k : k + 1] for k in range(TOP)]

    def lane_sum(values):
        return jnp.sum(values, axis=1, keepdims=True)

    difference = lane_sum(jnp.where(onehots[0], logits, jnp.where(onehots[1], -logits, 0.0)))
    gates = (sigmoid(difference), sigmoid(-difference))
    chosen = [
        [jnp.where(routes_ref[:, k : k + 1] == EXPERTS + 2 + j, 1.0, 0.0) for j in range(2)]
        for k in range(TOP)
    ]
    alphas = []
    for j in range(2):
        at = ROUTED + 2 * j
        gap = lane_sum(jnp.where(lane == at, logits, jnp.where(lane == at + 1, -logits, 0.0)))
        alphas.append((sigmoid(gap), sigmoid(-gap)))
    of_normed = [
        jnp.where(routes_ref[:, k : k + 1] == EXPERTS + 1, 1.0, 0.0)
        + chosen[k][0] * alphas[0][0]
        + chosen[k][1] * alphas[1][0]
        for k in range(TOP)
    ]
    vector_gate = [gates[0] * chosen[0][j] + gates[1] * chosen[1][j] for j in range(2)]
    values = {
        GATE: gates[0], GATE + 1: gates[1],
        OF_NORMED: of_normed[0], OF_NORMED + 1: of_normed[1],
        NORMED_SHARE: gates[0] * of_normed[0] + gates[1] * of_normed[1],
        SCALE: scale,
    }
    for j in range(2):
        values[VECTOR_SHARE + j] = vector_gate[j] * alphas[j][1]
        values[MIX + j] = vector_gate[j] * alphas[j][0] * alphas[j][1]
        for k in range(TOP):
            values[CHOSEN + 2 * k + j] = chosen[k][j] * alphas[j][1]
    scalars = placed_on_lanes(rows, values)
    scalars_ref[...] = scalars
    gates_ref[...] = rows_of(scalars, (GATE, GATE + 1))


def attention_output(hidden, attended, weights, prior, routes):
    length, width = hidden.shape
    rows = min(256, length)
    wide = pl.BlockSpec((rows, width), lambda t: (t, 0))
    lanes = pl.BlockSpec((rows, LANES), lambda t: (t, 0))
    return pl.pallas_call(
        attention_output_kernel,
        grid=(length // rows,),
        in_specs=[
            wide,
            wide,
            pl.BlockSpec((width, width), lambda t: (0, 3)),
            pl.BlockSpec((width, LANES), lambda t: (0, 4 * width // LANES)),
            pl.BlockSpec((8, width), lambda t: (0, 0)),
            lanes,
            pl.BlockSpec((LANES, LANES), lambda t: (0, 0)),
            pl.BlockSpec((rows, TOP), lambda t: (t, 0)),
        ],
        out_specs=[wide, wide, lanes, lanes, pl.BlockSpec((8, rows), lambda t: (0, t))],
        out_shape=[
            jax.ShapeDtypeStruct((length, width), f32),
            jax.ShapeDtypeStruct((length, width), bf16),
            jax.ShapeDtypeStruct((length, LANES), f32),
            jax.ShapeDtypeStruct((length, LANES), f32),
            jax.ShapeDtypeStruct((8, length), f32),
        ],
        compiler_params=pltpu.CompilerParams(vmem_limit_bytes=24 * MIB),
        cost_estimate=cost(8),
        name="attention_output",
    )(
        hidden, attended, weights["dense"], weights["dense"], weights["vectors"], prior,
        weights["residual"], routes,
    )


def selected(columns, block_refs, which):
    per_group = block_refs[0].shape[0]
    total = None
    for group, block_ref in enumerate(block_refs):
        slot = group * per_group + lax.broadcasted_iota(
            jnp.int32, (columns.shape[0], per_group), 1
        )
        hit = slot == columns[:, which[0] : which[0] + 1]
        for k in which[1:]:
            hit = hit | (slot == columns[:, k : k + 1])
        part = dot_on(jnp.where(hit, 1.0, 0.0).astype(bf16), block_ref[...], 1, 0)
        total = part if total is None else total + part
    return total


def combine_kernel(last, groups, waits, *refs):
    back_refs, (columns_ref, mid_ref, scalars_ref, vectors_ref, next_ref) = (
        refs[:groups], refs[groups : groups + 5],
    )
    out_refs = refs[groups + 5 + waits :]
    columns, scalars = columns_ref[...], scalars_ref[...]
    mid = mid_ref[...]
    normed = mid * scalars[:, SCALE : SCALE + 1] * vectors_ref[MOE_GAIN_ROW : MOE_GAIN_ROW + 1, :]
    total = mid + scalars[:, NORMED_SHARE : NORMED_SHARE + 1] * normed
    for j in range(2):
        row = vectors_ref[VECTOR_ROW + j : VECTOR_ROW + j + 1, :]
        total += scalars[:, VECTOR_SHARE + j : VECTOR_SHARE + j + 1] * row
    for k in range(TOP):
        branch = selected(columns, back_refs, (k,))
        out_refs[k][...] = branch.astype(bf16)
        total += scalars[:, GATE + k : GATE + k + 1] * branch
    if last:
        out_refs[TOP][...] = total.astype(bf16)
    else:
        out_refs[TOP][...] = total
        out_refs[TOP + 1][...] = (
            total * inverse_rms(total) * next_ref[ATTN_GAIN_ROW : ATTN_GAIN_ROW + 1, :]
        ).astype(bf16)


def combine(back, columns, mid, scalars, vectors, next_vectors, after):
    last = next_vectors is None
    length, width = mid.shape
    back, which = back
    groups, per_group = len(back), back[0].shape[1]
    rows = min(256, length)
    wide = pl.BlockSpec((rows, width), lambda t: (t, 0))
    lanes = pl.BlockSpec((rows, LANES), lambda t: (t, 0))
    vector_spec = pl.BlockSpec((8, width), lambda t: (0, 0))
    low = jax.ShapeDtypeStruct((length, width), bf16)
    return pl.pallas_call(
        functools.partial(combine_kernel, last, groups, len(after)),
        grid=(length // rows,),
        in_specs=[pl.BlockSpec((None, per_group, width), lambda t: (which, 0, 0))] * groups
        + [lanes, wide, lanes, vector_spec, vector_spec]
        + [ANY_SPEC] * len(after),
        out_specs=[wide] * (TOP + 1 if last else TOP + 2),
        out_shape=[low, low, low]
        if last
        else [low, low, jax.ShapeDtypeStruct((length, width), f32), low],
        compiler_params=pltpu.CompilerParams(vmem_limit_bytes=24 * MIB),
        cost_estimate=cost(8),
        name="combine",
    )(*back, columns, mid, scalars, vectors, vectors if last else next_vectors, *after)


def token_backward_kernel(
    has_prior, groups, *refs
):
    back_refs, rest = refs[:groups], refs[groups:]
    (
        columns_ref, grad_ref, mid_ref, scalars_ref, branch0_ref, branch1_ref, low_ref, prior_ref,
        attended_ref, routes_ref, out_w_ref, small_w_ref, vectors_ref, residual_ref,
    ) = rest[:14]
    rest = rest[14:]
    d_mid_ref, d_att_ref, d_prior_ref, g_out_ref, g_small_ref, g_residual_ref, g_gain_ref = (
        rest[-7:]
    )
    step = pl.program_id(0)
    rows = mid_ref.shape[0]
    columns, scalars = columns_ref[...], scalars_ref[...]
    grad = grad_ref[...].astype(f32)
    mid = mid_ref[...]
    gain = vectors_ref[MOE_GAIN_ROW : MOE_GAIN_ROW + 1, :]
    scale = scalars[:, SCALE : SCALE + 1]
    unit = mid * scale
    lane = lane_iota(rows)

    def scalar(index):
        return scalars[:, index : index + 1]

    def row_sum(values):
        return jnp.sum(values, axis=1, keepdims=True)

    along = row_sum(grad * (unit * gain))
    along_vector = [
        row_sum(grad * vectors_ref[VECTOR_ROW + j : VECTOR_ROW + j + 1, :]) for j in range(2)
    ]
    d_gate = []
    for k, branch_ref in enumerate((branch0_ref, branch1_ref)):
        value = row_sum(grad * branch_ref[...].astype(f32)) + scalar(OF_NORMED + k) * along
        for j in range(2):
            value += scalar(CHOSEN + 2 * k + j) * along_vector[j]
        d_gate.append(value)
    d_choice = scalar(GATE) * scalar(GATE + 1) * (d_gate[0] - d_gate[1])
    d_small = jnp.where(
        lane == routes_ref[:, 0:1], d_choice, jnp.where(lane == routes_ref[:, 1:2], -d_choice, 0.0)
    )
    if has_prior:
        d_small += jnp.where(lane < ROUTED, rest[0][...], 0.0)
    d_logits = d_small
    for j in range(2):
        value = scalar(MIX + j) * (along - along_vector[j])
        at = ROUTED + 2 * j
        d_small = jnp.where(lane == at, value, jnp.where(lane == at + 1, -value, d_small))
    d_small_low = d_small.astype(bf16)
    d_prior_ref[...] = lax.dot_general(
        d_logits, residual_ref[...], (((1,), (1,)), ((), ())), precision=highest
    )
    vector_shares = placed_on_lanes(
        rows, {ROUTED + 4 + j: scalar(VECTOR_SHARE + j) for j in range(2)}
    ).astype(bf16)
    g_small = dot_on(low_ref[...], d_small_low, 0, 0) + dot_on(
        grad.astype(bf16), vector_shares, 0, 0
    )
    g_residual = lax.dot_general(
        prior_ref[...], d_logits, (((0,), (0,)), ((), ())), precision=highest
    )
    d_normed = (
        selected(columns, back_refs, (0, 1))
        + scalar(NORMED_SHARE) * grad
        + dot_on(d_small_low, small_w_ref[...], 1, 1)
    )
    g_gain = jnp.sum(d_normed * unit, axis=0, keepdims=True)
    d_unit = d_normed * gain
    d_mid = grad + (d_unit - unit * jnp.mean(d_unit * unit, axis=-1, keepdims=True)) * scale
    d_mid_ref[...] = d_mid
    d_mid_low = d_mid.astype(bf16)
    d_att_ref[...] = dot_on(d_mid_low, out_w_ref[...], 1, 1).astype(bf16)
    g_out = dot_on(attended_ref[...], d_mid_low, 0, 0)

    @pl.when(step == 0)
    def _():
        g_out_ref[...] = g_out
        g_small_ref[...] = g_small
        g_residual_ref[...] = g_residual
        g_gain_ref[...] = jnp.broadcast_to(g_gain, g_gain_ref.shape)

    @pl.when(step > 0)
    def _():
        g_out_ref[...] += g_out
        g_small_ref[...] += g_small
        g_residual_ref[...] += g_residual
        g_gain_ref[...] += jnp.broadcast_to(g_gain, g_gain_ref.shape)


def token_backward(back, kept, grad, weights, columns, routes, d_prior, after):
    length, width = grad.shape
    back, which = back
    groups, per_group = len(back), back[0].shape[1]
    rows = min(256, length)
    wide = pl.BlockSpec((rows, width), lambda t: (t, 0))
    lanes = pl.BlockSpec((rows, LANES), lambda t: (t, 0))

    def fixed(*shape, at=0):
        return pl.BlockSpec(shape, lambda t: (0, at))

    operands = [
        *back, columns, grad, kept["mid"], kept["scalars"], kept["branch"][0], kept["branch"][1],
        kept["low"], kept["prior"], kept["attended"], routes, weights["dense"], weights["dense"],
        weights["vectors"], weights["residual"],
    ]
    specs = [
        *[pl.BlockSpec((None, per_group, width), lambda t: (which, 0, 0))] * groups,
        lanes, wide, wide, lanes, wide, wide, wide, lanes, wide,
        pl.BlockSpec((rows, TOP), lambda t: (t, 0)), fixed(width, width, at=3),
        fixed(width, LANES, at=4 * width // LANES), fixed(8, width), fixed(LANES, LANES),
    ]
    if d_prior is not None:
        operands.append(d_prior)
        specs.append(lanes)
    return pl.pallas_call(
        functools.partial(token_backward_kernel, d_prior is not None, groups),
        grid=(length // rows,),
        in_specs=specs + [ANY_SPEC] * len(after),
        out_specs=[
            wide, wide, lanes, fixed(width, width), fixed(width, LANES), fixed(LANES, LANES),
            fixed(8, width),
        ],
        out_shape=[
            jax.ShapeDtypeStruct((length, width), f32),
            jax.ShapeDtypeStruct((length, width), bf16),
            jax.ShapeDtypeStruct((length, LANES), f32),
            jax.ShapeDtypeStruct((width, width), f32),
            jax.ShapeDtypeStruct((width, LANES), f32),
            jax.ShapeDtypeStruct((LANES, LANES), f32),
            jax.ShapeDtypeStruct((8, width), f32),
        ],
        compiler_params=pltpu.CompilerParams(vmem_limit_bytes=48 * MIB),
        cost_estimate=cost(25),
        name="token_backward",
    )(*operands, *after)


def finish_backward_kernel(
    has_later, hidden_ref, d_mid_ref, d_attn_ref, vectors_ref, *rest
):
    out_ref, g_gain_ref = rest[-2:]
    hidden = hidden_ref[...]
    d_attn = d_attn_ref[...]
    if has_later:
        d_attn += rest[0][...].astype(f32)
    scale = inverse_rms(hidden)
    unit = hidden * scale
    g_gain = jnp.broadcast_to(jnp.sum(d_attn * unit, axis=0, keepdims=True), g_gain_ref.shape)
    d_unit = d_attn * vectors_ref[ATTN_GAIN_ROW : ATTN_GAIN_ROW + 1, :]
    out_ref[...] = (
        d_mid_ref[...] + (d_unit - unit * jnp.mean(d_unit * unit, axis=-1, keepdims=True)) * scale
    ).astype(out_ref.dtype)

    @pl.when(pl.program_id(0) == 0)
    def _():
        g_gain_ref[...] = g_gain

    @pl.when(pl.program_id(0) > 0)
    def _():
        g_gain_ref[...] += g_gain


def finish_backward(hidden, d_mid, d_attn, vectors, later, out_type, after):
    length, width = hidden.shape
    rows = min(256, length)
    wide = pl.BlockSpec((rows, width), lambda t: (t, 0))
    vector_spec = pl.BlockSpec((8, width), lambda t: (0, 0))
    extra = [] if later is None else [later]
    return pl.pallas_call(
        functools.partial(finish_backward_kernel, later is not None),
        grid=(length // rows,),
        in_specs=[wide, wide, wide, vector_spec] + [wide] * len(extra) + [ANY_SPEC] * len(after),
        out_specs=[wide, vector_spec],
        out_shape=[
            jax.ShapeDtypeStruct((length, width), out_type),
            jax.ShapeDtypeStruct((8, width), f32),
        ],
        compiler_params=pltpu.CompilerParams(vmem_limit_bytes=24 * MIB),
        cost_estimate=cost(6),
        name="finish_backward",
    )(hidden, d_mid, d_attn, vectors, *extra, *after)


def fetch_layer(layer, local):
    width = local["w_query"].shape[2]
    shard = local["w_query"].shape[1]
    const_w = jnp.transpose(local["w_const"][layer], (1, 0, 2)).reshape(shard, 4)
    small = jnp.concatenate(
        [
            local["w_router"][layer], const_w, local["const_vec"][layer].T,
            local["norm_attn"][layer][:, None], local["norm_moe"][layer][:, None],
            jnp.zeros((shard, LANES - ROUTED - 8), bf16),
        ],
        axis=1,
    )
    packed = jnp.concatenate(
        [local["w_query"][layer], local["w_key"][layer], local["w_value"][layer],
         local["w_out"][layer], small],
        axis=1,
    )
    dense = lax.all_gather(packed, SHARDED, axis=0, tiled=True)
    gate_up = jnp.concatenate([local["w_gate"][layer], local["w_up"][layer]], axis=0)
    gate_up = lax.all_gather(gate_up, SHARDED, axis=1, tiled=True)
    down = lax.all_gather(local["w_down"][layer], SHARDED, axis=1, tiled=True)
    at = 4 * width + ROUTED + 4
    vectors = dense[:, at : at + 8].T.astype(f32)
    residual = local["w_res"][layer].astype(f32)
    blank = LANES - ROUTED
    return dict(
        dense=dense, vectors=vectors, gate_up=gate_up, down=down,
        residual=jnp.pad(residual, ((0, blank), (0, blank))),
    )


def per_device(
    hidden_in, segments, routes, prev_logits, out_grad, norm_attn, w_query, w_key, w_value,
    w_out, norm_moe, w_router, w_res, w_const, const_vec, w_gate, w_up, w_down,
):
    local = dict(
        norm_attn=norm_attn, w_query=w_query, w_key=w_key, w_value=w_value, w_out=w_out,
        norm_moe=norm_moe, w_router=w_router, w_res=w_res, w_const=w_const,
        const_vec=const_vec, w_gate=w_gate, w_up=w_up, w_down=w_down,
    )
    micro_count, _, length, width = hidden_in.shape
    micros = range(micro_count)
    layers = norm_attn.shape[0]
    groups = lax.axis_size("expert")
    hop_count = min((WINDOW + length - 2) // length, lax.axis_size("context") - 1)
    capacity = length // 4
    slots = EXPERTS * capacity
    block_start = lax.axis_index("context") * length
    routes = routes[:, 0]
    columns, slot_rows = routing_slots(routes, groups, capacity)
    blank_gates = jnp.zeros((8, length), f32)

    def normed(hidden, gain):
        return (hidden * inverse_rms(hidden) * gain).astype(bf16)

    last_arrived = []

    def in_turn(blocks, micro):
        others = held(list(blocks[1:]), tuple(last_arrived[1:]) if micro > 0 else ())
        last_arrived[:] = exchange(list(blocks[:1]) + others, -1)
        return list(last_arrived)

    early = []

    def send_early(micro, after):
        sent = dispatch(
            out_grad[micro, 0], slot_rows[micro], blank_gates, "plain", slots, groups, after
        )
        early.append(exchange(sent, 1))

    send_early(0, ())
    fetched = [fetch_layer(layer, local) for layer in range(layers)]
    segs, state = [], []
    for micro in micros:
        whole = segments[micro, 0]
        padded = jnp.concatenate([jnp.full((WINDOW,), -1, jnp.int32), whole])
        query = lax.dynamic_slice_in_dim(whole, block_start, length, 0)
        key = lax.dynamic_slice_in_dim(padded, block_start, WINDOW + length, 0)
        segs.append((query, key))
        hidden = hidden_in[micro, 0].astype(f32)
        gain = fetched[0]["vectors"][ATTN_GAIN_ROW : ATTN_GAIN_ROW + 1]
        prior = jnp.pad(prev_logits[micro, 0], ((0, 0), (0, LANES - ROUTED)))
        state.append(
            (
                hidden, normed(hidden, gain),
                None if micro > 0 else earlier_rows(hidden_in[micro, 0], hop_count), prior,
            )
        )

    saved = [[None] * layers for _ in micros]
    expert_sums = [None] * layers

    def attention_part(layer, micro, after, after_output):
        weights = fetched[layer]
        hidden, attn_in, attn_earlier, prior = state[micro]
        if layer == 0:
            if micro > 0:
                (block,) = held([hidden_in[micro, 0]], (saved[micro - 1][0]["attended"],))
                attn_earlier = earlier_rows(block, hop_count)
            attn_earlier = normed(attn_earlier.astype(f32), weights["vectors"][ATTN_GAIN_ROW][None])
        qkv = dot_on(attn_in, weights["dense"][:, : 3 * width], 1, 0).astype(bf16)
        kv_earlier = dot_on(attn_earlier, weights["dense"][:, width : 3 * width], 1, 0).astype(bf16)
        query, key = segs[micro]
        attended, lse = attention_forward(qkv, kv_earlier, query[:, None], key[None, :], after)
        mid, low, logits, scalars, gate_rows = attention_output(
            hidden, attended, weights, prior, routes[micro]
        )
        mode = "with gate" if layer == layers - 1 else "plain"
        sent = dispatch(low, slot_rows[micro], gate_rows, mode, slots, groups, after_output)
        saved[micro][layer] = dict(
            hidden=hidden, attn_in=attn_in, attn_earlier=attn_earlier, prior=prior, qkv=qkv,
            kv_earlier=kv_earlier, attended=attended, lse=lse, mid=mid, low=low,
            scalars=scalars, gate_rows=gate_rows, logits=logits, arrived=exchange(sent, 1),
        )
        return sent[-1]

    def experts_part(layer, micro, after):
        kept = saved[micro][layer]
        gate_up_w, down_w = fetched[layer]["gate_up"], fetched[layer]["down"]
        if layer == layers - 1:
            out, expert_sums[layer] = experts_backward(
                kept["arrived"], early[micro], None, gate_up_w, down_w, expert_sums[layer], after
            )
            arrived = in_turn(out, 0)
            kept["returned"], kept["back"] = (arrived, 0), (arrived, 1)
        else:
            out, *kept["pre"] = experts_forward(kept["arrived"], gate_up_w, down_w, after)
            kept["returned"] = (in_turn(out, 0), 0)
        return out[-1]

    def combine_part(layer, micro, after):
        kept = saved[micro][layer]
        last = layer == layers - 1
        outs = combine(
            kept["returned"], columns[micro], kept["mid"], kept["scalars"],
            fetched[layer]["vectors"], None if last else fetched[layer + 1]["vectors"], after,
        )
        kept["branch"] = outs[:TOP]
        if last:
            return outs[TOP]
        state[micro] = (
            outs[TOP], outs[TOP + 1], earlier_rows(outs[TOP + 1], hop_count), kept["logits"],
        )
        return outs[TOP]

    def experts_back_part(layer, micro, d_rows, after):
        kept = saved[micro][layer]
        dx, expert_sums[layer] = experts_backward(
            kept["arrived"], d_rows, kept["pre"], fetched[layer]["gate_up"],
            fetched[layer]["down"], expert_sums[layer], after,
        )
        kept["back"] = (in_turn(dx, 0), 0)
        return dx[-1]

    def token_back_part(layer, micro, grad, d_prior, after):
        kept = saved[micro][layer]
        (
            kept["d_mid"], kept["d_att"], d_prior, kept["g_out"], kept["g_small"],
            kept["g_residual"], g_moe_gain,
        ) = token_backward(
            kept["back"], kept, grad, fetched[layer], columns[micro], routes[micro], d_prior, after
        )
        kept["g_moe_gain"] = g_moe_gain[0]
        return d_prior

    def attention_back_part(layer, micro, after):
        kept, dense = saved[micro][layer], fetched[layer]["dense"]
        query, key = segs[micro]
        dq, dk, dv = attention_backward(
            kept["qkv"], kept["kv_earlier"], kept["d_att"], kept["attended"], kept["lse"],
            query[None, :], key[:, None], after,
        )
        query_w, key_w, value_w = (dense[:, i * width : (i + 1) * width] for i in range(3))
        kept["later"] = None
        if hop_count > 0:
            d_earlier = (
                dot_on(dk[:WINDOW], key_w, 1, 1) + dot_on(dv[:WINDOW], value_w, 1, 1)
            ).astype(bf16)
            kept["later"] = returned_rows(d_earlier, length, hop_count)
        kept["d_attn"] = (
            dot_on(dq, query_w, 1, 1)
            + dot_on(dk[WINDOW:], key_w, 1, 1)
            + dot_on(dv[WINDOW:], value_w, 1, 1)
        )
        kept["grads"] = [
            dot_on(kept["attn_in"], dq, 0, 0),
            dot_on(kept["attn_in"], dk[WINDOW:], 0, 0)
            + dot_on(kept["attn_earlier"], dk[:WINDOW], 0, 0),
            dot_on(kept["attn_in"], dv[WINDOW:], 0, 0)
            + dot_on(kept["attn_earlier"], dv[:WINDOW], 0, 0),
            kept["g_out"],
            kept["g_small"],
        ]
        return dq

    def finish_back_part(layer, micro, after):
        kept = saved[micro][layer]
        d_hidden, g_attn_gain = finish_backward(
            kept["hidden"], kept["d_mid"], kept["d_attn"], fetched[layer]["vectors"],
            kept["later"], f32 if layer > 0 else bf16, after,
        )
        kept["g_attn_gain"] = g_attn_gain[0]
        return d_hidden

    expert_shares, dense_shares = [None] * layers, [None] * layers

    def reduce_experts(layer):
        gate_up, down = held(expert_sums[layer], saved[0][layer]["back"][0][1:])
        gate_up = gate_up.reshape((-1,) + gate_up.shape[2:])
        expert_shares[layer] = (
            lax.psum_scatter(gate_up, SHARDED, scatter_dimension=1, tiled=True),
            lax.psum_scatter(down, SHARDED, scatter_dimension=1, tiled=True),
        )
        return expert_shares[layer]

    def total_of(layer, name):
        parts = [saved[micro][layer][name] for micro in micros]
        return sum(parts[1:], parts[0])

    def packed_dense(layer):
        parts = [saved[micro][layer]["grads"] for micro in micros]
        sums = [sum(values[1:], values[0]) for values in zip(*parts)]
        shards = lax.axis_size("context") * lax.axis_size("dp")
        at = ROUTED + 8
        residual = jnp.pad(
            total_of(layer, "g_residual")[:ROUTED, :ROUTED],
            ((0, width // shards - ROUTED), (at, LANES - at - ROUTED)),
        )
        small = sums[-1] + jnp.tile(residual, (shards, 1))
        if layer == 0:
            gains = [total_of(l, "g_moe_gain") for l in range(layers)]
            gains += [total_of(l, "g_attn_gain") for l in range(layers)]
            blank = jnp.zeros((LANES - GAINS_LANE - len(gains), width), f32)
            above = jnp.zeros((GAINS_LANE, width), f32)
            small = small + jnp.concatenate([above, jnp.stack(gains), blank]).T
        return jnp.concatenate([total.astype(bf16) for total in sums[:-1] + [small]], axis=1)

    def reduce_dense(layer, packed, after):
        shards = lax.axis_size("context") * lax.axis_size("dp")
        parts = packed.reshape(shards, width // shards, packed.shape[1])
        parts = lax.all_to_all(parts, SHARDED, split_axis=0, concat_axis=0, tiled=True)
        share = jnp.sum(parts.astype(f32), axis=0)
        if layer > 0:
            (share,) = held([share.astype(bf16)], after)
            share = lax.psum(share, "expert").astype(f32)
        else:
            span = 1
            while span < groups:
                sent = share.astype(bf16)
                route = [(i, i ^ span) for i in range(groups)]
                share = sent.astype(f32) + lax.ppermute(sent, "expert", route).astype(f32)
                span *= 2
        dense_shares[layer] = share
        return (share,)

    last = layers - 1
    d_rows = [None] * micro_count

    def send_back(layer, micro, after):
        grads[micro] = finish_back_part(layer, micro, after)
        sent = dispatch(
            grads[micro], slot_rows[micro], saved[micro][layer - 1]["gate_rows"], "scaled", slots,
            groups,
        )
        d_rows[micro] = exchange(sent, 1)
        return sent[-1]

    before = ()
    for layer in range(layers):
        for micro in micros:
            if layer > 0:
                before = (combine_part(layer - 1, micro, before),)
        if layer == last:
            for micro in micros[1:]:
                send_early(micro, before)
        for micro in micros:
            waits = tuple(early[-1][1:]) if micro == 0 else ()
            before = (attention_part(layer, micro, before, waits),)
        for micro in micros:
            before = (experts_part(layer, micro, before),)
    hidden_out = []

    grads = [out_grad[micro, 0] for micro in micros]
    d_priors = [None] * micro_count
    dense_wait = ()
    for layer in range(last, -1, -1):
        experts_ready = reduce_experts(layer)
        for micro in micros:
            if layer == last:
                hidden_out.append(combine_part(last, micro, before))
                before = (hidden_out[-1],)
            d_priors[micro] = token_back_part(layer, micro, grads[micro], d_priors[micro], before)
            before = (saved[micro][layer]["d_att"],)
            before = (attention_back_part(layer, micro, before),)
            if layer > 0:
                before = (send_back(layer, micro, before),)
        if layer > 0:
            for micro in micros:
                if micro < len(experts_ready):
                    before += (experts_ready[micro],)
                before = (experts_back_part(layer - 1, micro, d_rows[micro], before),)
                if micro == 0:
                    first = before
            (packed,) = held([packed_dense(layer)], first)
            dense_wait = reduce_dense(layer, packed, before)
        else:
            for micro in micros:
                grads[micro] = finish_back_part(layer, micro, tuple(experts_ready) + dense_wait)
    reduce_dense(0, packed_dense(0), ())
    hidden_out = jnp.stack(hidden_out)[:, None]
    hidden_grad = jnp.stack(grads)[:, None]

    dense = jnp.stack(dense_shares)
    small = dense[:, :, 4 * width :]
    shard = small.shape[1]
    experts_total = [jnp.stack(parts).astype(f32) for parts in zip(*expert_shares)]
    per_dev = EXPERTS // groups
    return (
        hidden_out,
        hidden_grad,
        jnp.stack([small[0, :, GAINS_LANE + layers + l] for l in range(layers)]),
        dense[:, :, :width],
        dense[:, :, width : 2 * width],
        dense[:, :, 2 * width : 3 * width],
        dense[:, :, 3 * width : 4 * width],
        jnp.stack([small[0, :, GAINS_LANE + l] for l in range(layers)]),
        small[:, :, :ROUTED],
        small[:, :ROUTED, ROUTED + 8 : 2 * ROUTED + 8],
        jnp.transpose(
            small[:, :, ROUTED : ROUTED + 4].reshape(layers, shard, 2, 2), (0, 2, 1, 3)
        ),
        jnp.transpose(small[:, :, ROUTED + 4 : ROUTED + 6], (0, 2, 1)),
        experts_total[0][:, :per_dev],
        experts_total[0][:, per_dev:],
        experts_total[1],
    )

def solution(mesh):
    tokens = P(None, ("expert", "dp"), "context", None)
    rows = P(None, SHARDED, None)
    vector = P(None, SHARDED)
    experts = P(None, "expert", SHARDED, None)
    const = P(None, None, SHARDED, None)
    const_vector = P(None, None, SHARDED)
    return jax.shard_map(
        per_device,
        mesh=mesh,
        in_specs=(
            tokens, P(None, ("expert", "dp"), None), tokens, tokens, tokens, vector, rows, rows,
            rows, rows, vector, rows, P(), const, const_vector, experts, experts, experts,
        ),
        out_specs=(
            tokens, tokens, vector, rows, rows, rows, rows, vector, rows, P(), const,
            const_vector, experts, experts, experts,
        ),
        check_vma=False,
    )
```
